128 devices in a mesh: section: 2 (over core), group: 4 (over z), replica: 16 (over x, y).
Axes of the slice: x: 4, y: 4, z: 4, core: 2. Of those that a mesh axis runs over, the one named last changes fastest.
Arguments:
- tokens: bfloat16 [2, 16, 256, 896], P(None, 'replica', 'group'), may hold values from -6 to 6
- cotangent: bfloat16 [2, 16, 256, 896], P(None, 'replica', 'group'), may hold values from -6 to 6
- doc_lengths: int32 [2, 16, 5], P(None, 'replica'), may hold values from 1 to 193, 256 in all within a row
- w_qkv: bfloat16 [2, 896, 1152], P('section', 'group'), may hold values from -0.1875 to 0.1875
- b_qkv: bfloat16 [2, 1152], P('section', 'group'), may hold values from -3 to 3
- w_out: bfloat16 [2, 896, 896], P('section', 'group'), may hold values from -0.5 to 0.5
- w_gate: bfloat16 [2, 896, 4864], P('section', 'group'), may hold values from -0.1875 to 0.1875
- w_up: bfloat16 [2, 896, 4864], P('section', 'group'), may hold values from -0.1875 to 0.1875
- w_down: bfloat16 [2, 4864, 896], P('section', 'group'), may hold values from -0.15625 to 0.15625
- norm_attn: bfloat16 [2, 896], P('section', 'group'), may hold values from 0.5 to 1.5
- norm_ffn: bfloat16 [2, 896], P('section', 'group'), may hold values from 0.5 to 1.5
Outputs:
- acts: bfloat16 [2, 2, 16, 256, 896], P('section', None, 'replica', 'group')
- input_grads: float32 [2, 2, 16, 256, 896], P('section', None, 'replica', 'group')
- grad_w_qkv: float32 [2, 896, 1152], P('section', 'group')
- grad_b_qkv: float32 [2, 1152], P('section', 'group')
- grad_w_out: float32 [2, 896, 896], P('section', 'group')
- grad_w_gate: float32 [2, 896, 4864], P('section', 'group')
- grad_w_up: float32 [2, 896, 4864], P('section', 'group')
- grad_w_down: float32 [2, 4864, 896], P('section', 'group')
- grad_norm_attn: float32 [2, 896], P('section', 'group')
- grad_norm_ffn: float32 [2, 896], P('section', 'group')
The draws below stay inside these ranges and needn't reach their ends.
Inputs may be any that keep to these rules, and one draw needn't show every extreme that they name: `doc_lengths`: each row's 5 lengths sum to 256; in every row one document has exactly 193 tokens.
All inputs are finite; a program needn't handle non-finite values.
Results may differ from the reference program's by a relative error of at most 0.025.
Values may be sent and summed in bfloat16 or wider, within the bound.
A program may use at most 192 MiB of HBM per device.

```python
import math
import jax
import jax.numpy as jnp
import numpy as np
from jax import lax

D = 896
FF = 4864
HEADS = 14
KV_HEADS = 2
HEAD_DIM = 64
SPAN = 64
MICRO = 2
NDOC = 5
QKV = 1152
ROW = 256
ROWS = 16
LAYERS = 2


def steps_of(key, shape, split, least, top_value):
    level, own = 1.0, jax.random.fold_in(key, 6)
    for axis_at, parts in split:
        steps = jnp.exp(jax.random.uniform(jax.random.fold_in(own, axis_at), (parts,), jnp.float32, least / len(split), top_value / len(split)))
        level = level * jnp.repeat(steps, shape[axis_at] // parts).reshape([-1 if axis == axis_at else 1 for axis in range(len(shape))])
    return level


def length_profile(amount, total, bound, skew):
    loads = [(1 << 20) // math.isqrt(grade ** skew) + 1 for grade in range(2, amount + 1)]
    surplus, given = total - bound - (amount - 1), [1] * (amount - 1)
    while surplus > 0:
        movable = [i for i in range(amount - 1) if given[i] < bound]
        pool, left = sum([loads[i] for i in movable]), surplus
        for i in movable:
            extra = min(bound - given[i], max(1, left * loads[i] // pool), surplus)
            given[i] = given[i] + extra
            surplus = surplus - extra
    return np.array([bound] + given)


def uneven(key, count, total, reach, slope):
    if count == 2:
        one = jax.random.randint(key, (), max(1, total - reach), min(reach, total - 1) + 1)
        return jnp.stack([one, total - one])
    sizes = jnp.asarray(length_profile(count, total, reach, slope), jnp.int32)
    couples = (count - 1) // 2
    giver, taker = sizes[1:1 + 2 * couples:2], sizes[2:2 + 2 * couples:2]
    room = jnp.minimum(giver - 1, reach - taker)
    passed = jax.random.randint(jax.random.fold_in(key, 1), (couples,), 0, 1 << 20) % (room + 1)
    sizes = sizes.at[1:1 + 2 * couples:2].set(giver - passed).at[2:2 + 2 * couples:2].set(taker + passed)
    return sizes[jax.random.permutation(jax.random.fold_in(key, 2), count)]


def bell_draw(key, dims, spread, bound, cuts=(), kind=jnp.bfloat16):
    array = spread * jax.random.normal(key, dims, jnp.float32)
    if cuts:
        array = array * steps_of(key, dims, cuts, -0.22, 0.18)
    return jnp.clip(array, -bound, bound).astype(kind)


def setup_inputs(seed: int = 0) -> dict:
    keys = jax.random.split(jax.random.key(seed), 12)
    tokens = bell_draw(keys[0], (MICRO, ROWS, ROW, D), 1.0, 6.0, ((1, 16), (2, 4)))
    cotangent = bell_draw(keys[1], (MICRO, ROWS, ROW, D), 1.0, 6.0, ((1, 16), (2, 4)))
    doc_lengths = jax.vmap(lambda own: uneven(own, NDOC, ROW, ROW - SPAN + 1, 2))(jax.random.split(keys[2], MICRO * ROWS)).reshape((MICRO, ROWS, NDOC)).astype(jnp.int32)
    w_qkv = bell_draw(keys[3], (LAYERS, D, QKV), D ** -0.5, 0.1875, ((0, 2), (1, 4)))
    b_qkv = bell_draw(keys[4], (LAYERS, QKV), 0.5, 3.0, ((0, 2), (1, 4)))
    w_out = bell_draw(keys[5], (LAYERS, D, D), (D // 8) ** -0.5, 0.5, ((0, 2), (1, 4)))
    w_gate = bell_draw(keys[6], (LAYERS, D, FF), D ** -0.5, 0.1875, ((0, 2), (1, 4)))
    w_up = bell_draw(keys[7], (LAYERS, D, FF), D ** -0.5, 0.1875, ((0, 2), (1, 4)))
    w_down = bell_draw(keys[8], (LAYERS, FF, D), (FF // 4) ** -0.5, 0.15625, ((0, 2), (1, 4)))
    norm_attn = jnp.clip(1.0 + 0.1 * jax.random.normal(keys[9], (LAYERS, D), jnp.float32), 0.5, 1.5).astype(jnp.bfloat16)
    norm_ffn = jnp.clip(1.0 + 0.1 * jax.random.normal(keys[10], (LAYERS, D), jnp.float32), 0.5, 1.5).astype(jnp.bfloat16)
    return dict(tokens=tokens, cotangent=cotangent, doc_lengths=doc_lengths, w_qkv=w_qkv, b_qkv=b_qkv, w_out=w_out, w_gate=w_gate, w_up=w_up, w_down=w_down, norm_attn=norm_attn, norm_ffn=norm_ffn)


eps = 1e-06
rope_base = 1000000.0
highest = lax.Precision.HIGHEST

@jax.custom_vjp
def low(v):
    return lax.optimization_barrier(v.astype(jnp.bfloat16)).astype(jnp.float32)

@jax.custom_vjp
def low_back(v):
    return v

def low_keep(v):
    return (low(v), None)

def low_pass(kept, grad):
    return (grad,)

def back_keep(v):
    return (v, None)

def back_low(kept, grad):
    return (low(grad),)
low.defvjp(low_keep, low_pass)
low_back.defvjp(back_keep, back_low)

def rotate_half(values):
    half_len = values.shape[-1] // 2
    return jnp.concatenate([-values[..., half_len:], values[..., :half_len]], axis=-1)

def row_tables(doc_lens):
    doc_ends = jnp.cumsum(doc_lens).astype(jnp.int32)
    doc_starts = doc_ends - doc_lens
    row_spots = jnp.arange(ROW, dtype=jnp.int32)
    segment = lax.optimization_barrier(jnp.sum((doc_ends[None, :] <= row_spots[:, None]).astype(jnp.int32), axis=1))
    doc_pick = segment[:, None] == jnp.arange(NDOC, dtype=jnp.int32)[None, :]
    doc_begin = lax.optimization_barrier(jnp.sum(jnp.where(doc_pick, doc_starts[None, :], 0), axis=1))
    allowed = (segment[:, None] == segment[None, :]) & (row_spots[None, :] <= row_spots[:, None])
    inv_freqs = rope_base ** (-jnp.arange(0, HEAD_DIM, 2, dtype=jnp.float32) / HEAD_DIM)
    angles = (row_spots - doc_begin).astype(jnp.float32)[:, None] * inv_freqs[None, :]
    angles = jnp.concatenate([angles, angles], axis=1)
    return (allowed, jnp.cos(angles)[:, None, :], jnp.sin(angles)[:, None, :])

def dense(left, right):
    return jnp.dot(left, right, precision=highest)

def layer(values, weights, allowed, cosine, sine_table):
    w_qkv, b_qkv, w_out, w_gate, w_up, w_down, gain_attn, gain_ffn = weights
    row_len = values.shape[0]
    q_width = HEADS * HEAD_DIM
    kv_width = KV_HEADS * HEAD_DIM
    scale_one = lax.rsqrt(lax.optimization_barrier(jnp.mean(values * values, axis=-1, keepdims=True)) + eps)
    normed_one = low(values * scale_one * gain_attn)
    mixed_qkv = low_back(dense(normed_one, w_qkv) + b_qkv)
    query_pre = mixed_qkv[:, :q_width].reshape(row_len, HEADS, HEAD_DIM)
    key_pre = mixed_qkv[:, q_width:q_width + kv_width].reshape(row_len, KV_HEADS, HEAD_DIM)
    value_rows = low(mixed_qkv[:, q_width + kv_width:].reshape(row_len, KV_HEADS, HEAD_DIM))
    query_rot = low(query_pre * cosine + rotate_half(query_pre) * sine_table)
    key_rot = low(key_pre * cosine + rotate_half(key_pre) * sine_table)
    grouped = query_rot.reshape(row_len, KV_HEADS, HEADS // KV_HEADS, HEAD_DIM)
    scores = low_back(jnp.einsum('ikgd,jkd->kgij', grouped, key_rot, precision=highest) * HEAD_DIM ** (-0.5))
    scores = jnp.where(allowed[None, None], scores, -jnp.inf)
    attn_probs = low(jax.nn.softmax(scores, axis=-1))
    context = jnp.einsum('kgij,jkd->ikgd', attn_probs, value_rows, precision=highest).reshape(row_len, q_width)
    context = low(low_back(context))
    hidden = values + low_back(dense(context, w_out))
    scale_two = lax.rsqrt(lax.optimization_barrier(jnp.mean(hidden * hidden, axis=-1, keepdims=True)) + eps)
    normed_two = low(hidden * scale_two * gain_ffn)
    gate_proj = low_back(dense(normed_two, w_gate))
    up_proj = low_back(dense(normed_two, w_up))
    activated = low(jax.nn.silu(gate_proj) * up_proj)
    return hidden + low_back(dense(activated, w_down))

def reference(tokens, cotangent, doc_lengths, w_qkv, b_qkv, w_out, w_gate, w_up, w_down, norm_attn, norm_ffn):
    weights = tuple((member.astype(jnp.float32) for member in (w_qkv, b_qkv, w_out, w_gate, w_up, w_down, norm_attn, norm_ffn)))
    row_count = MICRO * ROWS
    inputs = tokens.astype(jnp.float32).reshape(row_count, ROW, D)
    probe = jnp.zeros((row_count, ROW, D), jnp.float32)
    lengths_all = doc_lengths.reshape(row_count, NDOC)

    def forward(inputs, probe, weights):
        first_set = tuple((member[0] for member in weights))
        second_set = tuple((member[1] for member in weights))

        def one_row(pieces):
            row_vals, probe_row, row_lens = pieces
            allowed, cosine, sine_table = row_tables(row_lens)
            first_out = low(layer(row_vals, first_set, allowed, cosine, sine_table))
            second_out = layer(low_back(first_out + probe_row), second_set, allowed, cosine, sine_table)
            return (first_out, second_out)
        return lax.map(jax.checkpoint(one_row), (inputs, probe, lengths_all))
    outputs, pullback = jax.vjp(forward, inputs, probe, weights)
    grad_inputs, grad_probe, grad_weights = pullback((jnp.zeros_like(outputs[0]), cotangent.astype(jnp.float32).reshape(row_count, ROW, D)))
    shape_out = (MICRO, ROWS, ROW, D)
    acts = jnp.stack([outputs[0].reshape(shape_out), outputs[1].reshape(shape_out)]).astype(jnp.bfloat16)
    input_grads = jnp.stack([grad_inputs.reshape(shape_out), grad_probe.reshape(shape_out)])
    return (acts, input_grads, grad_weights[0], grad_weights[1], grad_weights[2], grad_weights[3], grad_weights[4], grad_weights[5], grad_weights[6], grad_weights[7])
```

```python
import jax
import jax.numpy as jnp
import numpy as np
from jax import lax
from jax.sharding import PartitionSpec as P

HEADS = 14
KV_HEADS = 2
HEAD_DIM = 64
GROUPS = HEADS // KV_HEADS
D = 896
FF = 4864
QKV = 1152
SPAN = 64
ROW = 256
REPL = 16
ZDEV = 4
OWN = D // ZDEV
CHUNK = OWN // REPL
BLOCK = FF // ZDEV
WIN = 1280
STARTS = [128 * ((19 * z) // 2) for z in range(ZDEV)]
SHIFTS = [BLOCK * z - STARTS[z] for z in range(ZDEV)]
KV_WIDTH = KV_HEADS * HEAD_DIM

eps = 1e-06
rope_base = 1000000.0
f32 = jnp.float32
bf16 = jnp.bfloat16

PERM = np.zeros((D, REPL, ZDEV, 16), np.float32)
for z_at in range(ZDEV):
    for r_at in range(REPL):
        for i_at in range(CHUNK):
            PERM[z_at * OWN + r_at * CHUNK + i_at, r_at, z_at, i_at] = 1.0
PERM = PERM.reshape(D, REPL * ZDEV * 16)


def rms_scale(values):
    return lax.rsqrt(jnp.mean(values * values, axis=-1, keepdims=True) + eps)


def rotate_half(values):
    half_len = values.shape[-1] // 2
    return jnp.concatenate([-values[..., half_len:], values[..., :half_len]], axis=-1)


def norm_back(grad_norm, values, scale_rows, gain_vec):
    scaled = grad_norm * gain_vec
    row_inner = jnp.mean(scaled * values, axis=-1, keepdims=True)
    grad_in = scale_rows * (scaled - values * scale_rows * scale_rows * row_inner)
    grad_gain = jnp.sum(grad_norm * values * scale_rows, axis=0)
    return (grad_in, grad_gain)


def doc_tables(doc_lens, group_at):
    doc_ends = jnp.cumsum(doc_lens)
    doc_starts = doc_ends - doc_lens
    row_spots = jnp.arange(ROW, dtype=jnp.int32)
    segment = jnp.sum((doc_ends[None, :] <= row_spots[:, None]).astype(jnp.int32), axis=1)
    doc_pick = segment[:, None] == jnp.arange(doc_lens.shape[0], dtype=jnp.int32)[None, :]
    doc_begin = jnp.sum(jnp.where(doc_pick, doc_starts[None, :], 0), axis=1)
    first_row = group_at * SPAN
    own_segment = lax.dynamic_slice_in_dim(segment, first_row, SPAN)
    own_spots = lax.dynamic_slice_in_dim(row_spots, first_row, SPAN)
    own_begin = lax.dynamic_slice_in_dim(doc_begin, first_row, SPAN)
    allowed = (own_segment[:, None] == segment[None, :]) & (
        row_spots[None, :] <= own_spots[:, None]
    )
    inv_freqs = rope_base ** (-jnp.arange(0, HEAD_DIM, 2, dtype=f32) / HEAD_DIM)
    angles = (own_spots - own_begin).astype(f32)[:, None] * inv_freqs[None, :]
    angles = jnp.concatenate([angles, angles], axis=1)
    return (allowed, jnp.cos(angles)[:, None, :], jnp.sin(angles)[:, None, :])


def split_kv(all_kv):
    key_rows = all_kv[:, :KV_WIDTH].reshape(ROW, KV_HEADS, HEAD_DIM)
    value_rows = all_kv[:, KV_WIDTH:].reshape(ROW, KV_HEADS, HEAD_DIM)
    return (key_rows, value_rows)


def score_block(query_rot, key_rows, allowed):
    grouped = query_rot.reshape(SPAN, KV_HEADS, GROUPS, HEAD_DIM)
    scores = (
        jnp.einsum("ikgd,jkd->kgij", grouped, key_rows, preferred_element_type=f32)
        * HEAD_DIM ** (-0.5)
    )
    return jnp.where(allowed[None, None], scores, -jnp.inf)


def dot(left, right):
    return jnp.dot(left, right, preferred_element_type=f32)


def dot_t(left, right):
    return jnp.einsum("id,ed->ie", left, right, preferred_element_type=f32)


def layer_forward(entering, weights, tables):
    w_qo, w_gu, w_down, b_qkv, gain_attn, gain_ffn = weights
    allowed, cosine, sine_table = tables
    values = entering.astype(f32)
    scale_one = rms_scale(values)
    normed_one = (values * scale_one * gain_attn).astype(bf16)
    mixed_qkv = dot(normed_one, w_qo[:, :QKV]) + b_qkv
    query_pre = mixed_qkv[:, :D].reshape(SPAN, HEADS, HEAD_DIM)
    key_pre = mixed_qkv[:, D : D + KV_WIDTH].reshape(SPAN, KV_HEADS, HEAD_DIM)
    query_rot = (query_pre * cosine + rotate_half(query_pre) * sine_table).astype(bf16)
    key_rot = (key_pre * cosine + rotate_half(key_pre) * sine_table).astype(bf16)
    local_kv = jnp.concatenate(
        [key_rot.reshape(SPAN, KV_WIDTH), mixed_qkv[:, D + KV_WIDTH :].astype(bf16)], axis=1
    )
    all_kv = lax.all_gather(local_kv, "group", axis=0, tiled=True)
    key_rows, value_rows = split_kv(all_kv)
    scores = score_block(query_rot, key_rows, allowed)
    row_top = jnp.max(scores, axis=-1, keepdims=True)
    log_total = row_top + jnp.log(jnp.sum(jnp.exp(scores - row_top), axis=-1, keepdims=True))
    attn_probs = jnp.exp(scores - log_total).astype(bf16)
    context = jnp.einsum("kgij,jkd->ikgd", attn_probs, value_rows, preferred_element_type=f32)
    context = context.reshape(SPAN, D).astype(bf16)
    hidden = values + dot(context, w_qo[:, QKV:])
    scale_two = rms_scale(hidden)
    normed_two = (hidden * scale_two * gain_ffn).astype(bf16)
    normed_all = lax.all_gather(normed_two, "group", axis=0, tiled=True)
    gate_up = dot(normed_all, w_gu)
    gate_proj, up_proj = gate_up[:, :WIN], gate_up[:, WIN:]
    activated = (jax.nn.silu(gate_proj) * up_proj).astype(bf16)
    partial = dot(activated, w_down).astype(bf16)
    mlp = lax.psum_scatter(partial, "group", scatter_dimension=0, tiled=True).astype(f32)
    output = (hidden + mlp).astype(bf16)
    kept = (values, scale_one, normed_one, query_rot, all_kv, log_total, context, hidden)
    kept = kept + (scale_two, normed_all, gate_up, activated)
    return (output, kept)


def layer_backward(grad_out, kept, weights, tables):
    values, scale_one, normed_one, query_rot, all_kv, log_total, context, hidden = kept[:8]
    scale_two, normed_all, gate_up, activated = kept[8:]
    w_qo, w_gu, w_down, b_qkv, gain_attn, gain_ffn = weights
    allowed, cosine, sine_table = tables
    gate_proj, up_proj = gate_up[:, :WIN], gate_up[:, WIN:]
    grad_mlp = grad_out.astype(bf16)
    grad_mlp_all = lax.all_gather(grad_mlp, "group", axis=0, tiled=True)
    grad_act = dot_t(grad_mlp_all, w_down)
    sigma_gate = jax.nn.sigmoid(gate_proj)
    silu_gate = gate_proj * sigma_gate
    grad_gate = grad_act * up_proj * sigma_gate * (1.0 + gate_proj * (1.0 - sigma_gate))
    grad_up = grad_act * silu_gate
    grad_gu = jnp.concatenate([grad_gate.astype(bf16), grad_up.astype(bf16)], axis=1)
    partial = dot_t(grad_gu, w_gu).astype(bf16)
    grad_norm_two = lax.psum_scatter(
        partial, "group", scatter_dimension=0, tiled=True
    ).astype(f32)
    back_two, grad_gain_ffn = norm_back(grad_norm_two, hidden, scale_two, gain_ffn)
    grad_hidden = grad_out + back_two
    grad_attn = grad_hidden.astype(bf16)
    grad_context = dot_t(grad_attn, w_qo[:, QKV:]).astype(bf16)
    grad_context = grad_context.reshape(SPAN, KV_HEADS, GROUPS, HEAD_DIM)
    key_rows, value_rows = split_kv(all_kv)
    grouped = query_rot.reshape(SPAN, KV_HEADS, GROUPS, HEAD_DIM)
    attn_probs = jnp.exp(score_block(query_rot, key_rows, allowed) - log_total)
    grad_probs = jnp.einsum("ikgd,jkd->kgij", grad_context, value_rows, preferred_element_type=f32)
    row_inner = jnp.sum(attn_probs * grad_probs, axis=-1, keepdims=True)
    grad_scores = (attn_probs * (grad_probs - row_inner)).astype(bf16)
    score_scale = HEAD_DIM ** (-0.5)
    grad_query = jnp.einsum("kgij,jkd->ikgd", grad_scores, key_rows, preferred_element_type=f32)
    grad_query = grad_query.reshape(SPAN, HEADS, HEAD_DIM) * score_scale
    grad_key_all = (
        jnp.einsum("kgij,ikgd->jkd", grad_scores, grouped, preferred_element_type=f32)
        * score_scale
    )
    grad_value_all = jnp.einsum(
        "kgij,ikgd->jkd", attn_probs.astype(bf16), grad_context, preferred_element_type=f32
    )
    grad_kv_all = jnp.concatenate(
        [grad_key_all.reshape(ROW, KV_WIDTH), grad_value_all.reshape(ROW, KV_WIDTH)], axis=1
    )
    grad_kv = lax.psum_scatter(
        grad_kv_all.astype(bf16), "group", scatter_dimension=0, tiled=True
    ).astype(f32)
    grad_key = grad_kv[:, :KV_WIDTH].reshape(SPAN, KV_HEADS, HEAD_DIM)
    query_back = grad_query * cosine - rotate_half(grad_query * sine_table)
    key_back = grad_key * cosine - rotate_half(grad_key * sine_table)
    grad_mixed = jnp.concatenate(
        [query_back.reshape(SPAN, D), key_back.reshape(SPAN, KV_WIDTH), grad_kv[:, KV_WIDTH:]],
        axis=1,
    ).astype(bf16)
    grad_bias = jnp.sum(grad_mixed.astype(f32), axis=0)
    grad_norm_one = dot_t(grad_mixed, w_qo[:, :QKV])
    back_one, grad_gain_attn = norm_back(grad_norm_one, values, scale_one, gain_attn)
    grad_in = grad_hidden + back_one
    pieces = (
        jnp.concatenate([normed_one, grad_mixed, context, grad_attn], axis=1),
        jnp.concatenate([normed_all, grad_gu, activated, grad_mlp_all], axis=1),
        jnp.concatenate([grad_gain_attn, grad_gain_ffn, grad_bias])[None],
    )
    return (grad_in, pieces)


def gather_weights(w_qkv, b_qkv, w_out, w_gate, w_up, w_down, norm_attn, norm_ffn):
    group_at = lax.axis_index("group")
    replica_at = lax.axis_index("replica")

    def own_rows(block):
        return lax.dynamic_slice_in_dim(block, replica_at * CHUNK, CHUNK, 0)

    vectors = jnp.concatenate([norm_attn, norm_ffn, b_qkv])
    joint = jnp.concatenate([own_rows(w_qkv), own_rows(w_out)], axis=1)
    extra = jnp.zeros((2, joint.shape[1]), bf16)
    extra = lax.dynamic_update_slice(extra, vectors[None], (0, 0))
    joint = jnp.concatenate([joint, extra], axis=0)
    joint = lax.all_gather(joint, ("group", "replica"), axis=0, tiled=False)
    joint = joint.reshape(ZDEV, REPL, 16, joint.shape[-1])
    w_qo = joint[:, :, :CHUNK].reshape(D, QKV + D)
    vectors = joint[:, 0, CHUNK, : vectors.shape[0]]
    gain_attn = vectors[:, :OWN].reshape(D)
    gain_ffn = vectors[:, OWN : 2 * OWN].reshape(D)
    bias = vectors[:, 2 * OWN :].reshape(QKV)
    gate_rows, up_rows = own_rows(w_gate), own_rows(w_up)
    pieces = jnp.stack(
        [
            jnp.concatenate([gate_rows[:, s : s + WIN], up_rows[:, s : s + WIN]], axis=1)
            for s in STARTS
        ]
    )
    pieces = jnp.pad(pieces, ((0, 0), (0, 2), (0, 0)))
    pieces = lax.all_to_all(pieces, "group", split_axis=0, concat_axis=0, tiled=True)
    w_gu = lax.all_gather(pieces, "replica", axis=0, tiled=False)
    w_gu = jnp.transpose(w_gu[:, :, :CHUNK], (1, 0, 2, 3)).reshape(D, 2 * WIN)
    padded_down = lax.dynamic_update_slice(
        jnp.zeros((WIN, D), bf16), w_down, ((group_at % 2) * 64, 0)
    )
    return (w_qo, w_gu, padded_down, jnp.concatenate([bias, gain_attn, gain_ffn])[None])


def swap(value):
    return lax.ppermute(value, "section", [(0, 1), (1, 0)])


def weight_grads(token_pieces, row_pieces, vector_sum):
    perm = jnp.asarray(PERM, bf16)
    group_at = lax.axis_index("group")
    normed_one, grad_mixed, context, grad_attn = (
        token_pieces[:, :D],
        token_pieces[:, D : D + QKV],
        token_pieces[:, D + QKV : 2 * D + QKV],
        token_pieces[:, 2 * D + QKV :],
    )
    normed_all, grad_gu, activated, grad_mlp = (
        row_pieces[:, :D],
        row_pieces[:, D : D + 2 * WIN],
        row_pieces[:, D + 2 * WIN : D + 3 * WIN],
        row_pieces[:, D + 3 * WIN :],
    )

    def outer(left, right):
        return jnp.einsum("id,ie->de", left, right, preferred_element_type=f32).astype(bf16)

    left_one = dot(normed_one, perm).astype(bf16)
    left_out = dot(context, perm).astype(bf16)
    left_two = dot(normed_all, perm).astype(bf16)
    vec = vector_sum[0]
    rows = jnp.stack(
        [vec[:D].reshape(ZDEV, REPL, CHUNK), vec[D : 2 * D].reshape(ZDEV, REPL, CHUNK)], axis=2
    ).reshape(ZDEV, REPL, 2 * CHUNK)
    rows = jnp.concatenate([rows, vec[2 * D :].reshape(ZDEV, REPL, QKV // 64)], axis=2)
    rows = jnp.pad(rows, ((0, 0), (0, 0), (0, QKV - rows.shape[-1])))
    rows = jnp.transpose(rows, (1, 0, 2)).astype(bf16)
    spot = jnp.arange(16)[None, None, :, None] == CHUNK
    part_qkv = outer(left_one, grad_mixed).reshape(REPL, ZDEV, 16, QKV)
    part_qkv = jnp.where(spot, rows[:, :, None, :], part_qkv)
    part_out = outer(left_out, grad_attn).reshape(REPL, ZDEV, 16, D)
    part_gu = outer(left_two, grad_gu).reshape(REPL, ZDEV, 16, 2 * WIN)
    part_down = outer(activated, grad_mlp).reshape(REPL, WIN // REPL, D)

    def scatter(part):
        return lax.psum_scatter(part, "replica", scatter_dimension=0, tiled=False)

    part_qkv, part_out, part_gu, part_down = map(scatter, (part_qkv, part_out, part_gu, part_down))
    mixed = jnp.concatenate([part_qkv, part_out, part_gu], axis=-1)
    mixed = lax.all_to_all(mixed, "group", split_axis=0, concat_axis=0, tiled=True)
    joint = jnp.sum(mixed[:, :, : QKV + D].astype(f32), axis=0).astype(bf16)
    gate = jnp.concatenate(
        [mixed[z, :, QKV + D + SHIFTS[z] :][:, :BLOCK] for z in range(ZDEV)], axis=-1
    )
    up = jnp.concatenate(
        [mixed[z, :, QKV + D + WIN + SHIFTS[z] :][:, :BLOCK] for z in range(ZDEV)], axis=-1
    )
    final = jnp.concatenate([joint, gate, up], axis=-1)
    final = lax.all_gather(final, "replica", axis=0, tiled=False)
    final_down = lax.all_gather(part_down, "replica", axis=0, tiled=True)
    grad_down = lax.dynamic_slice_in_dim(final_down, (group_at % 2) * 64, BLOCK, 0)
    body = final[:, :CHUNK].reshape(OWN, final.shape[-1]).astype(f32)
    tail = final[:, CHUNK, :128].astype(f32)
    grad_gain_attn = tail[:, :CHUNK].reshape(OWN)
    grad_gain_ffn = tail[:, CHUNK : 2 * CHUNK].reshape(OWN)
    grad_bias = tail[:, 2 * CHUNK : 2 * CHUNK + QKV // 64].reshape(QKV // 4)
    return (
        body[:, :QKV],
        grad_bias,
        body[:, QKV : QKV + D],
        body[:, QKV + D : QKV + D + FF],
        body[:, QKV + D + FF :],
        grad_down.astype(f32),
        grad_gain_attn,
        grad_gain_ffn,
    )


def on_device(
    tokens, cotangent, doc_lengths, w_qkv, b_qkv, w_out, w_gate, w_up, w_down, norm_attn, norm_ffn
):
    section_at = lax.axis_index("section")
    group_at = lax.axis_index("group")
    first = section_at == 0
    own_set = gather_weights(
        w_qkv[0], b_qkv[0], w_out[0], w_gate[0], w_up[0], w_down[0], norm_attn[0], norm_ffn[0]
    )
    other_set = tuple(map(swap, own_set))

    def unpack(members):
        w_qo, w_gu, padded_down, vectors = members
        vectors = vectors[0].astype(f32)
        return (
            w_qo,
            w_gu,
            padded_down,
            vectors[:QKV],
            vectors[QKV : QKV + D],
            vectors[QKV + D :],
        )

    layer_sets = [
        unpack([jnp.where(first, a, b) for a, b in zip(own_set, other_set)]),
        unpack([jnp.where(first, b, a) for a, b in zip(own_set, other_set)]),
    ]
    own_tokens = lax.dynamic_index_in_dim(tokens, section_at, 0, keepdims=False)[0]
    own_cotangent = lax.dynamic_index_in_dim(cotangent, section_at, 0, keepdims=False)[0]
    lengths = lax.dynamic_index_in_dim(doc_lengths, section_at, 0, keepdims=False)[0]
    tables = doc_tables(lengths, group_at)
    out_first, kept_first = layer_forward(own_tokens, layer_sets[0], tables)
    out_second, kept_second = layer_forward(out_first, layer_sets[1], tables)
    grad_second, pieces_second = layer_backward(
        own_cotangent.astype(f32), kept_second, layer_sets[1], tables
    )
    grad_second = grad_second.astype(bf16)
    grad_first, pieces_first = layer_backward(
        grad_second.astype(f32), kept_first, layer_sets[0], tables
    )
    sent = [jnp.where(first, b, a) for a, b in zip(pieces_first, pieces_second)]
    kept = [jnp.where(first, a, b) for a, b in zip(pieces_first, pieces_second)]
    got = [swap(member) for member in sent]
    token_pieces = jnp.concatenate([kept[0], got[0]], axis=0)
    row_pieces = jnp.concatenate([kept[1], got[1]], axis=0)
    grads = weight_grads(token_pieces, row_pieces, kept[2] + got[2])

    def placed(lead, second):
        mine = jnp.where(first, lead, second)
        theirs = swap(jnp.where(first, second, lead))
        return jnp.stack([jnp.where(first, mine, theirs), jnp.where(first, theirs, mine)])

    acts = placed(out_first, out_second)
    input_grads = placed(grad_first, grad_second.astype(f32))
    return (acts[None, :, None], input_grads[None, :, None]) + tuple(g[None] for g in grads)


def solution(mesh):
    rows = P("section", "group", None)
    vector = P("section", "group")
    spans = P("section", None, "replica", "group", None)
    return jax.shard_map(
        on_device,
        mesh=mesh,
        in_specs=(
            P(None, "replica", "group", None),
            P(None, "replica", "group", None),
            P(None, "replica", None),
            rows,
            vector,
            rows,
            rows,
            rows,
            rows,
            vector,
            vector,
        ),
        out_specs=(spans, spans, rows, vector, rows, rows, rows, rows, vector, vector),
        check_vma=False,
    )
```

```python
import jax
import jax.numpy as jnp
from jax import lax
from jax.experimental import pallas as pl
from jax.experimental.pallas import tpu as pltpu
from jax.sharding import PartitionSpec as P

HEADS = 14
KV_HEADS = 2
HEAD_DIM = 64
GROUPS = HEADS // KV_HEADS
D = 896
FF = 4864
QKV = 1152
SPAN = 64
ROW = 256
REPL = 16
ZDEV = 4
OWN = D // ZDEV
CHUNK = OWN // REPL
BLOCK = FF // ZDEV
WIN = 1280
STARTS = [128 * ((19 * z) // 2) for z in range(ZDEV)]
SHIFTS = [BLOCK * z - STARTS[z] for z in range(ZDEV)]
KV_WIDTH = KV_HEADS * HEAD_DIM

eps = 1e-06
rope_base = 1000000.0
f32 = jnp.float32
bf16 = jnp.bfloat16

def rms_scale(values):
    return lax.rsqrt(jnp.mean(values * values, axis=-1, keepdims=True) + eps)


def rotate_half(values):
    half_len = values.shape[-1] // 2
    return jnp.concatenate([-values[..., half_len:], values[..., :half_len]], axis=-1)


def norm_back(grad_norm, values, scale_rows, gain_vec):
    scaled = grad_norm * gain_vec
    row_inner = jnp.mean(scaled * values, axis=-1, keepdims=True)
    grad_in = scale_rows * (scaled - values * scale_rows * scale_rows * row_inner)
    grad_gain = jnp.sum(grad_norm * values * scale_rows, axis=0)
    return (grad_in, grad_gain)


def doc_tables(doc_lens, group_at):
    doc_ends = jnp.cumsum(doc_lens)
    doc_starts = doc_ends - doc_lens
    row_spots = jnp.arange(ROW, dtype=jnp.int32)
    segment = jnp.sum((doc_ends[None, :] <= row_spots[:, None]).astype(jnp.int32), axis=1)
    doc_pick = segment[:, None] == jnp.arange(doc_lens.shape[0], dtype=jnp.int32)[None, :]
    doc_begin = jnp.sum(jnp.where(doc_pick, doc_starts[None, :], 0), axis=1)
    first_row = group_at * SPAN
    own_segment = lax.dynamic_slice_in_dim(segment, first_row, SPAN)
    own_spots = lax.dynamic_slice_in_dim(row_spots, first_row, SPAN)
    own_begin = lax.dynamic_slice_in_dim(doc_begin, first_row, SPAN)
    allowed = (own_segment[:, None] == segment[None, :]) & (
        row_spots[None, :] <= own_spots[:, None]
    )
    inv_freqs = rope_base ** (-jnp.arange(0, HEAD_DIM, 2, dtype=f32) / HEAD_DIM)
    angles = (own_spots - own_begin).astype(f32)[:, None] * inv_freqs[None, :]
    angles = jnp.concatenate([angles, angles], axis=1)
    return (allowed, jnp.cos(angles)[:, None, :], jnp.sin(angles)[:, None, :])


def split_kv(all_kv):
    key_rows = all_kv[:, :KV_WIDTH].reshape(ROW, KV_HEADS, HEAD_DIM)
    value_rows = all_kv[:, KV_WIDTH:].reshape(ROW, KV_HEADS, HEAD_DIM)
    return (key_rows, value_rows)


def score_block(query_rot, key_rows, allowed):
    grouped = query_rot.reshape(SPAN, KV_HEADS, GROUPS, HEAD_DIM)
    scores = (
        jnp.einsum("ikgd,jkd->kgij", grouped, key_rows, preferred_element_type=f32)
        * HEAD_DIM ** (-0.5)
    )
    return jnp.where(allowed[None, None], scores, -jnp.inf)


def dot(left, right):
    return jnp.dot(left, right, preferred_element_type=f32)


def dot_t(left, right):
    return jnp.einsum("id,ed->ie", left, right, preferred_element_type=f32)


def layer_forward(entering, weights, tables):
    w_qo, w_gu, w_down, b_qkv, gain_attn, gain_ffn = weights
    allowed, cosine, sine_table = tables
    values = entering.astype(f32)
    scale_one = rms_scale(values)
    normed_one = (values * scale_one * gain_attn).astype(bf16)
    mixed_qkv = dot(normed_one, w_qo[:, :QKV]) + b_qkv
    query_pre = mixed_qkv[:, :D].reshape(SPAN, HEADS, HEAD_DIM)
    key_pre = mixed_qkv[:, D : D + KV_WIDTH].reshape(SPAN, KV_HEADS, HEAD_DIM)
    query_rot = (query_pre * cosine + rotate_half(query_pre) * sine_table).astype(bf16)
    key_rot = (key_pre * cosine + rotate_half(key_pre) * sine_table).astype(bf16)
    local_kv = jnp.concatenate(
        [key_rot.reshape(SPAN, KV_WIDTH), mixed_qkv[:, D + KV_WIDTH :].astype(bf16)], axis=1
    )
    all_kv = lax.all_gather(local_kv, "group", axis=0, tiled=True)
    key_rows, value_rows = split_kv(all_kv)
    scores = score_block(query_rot, key_rows, allowed)
    row_top = jnp.max(scores, axis=-1, keepdims=True)
    log_total = row_top + jnp.log(jnp.sum(jnp.exp(scores - row_top), axis=-1, keepdims=True))
    attn_probs = jnp.exp(scores - log_total).astype(bf16)
    context = jnp.einsum("kgij,jkd->ikgd", attn_probs, value_rows, preferred_element_type=f32)
    context = context.reshape(SPAN, D).astype(bf16)
    hidden = values + dot(context, w_qo[:, QKV:])
    scale_two = rms_scale(hidden)
    normed_two = (hidden * scale_two * gain_ffn).astype(bf16)
    normed_all = lax.all_gather(normed_two, "group", axis=0, tiled=True)
    gate_up = dot(normed_all, w_gu)
    gate_proj, up_proj = gate_up[:, :WIN], gate_up[:, WIN:]
    activated = (jax.nn.silu(gate_proj) * up_proj).astype(bf16)
    partial = dot(activated, w_down).astype(bf16)
    mlp = lax.psum_scatter(partial, "group", scatter_dimension=0, tiled=True).astype(f32)
    output = (hidden + mlp).astype(bf16)
    kept = (values, scale_one, normed_one, query_rot, all_kv, log_total, context, hidden)
    kept = kept + (scale_two, normed_all, gate_up, activated)
    return (output, kept)


def layer_backward(grad_out, kept, weights, tables):
    values, scale_one, normed_one, query_rot, all_kv, log_total, context, hidden = kept[:8]
    scale_two, normed_all, gate_up, activated = kept[8:]
    w_qo, w_gu, w_down, b_qkv, gain_attn, gain_ffn = weights
    allowed, cosine, sine_table = tables
    gate_proj, up_proj = gate_up[:, :WIN], gate_up[:, WIN:]
    grad_mlp = grad_out.astype(bf16)
    grad_mlp_all = lax.all_gather(grad_mlp, "group", axis=0, tiled=True)
    grad_act = dot_t(grad_mlp_all, w_down)
    sigma_gate = jax.nn.sigmoid(gate_proj)
    silu_gate = gate_proj * sigma_gate
    grad_gate = grad_act * up_proj * sigma_gate * (1.0 + gate_proj * (1.0 - sigma_gate))
    grad_up = grad_act * silu_gate
    grad_gu = jnp.concatenate([grad_gate.astype(bf16), grad_up.astype(bf16)], axis=1)
    partial = dot_t(grad_gu, w_gu).astype(bf16)
    grad_norm_two = lax.psum_scatter(
        partial, "group", scatter_dimension=0, tiled=True
    ).astype(f32)
    back_two, grad_gain_ffn = norm_back(grad_norm_two, hidden, scale_two, gain_ffn)
    grad_hidden = grad_out + back_two
    grad_attn = grad_hidden.astype(bf16)
    grad_context = dot_t(grad_attn, w_qo[:, QKV:]).astype(bf16)
    grad_context = grad_context.reshape(SPAN, KV_HEADS, GROUPS, HEAD_DIM)
    key_rows, value_rows = split_kv(all_kv)
    grouped = query_rot.reshape(SPAN, KV_HEADS, GROUPS, HEAD_DIM)
    attn_probs = jnp.exp(score_block(query_rot, key_rows, allowed) - log_total)
    grad_probs = jnp.einsum("ikgd,jkd->kgij", grad_context, value_rows, preferred_element_type=f32)
    row_inner = jnp.sum(attn_probs * grad_probs, axis=-1, keepdims=True)
    grad_scores = (attn_probs * (grad_probs - row_inner)).astype(bf16)
    score_scale = HEAD_DIM ** (-0.5)
    grad_query = jnp.einsum("kgij,jkd->ikgd", grad_scores, key_rows, preferred_element_type=f32)
    grad_query = grad_query.reshape(SPAN, HEADS, HEAD_DIM) * score_scale
    grad_key_all = (
        jnp.einsum("kgij,ikgd->jkd", grad_scores, grouped, preferred_element_type=f32)
        * score_scale
    )
    grad_value_all = jnp.einsum(
        "kgij,ikgd->jkd", attn_probs.astype(bf16), grad_context, preferred_element_type=f32
    )
    grad_kv_all = jnp.concatenate(
        [grad_key_all.reshape(ROW, KV_WIDTH), grad_value_all.reshape(ROW, KV_WIDTH)], axis=1
    )
    grad_kv = lax.psum_scatter(
        grad_kv_all.astype(bf16), "group", scatter_dimension=0, tiled=True
    ).astype(f32)
    grad_key = grad_kv[:, :KV_WIDTH].reshape(SPAN, KV_HEADS, HEAD_DIM)
    query_back = grad_query * cosine - rotate_half(grad_query * sine_table)
    key_back = grad_key * cosine - rotate_half(grad_key * sine_table)
    grad_mixed = jnp.concatenate(
        [query_back.reshape(SPAN, D), key_back.reshape(SPAN, KV_WIDTH), grad_kv[:, KV_WIDTH:]],
        axis=1,
    ).astype(bf16)
    grad_bias = jnp.sum(grad_mixed.astype(f32), axis=0)
    grad_norm_one = dot_t(grad_mixed, w_qo[:, :QKV])
    back_one, grad_gain_attn = norm_back(grad_norm_one, values, scale_one, gain_attn)
    grad_in = grad_hidden + back_one
    pieces = (
        jnp.concatenate([normed_one, grad_mixed, context, grad_attn], axis=1),
        jnp.concatenate([normed_all, grad_gu, activated, grad_mlp_all], axis=1),
        jnp.concatenate([grad_gain_attn, grad_gain_ffn, grad_bias])[None],
    )
    return (grad_in, pieces)


def gather_weights(w_qkv, b_qkv, w_out, w_gate, w_up, w_down, norm_attn, norm_ffn):
    group_at = lax.axis_index("group")
    replica_at = lax.axis_index("replica")

    def own_rows(block):
        return lax.dynamic_slice_in_dim(block, replica_at * CHUNK, CHUNK, 0)

    vectors = jnp.concatenate([norm_attn, norm_ffn, b_qkv])
    joint = jnp.concatenate([own_rows(w_qkv), own_rows(w_out)], axis=1)
    extra = jnp.zeros((2, joint.shape[1]), bf16)
    extra = lax.dynamic_update_slice(extra, vectors[None], (0, 0))
    joint = jnp.concatenate([joint, extra], axis=0)
    joint = lax.all_gather(joint, ("group", "replica"), axis=0, tiled=False)
    joint = joint.reshape(ZDEV, REPL, 16, joint.shape[-1])
    w_qo = joint[:, :, :CHUNK].reshape(D, QKV + D)
    vectors = joint[:, 0, CHUNK, : vectors.shape[0]]
    gain_attn = vectors[:, :OWN].reshape(D)
    gain_ffn = vectors[:, OWN : 2 * OWN].reshape(D)
    bias = vectors[:, 2 * OWN :].reshape(QKV)
    gate_rows, up_rows = own_rows(w_gate), own_rows(w_up)
    pieces = jnp.stack(
        [
            jnp.concatenate([gate_rows[:, s : s + WIN], up_rows[:, s : s + WIN]], axis=1)
            for s in STARTS
        ]
    )
    pieces = jnp.pad(pieces, ((0, 0), (0, 2), (0, 0)))
    pieces = lax.all_to_all(pieces, "group", split_axis=0, concat_axis=0, tiled=True)
    w_gu = lax.all_gather(pieces, "replica", axis=0, tiled=False)
    w_gu = jnp.transpose(w_gu[:, :, :CHUNK], (1, 0, 2, 3)).reshape(D, 2 * WIN)
    padded_down = lax.dynamic_update_slice(
        jnp.zeros((WIN, D), bf16), w_down, ((group_at % 2) * 64, 0)
    )
    return (w_qo, w_gu, padded_down, jnp.concatenate([bias, gain_attn, gain_ffn])[None])


def swap(value):
    return lax.ppermute(value, "section", [(0, 1), (1, 0)])


MESH = pl.DeviceIdType.MESH
TILES_R = OWN // 16
COLS = 15232
PART_A = (0, 7680)
PART_B = (7680, 12928)
PART_C = (12928, 15232)
DOWN_AT = 4 * 2 * WIN
QO_AT = PART_C[0]
VEC_AT = QO_AT + QKV + D
RING = 4


def halves(start, stop):
    middle = start + ((stop - start) // 128 + 1) // 2 * 128
    return ((start, middle), (middle, stop))


def ring_spot(spot, steps):
    return lax.rem(spot + steps + RING, RING)


class Links:
    def __init__(self, send_sems, recv_sems):
        self.send_sems, self.recv_sems, self.used, self.started = send_sems, recv_sems, 0, []

    def take(self, count):
        first = self.used
        self.used += count
        return first

    def copy(self, source, target, sem_at, device):
        return pltpu.make_async_remote_copy(
            src_ref=source,
            dst_ref=target,
            send_sem=self.send_sems.at[sem_at],
            recv_sem=self.recv_sems.at[sem_at],
            device_id=device,
            device_id_type=MESH,
        )

    def send(self, source, target, sem_at, device):
        copy = self.copy(source, target, sem_at, device)
        copy.start()
        self.started.append(copy)

    def arrived(self, target, sem_at, device):
        self.copy(target, target, sem_at, device).wait_recv()

    def finish(self):
        for copy in self.started:
            copy.wait_send()
        self.started = []


class RingSum:
    def __init__(self, links, spot, device_at, block, first, second, left, right, add):
        self.links, self.spot, self.block, self.add = links, spot, block, add
        self.right, self.left = device_at(ring_spot(spot, 1)), device_at(ring_spot(spot, -1))
        self.first, self.second, self.from_left, self.from_right = first, second, left, right
        self.sem = links.take(6)

    def start(self):
        send, sem, spot = self.links.send, self.sem, self.spot
        far = ring_spot(spot, 2)
        send(self.block(far, 0), self.first, sem, self.right)
        send(self.block(far, 1), self.second, sem + 1, self.left)
        send(self.block(ring_spot(spot, 1), 1), self.from_left(1), sem + 2, self.right)
        send(self.block(ring_spot(spot, -1), 0), self.from_right(0), sem + 3, self.left)

    def middle(self):
        links, sem, spot = self.links, self.sem, self.spot
        links.arrived(self.first, sem, self.right)
        onward = self.block(ring_spot(spot, 1), 0)
        self.add(onward, onward, self.first)
        links.send(onward, self.from_left(0), sem + 4, self.right)
        links.arrived(self.second, sem + 1, self.left)
        onward = self.block(ring_spot(spot, -1), 1)
        self.add(onward, onward, self.second)
        links.send(onward, self.from_right(1), sem + 5, self.left)

    def end(self, result):
        links, sem, spot = self.links, self.sem, self.spot
        links.arrived(self.from_left(1), sem + 2, self.right)
        links.arrived(self.from_right(0), sem + 3, self.left)
        links.arrived(self.from_left(0), sem + 4, self.right)
        links.arrived(self.from_right(1), sem + 5, self.left)
        for half in (0, 1):
            self.add(
                result(half), self.block(spot, half), self.from_left(half), self.from_right(half)
            )


class RingShare:
    def __init__(self, links, spot, device_at, block):
        self.links, self.spot, self.block = links, spot, block
        self.right, self.left = device_at(ring_spot(spot, 1)), device_at(ring_spot(spot, -1))
        self.sem = links.take(6)

    def start(self):
        send, sem = self.links.send, self.sem
        low, high = self.block(self.spot, 0), self.block(self.spot, 1)
        send(low, low, sem, self.right)
        send(high, high, sem + 2, self.left)
        send(high, high, sem + 1, self.right)
        send(low, low, sem + 3, self.left)

    def middle(self):
        links, sem, spot = self.links, self.sem, self.spot
        low = self.block(ring_spot(spot, -1), 0)
        links.arrived(low, sem, self.right)
        links.send(low, low, sem + 4, self.right)
        high = self.block(ring_spot(spot, 1), 1)
        links.arrived(high, sem + 2, self.left)
        links.send(high, high, sem + 5, self.left)

    def end(self):
        links, sem, spot = self.links, self.sem, self.spot
        links.arrived(self.block(ring_spot(spot, -1), 1), sem + 1, self.right)
        links.arrived(self.block(ring_spot(spot, 1), 0), sem + 3, self.left)
        links.arrived(self.block(ring_spot(spot, 2), 0), sem + 4, self.right)
        links.arrived(self.block(ring_spot(spot, 2), 1), sem + 5, self.left)


def add_into(target, *sources):
    if len(target.shape) == 3:
        for at in range(target.shape[0]):
            add_into(target.at[at], *[source.at[at] for source in sources])
        return
    total = sources[0][...].astype(f32)
    for source in sources[1:]:
        total = total + source[...].astype(f32)
    target[...] = total.astype(target.dtype)


def greet(replica_spots, group_spots):
    barrier = pltpu.get_barrier_semaphore()
    for spot in replica_spots:
        pl.semaphore_signal(barrier, inc=1, device_id={"replica": spot}, device_id_type=MESH)
    for spot in group_spots:
        pl.semaphore_signal(barrier, inc=1, device_id={"group": spot}, device_id_type=MESH)
    pl.semaphore_wait(barrier, len(replica_spots) + len(group_spots))


def grads_kernel(
    n2t, dgu, act, dmlp, left_rows, right_rows, vec,
    shared, part, own, zbuf, left_all, right_all, vec_all,
    a_first, a_second, a_left, a_right, a_sum, a_first2, a_second2, a_left2, a_right2,
    b_first, b_second, b_left, b_right, b_sum, b_first2, b_second2, b_left2, b_right2,
    c_first, c_second, c_left, c_right, c_sum, c_first2, c_second2, c_left2, c_right2,
    send_sems, recv_sems,
):
    group_at = lax.axis_index("group")
    replica_at = lax.axis_index("replica")
    x_at, y_at = replica_at // RING, lax.rem(replica_at, RING)
    links = Links(send_sems, recv_sems)

    def along_x(spot):
        return {"replica": spot * RING + y_at}

    def along_y(spot):
        return {"replica": x_at * RING + spot}

    peers = [ring_spot(group_at, step) for step in (1, 2, 3)]
    greet(
        [
            ring_spot(x_at, 1) * RING + y_at,
            ring_spot(x_at, -1) * RING + y_at,
            x_at * RING + ring_spot(y_at, 1),
            x_at * RING + ring_spot(y_at, -1),
        ],
        peers,
    )
    tok_sem = links.take(9)
    for step, peer in enumerate(peers):
        for at, (source, target) in enumerate(
            [
                (left_rows.at[peer], left_all.at[group_at]),
                (right_rows, right_all.at[group_at]),
                (vec, vec_all.at[group_at]),
            ]
        ):
            links.send(source, target, tok_sem + 3 * step + at, {"group": peer})
    left_all[group_at] = left_rows[group_at]
    right_all[group_at] = right_rows[...]
    vec_all[group_at] = vec[...]

    def gate_up(tile, carry):
        at = pl.multiple_of(tile * 256, 256)
        block = jnp.dot(n2t[...], dgu[:, pl.ds(at, 256)], preferred_element_type=f32).astype(bf16)
        block = block.reshape(ZDEV, TILES_R, 16, 256)
        for z in range(ZDEV):
            where = pl.multiple_of(tile * 256 + z * 2 * WIN, 128)
            for r in range(TILES_R):
                part[r // RING, r % RING, :, pl.ds(where, 256)] = block[z, r]
        return carry

    lax.fori_loop(0, 2 * WIN // 256, gate_up, 0)
    shift = lax.rem(group_at, 2) * 64
    for quarter in range(4):
        rows = pl.ds(pl.multiple_of(shift + 304 * quarter, 16), 304)
        block = jnp.dot(act[rows, :], dmlp[...], preferred_element_type=f32).astype(bf16)
        block = block.reshape(19, 16, D)
        for inner in range(19):
            tile = 19 * quarter + inner
            if tile < 3 * TILES_R:
                r, at = tile // 3, DOWN_AT + D * (tile % 3)
            else:
                r, at = TILES_R + (tile - 3 * TILES_R) // 17, D * ((tile - 3 * TILES_R) % 17)
            part[r // RING, r % RING, :, at : at + D] = block[inner]

    def summers(cols, x_first, bufs):
        first, second, left, right, total, first2, second2, left2, right2 = bufs
        start, stop = cols

        def big(spot, half):
            span = pl.ds(2 * half, 2)
            if x_first:
                return part.at[spot, span, :, start:stop]
            return part.at[span, spot, :, start:stop]

        cuts = halves(0, stop - start)

        def small(spot, half):
            return total.at[spot, :, cuts[half][0] : cuts[half][1]]

        def pair(buf):
            return lambda half: buf.at[pl.ds(2 * half, 2)]

        def cut(buf):
            return lambda half: buf.at[:, cuts[half][0] : cuts[half][1]]

        one = (x_at, along_x) if x_first else (y_at, along_y)
        two = (y_at, along_y) if x_first else (x_at, along_x)
        stage_one = RingSum(
            links, *one, big, first, second, pair(left), pair(right), add_into
        )
        stage_two = RingSum(
            links, *two, small, first2, second2, cut(left2), cut(right2), add_into
        )

        def result(half):
            return own.at[:, start + cuts[half][0] : start + cuts[half][1]]

        return stage_one, stage_two, pair(total), result

    a_one, a_two, a_mid, a_result = summers(
        PART_A, True,
        (a_first, a_second, a_left, a_right, a_sum, a_first2, a_second2, a_left2, a_right2),
    )
    b_one, b_two, b_mid, b_result = summers(
        PART_B, False,
        (b_first, b_second, b_left, b_right, b_sum, b_first2, b_second2, b_left2, b_right2),
    )
    c_one, c_two, c_mid, c_result = summers(
        PART_C, False,
        (c_first, c_second, c_left, c_right, c_sum, c_first2, c_second2, c_left2, c_right2),
    )
    a_one.start()
    b_one.start()
    a_one.middle()
    b_one.middle()
    for step, peer in enumerate(peers):
        source = ring_spot(group_at, -1 - step)
        for at, target in enumerate((left_all, right_all, vec_all)):
            links.arrived(target.at[source], tok_sem + 3 * step + at, {"group": peer})
    for width, col, row in ((QKV, 0, 0), (D, QKV, OWN)):
        total = jnp.dot(
            left_all[0, row : row + OWN], right_all[0, :, col : col + width],
            preferred_element_type=f32,
        )
        for z in range(1, ZDEV):
            total = total + jnp.dot(
                left_all[z, row : row + OWN], right_all[z, :, col : col + width],
                preferred_element_type=f32,
            )
        total = total.astype(bf16).reshape(TILES_R, 16, width)
        for r in range(TILES_R):
            part[r // RING, r % RING, :, QO_AT + col : QO_AT + col + width] = total[r]
    part[0, 0, :, VEC_AT:COLS] = (
        vec_all[0] + vec_all[1] + vec_all[2] + vec_all[3]
    ).astype(bf16)
    for r in range(1, TILES_R):
        part[r // RING, r % RING, :, VEC_AT:COLS] = jnp.zeros((16, COLS - VEC_AT), bf16)
    c_one.start()
    a_one.end(a_mid)
    a_two.start()
    b_one.end(b_mid)
    b_two.start()
    c_one.middle()
    a_two.middle()
    b_two.middle()
    c_one.end(c_mid)
    c_two.start()
    a_two.end(a_result)
    b_two.end(b_result)
    slot_sem = links.take(3)
    for step, peer in enumerate(peers):
        where = pl.multiple_of(peer * 2 * WIN, 128)
        links.send(
            own.at[:, pl.ds(where, 2 * WIN)], zbuf.at[group_at], slot_sem + step, {"group": peer}
        )
    where = pl.multiple_of(group_at * 2 * WIN, 128)
    zbuf[group_at] = own[:, pl.ds(where, 2 * WIN)]
    c_two.middle()
    c_two.end(c_result)
    for step, peer in enumerate(peers):
        links.arrived(zbuf.at[ring_spot(group_at, -1 - step)], slot_sem + step, {"group": peer})

    @pl.when(replica_at < TILES_R)
    def _():
        for which in (0, 1):
            base, at = which * FF, which * WIN
            for z in range(ZDEV):
                low = 128 if z % 2 else 0
                high = WIN if z % 2 else WIN - 128
                to = base + STARTS[z]
                shared[x_at, y_at, :, to + low : to + high] = zbuf[z, :, at + low : at + high]
            for z in (0, 2):
                to = base + STARTS[z + 1]
                shared[x_at, y_at, :, to : to + 128] = (
                    zbuf[z, :, at + WIN - 128 : at + WIN] + zbuf[z + 1, :, at : at + 128]
                )
        shared[x_at, y_at, :, 2 * FF : 2 * FF + 512] = jnp.zeros((16, 512), bf16)
        shared[x_at, y_at, :, DOWN_AT:COLS] = own[:, DOWN_AT:COLS]

    @pl.when(replica_at >= TILES_R)
    def _():
        shared[x_at, y_at] = own[...]

    def sharers(cols, x_first):
        start, stop = cols
        cuts = halves(start, stop)

        def small(spot, half):
            low, high = cuts[half]
            if x_first:
                return shared.at[spot, y_at, :, low:high]
            return shared.at[x_at, spot, :, low:high]

        def big(spot, half):
            span = pl.ds(2 * half, 2)
            if x_first:
                return shared.at[span, spot, :, start:stop]
            return shared.at[spot, span, :, start:stop]

        one = (x_at, along_x) if x_first else (y_at, along_y)
        two = (y_at, along_y) if x_first else (x_at, along_x)
        return RingShare(links, *one, small), RingShare(links, *two, big)

    a_one, a_two = sharers((0, 7680), False)
    b_one, b_two = sharers((7680, COLS), True)
    a_one.start()
    b_one.start()
    a_one.middle()
    b_one.middle()
    a_one.end()
    a_two.start()
    b_one.end()
    b_two.start()
    a_two.middle()
    b_two.middle()
    a_two.end()
    b_two.end()
    links.finish()


def share_grads(n2t, dgu, act, dmlp, left_rows, right_rows, vec):
    def bufs(cols):
        width = cols[1] - cols[0]
        low, high = [b - a for a, b in halves(0, width)]
        shapes = [(2, 16, width), (2, 16, width), (4, 16, width), (4, 16, width), (4, 16, width)]
        shapes = shapes + [(16, low), (16, high), (16, width), (16, width)]
        return [pltpu.VMEM(shape, bf16) for shape in shapes]

    vmem = pl.BlockSpec(memory_space=pltpu.VMEM)
    sems = 9 + 3 + 6 * 6 + 4 * 6
    return pl.pallas_call(
        grads_kernel,
        out_shape=jax.ShapeDtypeStruct((RING, RING, 16, COLS), bf16),
        in_specs=[vmem] * 7,
        out_specs=vmem,
        scratch_shapes=[
            pltpu.VMEM((RING, RING, 16, COLS), bf16),
            pltpu.VMEM((16, COLS), bf16),
            pltpu.VMEM((ZDEV, 16, 2 * WIN), bf16),
            pltpu.VMEM((ZDEV, 2 * OWN, 2 * SPAN), bf16),
            pltpu.VMEM((ZDEV, 2 * SPAN, QKV + D), bf16),
            pltpu.VMEM((ZDEV, 16, 256), f32),
            *bufs(PART_A),
            *bufs(PART_B),
            *bufs(PART_C),
            pltpu.SemaphoreType.DMA((sems,)),
            pltpu.SemaphoreType.DMA((sems,)),
        ],
        compiler_params=pltpu.CompilerParams(
            collective_id=1, has_side_effects=True, vmem_limit_bytes=58 * 1024 * 1024
        ),
        name="grads",
    )(n2t, dgu, act, dmlp, left_rows, right_rows, vec)


def weight_grads(token_pieces, row_pieces, vector_sum):
    group_at = lax.axis_index("group")
    normed_all = row_pieces[:, :D]
    grad_gu = row_pieces[:, D : D + 2 * WIN]
    activated = row_pieces[:, D + 2 * WIN : D + 3 * WIN]
    grad_mlp = row_pieces[:, D + 3 * WIN :]
    lefts = jnp.concatenate(
        [
            token_pieces[:, :D].reshape(2 * SPAN, ZDEV, OWN),
            token_pieces[:, D + QKV : 2 * D + QKV].reshape(2 * SPAN, ZDEV, OWN),
        ],
        axis=2,
    )
    rights = jnp.concatenate(
        [token_pieces[:, D : D + QKV], token_pieces[:, 2 * D + QKV :]], axis=1
    )
    vec = jnp.pad(vector_sum[0], (0, 16 * 256 - vector_sum.shape[1])).reshape(16, 256)
    shared = share_grads(
        normed_all.T, grad_gu, activated.T, grad_mlp, jnp.transpose(lefts, (1, 2, 0)), rights, vec
    )
    shared = shared.reshape(REPL, 16, COLS)

    def rows_of(start, width):
        block = shared[:TILES_R, :, start : start + width]
        return block.reshape(OWN, width).astype(f32)

    lead = shared[:TILES_R, :, DOWN_AT : DOWN_AT + 3 * D].reshape(TILES_R, 16, 3, D)
    rest = shared[TILES_R:].reshape(2, 16, 17, D)
    grad_down = jnp.concatenate(
        [
            jnp.transpose(lead, (0, 2, 1, 3)).reshape(-1, D),
            jnp.transpose(rest, (0, 2, 1, 3)).reshape(-1, D),
        ]
    ).astype(f32)
    vec = shared[0, :, VEC_AT:].reshape(16 * 256).astype(f32)

    def own_part(start, width):
        return lax.dynamic_slice_in_dim(vec, start + group_at * width, width, 0)

    return (
        rows_of(QO_AT, QKV),
        own_part(2 * D, QKV // ZDEV),
        rows_of(QO_AT + QKV, D),
        rows_of(0, FF),
        rows_of(FF, FF),
        grad_down,
        own_part(0, OWN),
        own_part(D, OWN),
    )


def on_device(
    tokens, cotangent, doc_lengths, w_qkv, b_qkv, w_out, w_gate, w_up, w_down, norm_attn, norm_ffn
):
    section_at = lax.axis_index("section")
    group_at = lax.axis_index("group")
    first = section_at == 0
    own_set = gather_weights(
        w_qkv[0], b_qkv[0], w_out[0], w_gate[0], w_up[0], w_down[0], norm_attn[0], norm_ffn[0]
    )
    other_set = tuple(map(swap, own_set))

    def unpack(members):
        w_qo, w_gu, padded_down, vectors = members
        vectors = vectors[0].astype(f32)
        return (
            w_qo,
            w_gu,
            padded_down,
            vectors[:QKV],
            vectors[QKV : QKV + D],
            vectors[QKV + D :],
        )

    layer_sets = [
        unpack([jnp.where(first, a, b) for a, b in zip(own_set, other_set)]),
        unpack([jnp.where(first, b, a) for a, b in zip(own_set, other_set)]),
    ]
    own_tokens = lax.dynamic_index_in_dim(tokens, section_at, 0, keepdims=False)[0]
    own_cotangent = lax.dynamic_index_in_dim(cotangent, section_at, 0, keepdims=False)[0]
    lengths = lax.dynamic_index_in_dim(doc_lengths, section_at, 0, keepdims=False)[0]
    tables = doc_tables(lengths, group_at)
    out_first, kept_first = layer_forward(own_tokens, layer_sets[0], tables)
    out_second, kept_second = layer_forward(out_first, layer_sets[1], tables)
    grad_second, pieces_second = layer_backward(
        own_cotangent.astype(f32), kept_second, layer_sets[1], tables
    )
    grad_second = grad_second.astype(bf16)
    grad_first, pieces_first = layer_backward(
        grad_second.astype(f32), kept_first, layer_sets[0], tables
    )
    sent = [jnp.where(first, b, a) for a, b in zip(pieces_first, pieces_second)]
    kept = [jnp.where(first, a, b) for a, b in zip(pieces_first, pieces_second)]
    got = [swap(member) for member in sent]
    token_pieces = jnp.concatenate([kept[0], got[0]], axis=0)
    row_pieces = jnp.concatenate([kept[1], got[1]], axis=0)
    grads = weight_grads(token_pieces, row_pieces, kept[2] + got[2])

    def placed(lead, second):
        mine = jnp.where(first, lead, second)
        theirs = swap(jnp.where(first, second, lead))
        return jnp.stack([jnp.where(first, mine, theirs), jnp.where(first, theirs, mine)])

    acts = placed(out_first, out_second)
    input_grads = placed(grad_first, grad_second.astype(f32))
    return (acts[None, :, None], input_grads[None, :, None]) + tuple(g[None] for g in grads)


def solution(mesh):
    rows = P("section", "group", None)
    vector = P("section", "group")
    spans = P("section", None, "replica", "group", None)
    return jax.shard_map(
        on_device,
        mesh=mesh,
        in_specs=(
            P(None, "replica", "group", None),
            P(None, "replica", "group", None),
            P(None, "replica", None),
            rows,
            vector,
            rows,
            rows,
            rows,
            rows,
            vector,
            vector,
        ),
        out_specs=(spans, spans, rows, vector, rows, rows, rows, rows, vector, vector),
        check_vma=False,
    )
```

```python
import jax
import jax.numpy as jnp
from jax import lax
from jax.experimental import pallas as pl
from jax.experimental.pallas import tpu as pltpu
from jax.sharding import PartitionSpec as P

HEADS = 14
KV_HEADS = 2
HEAD_DIM = 64
GROUPS = HEADS // KV_HEADS
D = 896
FF = 4864
QKV = 1152
SPAN = 64
ROW = 256
REPL = 16
ZDEV = 4
OWN = D // ZDEV
CHUNK = OWN // REPL
BLOCK = FF // ZDEV
WIN = 1280
STARTS = [128 * ((19 * z) // 2) for z in range(ZDEV)]
SHIFTS = [BLOCK * z - STARTS[z] for z in range(ZDEV)]
KV_WIDTH = KV_HEADS * HEAD_DIM

eps = 1e-06
rope_base = 1000000.0
f32 = jnp.float32
bf16 = jnp.bfloat16

def rms_scale(values):
    return lax.rsqrt(jnp.mean(values * values, axis=-1, keepdims=True) + eps)


def doc_tables(doc_lens, group_at):
    doc_ends = jnp.cumsum(doc_lens)
    doc_starts = doc_ends - doc_lens
    row_spots = jnp.arange(ROW, dtype=jnp.int32)
    segment = jnp.sum((doc_ends[None, :] <= row_spots[:, None]).astype(jnp.int32), axis=1)
    doc_pick = segment[:, None] == jnp.arange(doc_lens.shape[0], dtype=jnp.int32)[None, :]
    doc_begin = jnp.sum(jnp.where(doc_pick, doc_starts[None, :], 0), axis=1)
    first_row = group_at * SPAN
    own_segment = lax.dynamic_slice_in_dim(segment, first_row, SPAN)
    own_spots = lax.dynamic_slice_in_dim(row_spots, first_row, SPAN)
    own_begin = lax.dynamic_slice_in_dim(doc_begin, first_row, SPAN)
    allowed = (own_segment[:, None] == segment[None, :]) & (
        row_spots[None, :] <= own_spots[:, None]
    )
    inv_freqs = rope_base ** (-jnp.arange(0, HEAD_DIM, 2, dtype=f32) / HEAD_DIM)
    angles = (own_spots - own_begin).astype(f32)[:, None] * inv_freqs[None, :]
    cosine, sine = jnp.cos(angles), jnp.sin(angles)
    blank = jnp.zeros_like(sine)
    cosine = jnp.concatenate([cosine] * 4, axis=1)
    sine_up = jnp.concatenate([-sine, blank] * 2, axis=1)
    sine_down = jnp.concatenate([blank, sine] * 2, axis=1)
    return (allowed.astype(f32), cosine, sine_up, sine_down)


MESH = pl.DeviceIdType.MESH
TILES_R = OWN // 16
COLS = 15232
PART_A = (0, 7680)
PART_B = (7680, 12928)
PART_C = (12928, 15232)
DOWN_AT = 4 * 2 * WIN
QO_AT = PART_C[0]
VEC_AT = QO_AT + QKV + D
RING = 4


def halves(start, stop):
    middle = start + ((stop - start) // 128 + 1) // 2 * 128
    return ((start, middle), (middle, stop))


def ring_spot(spot, steps):
    return lax.rem(spot + steps + RING, RING)


class Links:
    def __init__(self, send_sems, recv_sems):
        self.send_sems, self.recv_sems, self.used, self.started = send_sems, recv_sems, 0, []

    def take(self, count):
        first = self.used
        self.used += count
        return first

    def copy(self, source, target, sem_at, device):
        return pltpu.make_async_remote_copy(
            src_ref=source,
            dst_ref=target,
            send_sem=self.send_sems.at[sem_at],
            recv_sem=self.recv_sems.at[sem_at],
            device_id=device,
            device_id_type=MESH,
        )

    def send(self, source, target, sem_at, device):
        copy = self.copy(source, target, sem_at, device)
        copy.start()
        self.started.append(copy)

    def arrived(self, target, sem_at, device):
        self.copy(target, target, sem_at, device).wait_recv()

    def finish(self):
        for copy in self.started:
            copy.wait_send()
        self.started = []


class RingSum:
    def __init__(self, links, spot, device_at, block, first, second, left, right, add):
        self.links, self.spot, self.block, self.add = links, spot, block, add
        self.right, self.left = device_at(ring_spot(spot, 1)), device_at(ring_spot(spot, -1))
        self.first, self.second, self.from_left, self.from_right = first, second, left, right
        self.sem = links.take(6)

    def start(self):
        send, sem, spot = self.links.send, self.sem, self.spot
        far = ring_spot(spot, 2)
        send(self.block(far, 0), self.first, sem, self.right)
        send(self.block(far, 1), self.second, sem + 1, self.left)
        send(self.block(ring_spot(spot, 1), 1), self.from_left(1), sem + 2, self.right)
        send(self.block(ring_spot(spot, -1), 0), self.from_right(0), sem + 3, self.left)

    def middle(self):
        links, sem, spot = self.links, self.sem, self.spot
        links.arrived(self.first, sem, self.right)
        onward = self.block(ring_spot(spot, 1), 0)
        self.add(onward, onward, self.first)
        links.send(onward, self.from_left(0), sem + 4, self.right)
        links.arrived(self.second, sem + 1, self.left)
        onward = self.block(ring_spot(spot, -1), 1)
        self.add(onward, onward, self.second)
        links.send(onward, self.from_right(1), sem + 5, self.left)

    def end(self, result):
        links, sem, spot = self.links, self.sem, self.spot
        links.arrived(self.from_left(1), sem + 2, self.right)
        links.arrived(self.from_right(0), sem + 3, self.left)
        links.arrived(self.from_left(0), sem + 4, self.right)
        links.arrived(self.from_right(1), sem + 5, self.left)
        for half in (0, 1):
            self.add(
                result(half), self.block(spot, half), self.from_left(half), self.from_right(half)
            )


class RingShare:
    def __init__(self, links, spot, device_at, block, sibling=None):
        self.links, self.spot, self.block, self.sibling = links, spot, block, sibling
        self.right, self.left = device_at(ring_spot(spot, 1)), device_at(ring_spot(spot, -1))
        self.sem = links.take(6)
        self.twin = links.take(8) if sibling else 0

    def pass_on(self, steps, half):
        if self.sibling:
            view = self.block(ring_spot(self.spot, steps), half)
            self.links.send(view, view, self.twin + 2 * (steps % RING) + half, self.sibling)

    def start(self):
        send, sem = self.links.send, self.sem
        low, high = self.block(self.spot, 0), self.block(self.spot, 1)
        send(low, low, sem, self.right)
        send(high, high, sem + 2, self.left)
        send(high, high, sem + 1, self.right)
        send(low, low, sem + 3, self.left)
        self.pass_on(0, 0)
        self.pass_on(0, 1)

    def middle(self):
        links, sem, spot = self.links, self.sem, self.spot
        low = self.block(ring_spot(spot, -1), 0)
        links.arrived(low, sem, self.right)
        links.send(low, low, sem + 4, self.right)
        self.pass_on(-1, 0)
        high = self.block(ring_spot(spot, 1), 1)
        links.arrived(high, sem + 2, self.left)
        links.send(high, high, sem + 5, self.left)
        self.pass_on(1, 1)

    def end(self):
        links, sem, spot = self.links, self.sem, self.spot
        for steps, half, at, device in (
            (-1, 1, 1, self.right),
            (1, 0, 3, self.left),
            (2, 0, 4, self.right),
            (2, 1, 5, self.left),
        ):
            links.arrived(self.block(ring_spot(spot, steps), half), sem + at, device)
            self.pass_on(steps, half)

    def end_twin(self, twin_block):
        for steps in range(RING):
            for half in (0, 1):
                view = twin_block(ring_spot(self.spot, steps), half)
                self.links.arrived(view, self.twin + 2 * steps + half, self.sibling)


def add_into(target, *sources):
    if len(target.shape) == 3:
        for at in range(target.shape[0]):
            add_into(target.at[at], *[source.at[at] for source in sources])
        return
    total = sources[0][...].astype(f32)
    for source in sources[1:]:
        total = total + source[...].astype(f32)
    target[...] = total.astype(target.dtype)


def greet(replica_spots, group_spots, section_spots=()):
    barrier = pltpu.get_barrier_semaphore()
    spots = {"replica": replica_spots, "group": group_spots, "section": section_spots}
    for axis, members in spots.items():
        for spot in members:
            pl.semaphore_signal(barrier, inc=1, device_id={axis: spot}, device_id_type=MESH)
    pl.semaphore_wait(barrier, sum(map(len, spots.values())))


def grads_kernel(
    n2_rows, dgu, act_rows, dmlp, left_tokens, right_tokens, vecs,
    shared, n2t, act, left_rows, right_rows, vec, part, own, zbuf, left_all, right_all, vec_all,
    a_first, a_second, a_left, a_right, a_sum, a_first2, a_second2, a_left2, a_right2,
    b_first, b_second, b_left, b_right, b_sum, b_first2, b_second2, b_left2, b_right2,
    c_first, c_second, c_left, c_right, c_sum, c_first2, c_second2, c_left2, c_right2,
    send_sems, recv_sems,
):
    group_at = lax.axis_index("group")
    replica_at = lax.axis_index("replica")
    x_at, y_at = replica_at // RING, lax.rem(replica_at, RING)
    links = Links(send_sems, recv_sems)

    def along_x(spot):
        return {"replica": spot * RING + y_at}

    def along_y(spot):
        return {"replica": x_at * RING + spot}

    peers = [ring_spot(group_at, step) for step in (1, 2, 3)]
    greet(
        [
            ring_spot(x_at, 1) * RING + y_at,
            ring_spot(x_at, -1) * RING + y_at,
            x_at * RING + ring_spot(y_at, 1),
            x_at * RING + ring_spot(y_at, -1),
        ],
        peers,
    )
    right_rows[...] = right_tokens[...].reshape(2 * SPAN, QKV + D)
    vec[...] = vecs[0] + vecs[1]
    tall = left_tokens[...].reshape(2 * SPAN, 2 * D).T
    for z in range(ZDEV):
        left_rows[z, :OWN] = tall[OWN * z : OWN * (z + 1)]
        left_rows[z, OWN:] = tall[D + OWN * z : D + OWN * (z + 1)]
    tok_sem = links.take(9)
    for step, peer in enumerate(peers):
        for at, (source, target) in enumerate(
            [
                (left_rows.at[peer], left_all.at[group_at]),
                (right_rows, right_all.at[group_at]),
                (vec, vec_all.at[group_at]),
            ]
        ):
            links.send(source, target, tok_sem + 3 * step + at, {"group": peer})
    left_all[group_at] = left_rows[group_at]
    right_all[group_at] = right_rows[...]
    vec_all[group_at] = vec[...]

    n2t[...] = n2_rows[...].T
    act[...] = act_rows[...].T

    def gate_up(tile, carry):
        at = pl.multiple_of(tile * 256, 256)
        block = jnp.dot(n2t[...], dgu[:, pl.ds(at, 256)], preferred_element_type=f32).astype(bf16)
        block = block.reshape(ZDEV, TILES_R, 16, 256)
        for z in range(ZDEV):
            where = pl.multiple_of(tile * 256 + z * 2 * WIN, 128)
            for r in range(TILES_R):
                part[r // RING, r % RING, :, pl.ds(where, 256)] = block[z, r]
        return carry

    lax.fori_loop(0, 2 * WIN // 256, gate_up, 0)
    shift = lax.rem(group_at, 2) * 64
    for quarter in range(4):
        rows = pl.ds(pl.multiple_of(shift + 304 * quarter, 16), 304)
        block = jnp.dot(act[rows, :], dmlp[...], preferred_element_type=f32).astype(bf16)
        block = block.reshape(19, 16, D)
        for inner in range(19):
            tile = 19 * quarter + inner
            if tile < 3 * TILES_R:
                r, at = tile // 3, DOWN_AT + D * (tile % 3)
            else:
                r, at = TILES_R + (tile - 3 * TILES_R) // 17, D * ((tile - 3 * TILES_R) % 17)
            part[r // RING, r % RING, :, at : at + D] = block[inner]

    def summers(cols, x_first, bufs):
        first, second, left, right, total, first2, second2, left2, right2 = bufs
        start, stop = cols

        def big(spot, half):
            span = pl.ds(2 * half, 2)
            if x_first:
                return part.at[spot, span, :, start:stop]
            return part.at[span, spot, :, start:stop]

        cuts = halves(0, stop - start)

        def small(spot, half):
            return total.at[spot, :, cuts[half][0] : cuts[half][1]]

        def pair(buf):
            return lambda half: buf.at[pl.ds(2 * half, 2)]

        def cut(buf):
            return lambda half: buf.at[:, cuts[half][0] : cuts[half][1]]

        one = (x_at, along_x) if x_first else (y_at, along_y)
        two = (y_at, along_y) if x_first else (x_at, along_x)
        stage_one = RingSum(
            links, *one, big, first, second, pair(left), pair(right), add_into
        )
        stage_two = RingSum(
            links, *two, small, first2, second2, cut(left2), cut(right2), add_into
        )

        def result(half):
            return own.at[:, start + cuts[half][0] : start + cuts[half][1]]

        return stage_one, stage_two, pair(total), result

    a_one, a_two, a_mid, a_result = summers(
        PART_A, True,
        (a_first, a_second, a_left, a_right, a_sum, a_first2, a_second2, a_left2, a_right2),
    )
    b_one, b_two, b_mid, b_result = summers(
        PART_B, False,
        (b_first, b_second, b_left, b_right, b_sum, b_first2, b_second2, b_left2, b_right2),
    )
    c_one, c_two, c_mid, c_result = summers(
        PART_C, False,
        (c_first, c_second, c_left, c_right, c_sum, c_first2, c_second2, c_left2, c_right2),
    )
    a_one.start()
    b_one.start()
    a_one.middle()
    b_one.middle()
    for step, peer in enumerate(peers):
        source = ring_spot(group_at, -1 - step)
        for at, target in enumerate((left_all, right_all, vec_all)):
            links.arrived(target.at[source], tok_sem + 3 * step + at, {"group": peer})
    for width, col, row in ((QKV, 0, 0), (D, QKV, OWN)):
        total = jnp.dot(
            left_all[0, row : row + OWN], right_all[0, :, col : col + width],
            preferred_element_type=f32,
        )
        for z in range(1, ZDEV):
            total = total + jnp.dot(
                left_all[z, row : row + OWN], right_all[z, :, col : col + width],
                preferred_element_type=f32,
            )
        total = total.astype(bf16).reshape(TILES_R, 16, width)
        for r in range(TILES_R):
            part[r // RING, r % RING, :, QO_AT + col : QO_AT + col + width] = total[r]
    part[0, 0, :, VEC_AT:COLS] = (
        vec_all[0] + vec_all[1] + vec_all[2] + vec_all[3]
    ).astype(bf16)
    for r in range(1, TILES_R):
        part[r // RING, r % RING, :, VEC_AT:COLS] = jnp.zeros((16, COLS - VEC_AT), bf16)
    c_one.start()
    a_one.end(a_mid)
    a_two.start()
    b_one.end(b_mid)
    b_two.start()
    c_one.middle()
    a_two.middle()
    b_two.middle()
    c_one.end(c_mid)
    c_two.start()
    a_two.end(a_result)
    b_two.end(b_result)
    slot_sem = links.take(3)
    for step, peer in enumerate(peers):
        where = pl.multiple_of(peer * 2 * WIN, 128)
        links.send(
            own.at[:, pl.ds(where, 2 * WIN)], zbuf.at[group_at], slot_sem + step, {"group": peer}
        )
    where = pl.multiple_of(group_at * 2 * WIN, 128)
    zbuf[group_at] = own[:, pl.ds(where, 2 * WIN)]
    c_two.middle()
    c_two.end(c_result)
    for step, peer in enumerate(peers):
        links.arrived(zbuf.at[ring_spot(group_at, -1 - step)], slot_sem + step, {"group": peer})

    @pl.when(replica_at < TILES_R)
    def _():
        for which in (0, 1):
            base, at = which * FF, which * WIN
            for z in range(ZDEV):
                low = 128 if z % 2 else 0
                high = WIN if z % 2 else WIN - 128
                to = base + STARTS[z]
                shared[x_at, y_at, :, to + low : to + high] = zbuf[z, :, at + low : at + high]
            for z in (0, 2):
                to = base + STARTS[z + 1]
                shared[x_at, y_at, :, to : to + 128] = (
                    zbuf[z, :, at + WIN - 128 : at + WIN] + zbuf[z + 1, :, at : at + 128]
                )
        shared[x_at, y_at, :, 2 * FF : 2 * FF + 512] = jnp.zeros((16, 512), bf16)
        shared[x_at, y_at, :, DOWN_AT:COLS] = own[:, DOWN_AT:COLS]

    @pl.when(replica_at >= TILES_R)
    def _():
        shared[x_at, y_at] = own[...]

    def sharers(cols, x_first):
        start, stop = cols
        cuts = halves(start, stop)

        def small(spot, half):
            low, high = cuts[half]
            if x_first:
                return shared.at[spot, y_at, :, low:high]
            return shared.at[x_at, spot, :, low:high]

        def big(spot, half):
            span = pl.ds(2 * half, 2)
            if x_first:
                return shared.at[span, spot, :, start:stop]
            return shared.at[spot, span, :, start:stop]

        one = (x_at, along_x) if x_first else (y_at, along_y)
        two = (y_at, along_y) if x_first else (x_at, along_x)
        return RingShare(links, *one, small), RingShare(links, *two, big)

    a_one, a_two = sharers((0, 7680), False)
    b_one, b_two = sharers((7680, COLS), True)
    a_one.start()
    b_one.start()
    a_one.middle()
    b_one.middle()
    a_one.end()
    a_two.start()
    b_one.end()
    b_two.start()
    a_two.middle()
    b_two.middle()
    a_two.end()
    b_two.end()
    links.finish()


def share_grads(n2, dgu, act, dmlp, lefts, rights, vecs):
    def bufs(cols):
        width = cols[1] - cols[0]
        low, high = [b - a for a, b in halves(0, width)]
        shapes = [(2, 16, width), (2, 16, width), (4, 16, width), (4, 16, width), (4, 16, width)]
        shapes = shapes + [(16, low), (16, high), (16, width), (16, width)]
        return [pltpu.VMEM(shape, bf16) for shape in shapes]

    vmem = pl.BlockSpec(memory_space=pltpu.VMEM)
    sems = 9 + 3 + 6 * 6 + 4 * 6
    return pl.pallas_call(
        grads_kernel,
        out_shape=jax.ShapeDtypeStruct((RING, RING, 16, COLS), bf16),
        in_specs=[vmem] * 7,
        out_specs=vmem,
        scratch_shapes=[
            pltpu.VMEM((D, 2 * ROW), bf16),
            pltpu.VMEM((WIN, 2 * ROW), bf16),
            pltpu.VMEM((ZDEV, 2 * OWN, 2 * SPAN), bf16),
            pltpu.VMEM((2 * SPAN, QKV + D), bf16),
            pltpu.VMEM((16, 256), f32),
            pltpu.VMEM((RING, RING, 16, COLS), bf16),
            pltpu.VMEM((16, COLS), bf16),
            pltpu.VMEM((ZDEV, 16, 2 * WIN), bf16),
            pltpu.VMEM((ZDEV, 2 * OWN, 2 * SPAN), bf16),
            pltpu.VMEM((ZDEV, 2 * SPAN, QKV + D), bf16),
            pltpu.VMEM((ZDEV, 16, 256), f32),
            *bufs(PART_A),
            *bufs(PART_B),
            *bufs(PART_C),
            pltpu.SemaphoreType.DMA((sems,)),
            pltpu.SemaphoreType.DMA((sems,)),
        ],
        compiler_params=pltpu.CompilerParams(
            collective_id=1, has_side_effects=True, vmem_limit_bytes=58 * 1024 * 1024
        ),
        name="grads",
    )(n2, dgu, act, dmlp, lefts, rights, vecs)


def weight_grads(n2, dgu, act, dmlp, lefts, rights, vecs):
    group_at = lax.axis_index("group")
    shared = share_grads(
        n2.reshape(2 * ROW, D),
        dgu.reshape(2 * ROW, 2 * WIN),
        act.reshape(2 * ROW, WIN),
        dmlp.reshape(2 * ROW, D),
        lefts,
        rights,
        vecs,
    )
    shared = shared.reshape(REPL, 16, COLS)

    def rows_of(start, width):
        block = shared[:TILES_R, :, start : start + width]
        return block.reshape(OWN, width).astype(f32)

    lead = shared[:TILES_R, :, DOWN_AT : DOWN_AT + 3 * D].reshape(TILES_R, 16, 3, D)
    rest = shared[TILES_R:].reshape(2, 16, 17, D)
    grad_down = jnp.concatenate(
        [
            jnp.transpose(lead, (0, 2, 1, 3)).reshape(-1, D),
            jnp.transpose(rest, (0, 2, 1, 3)).reshape(-1, D),
        ]
    ).astype(f32)
    vec = shared[0, :, VEC_AT:].reshape(16 * 256).astype(f32)

    def own_part(start, width):
        return lax.dynamic_slice_in_dim(vec, start + group_at * width, width, 0)

    return (
        rows_of(QO_AT, QKV),
        own_part(0, QKV // ZDEV),
        rows_of(QO_AT + QKV, D),
        rows_of(0, FF),
        rows_of(FF, FF),
        grad_down,
        own_part(QKV, OWN),
        own_part(QKV + D, OWN),
    )


PAIRS = HEADS // 2
KINDS = (((0, 1, 2, 3), 0), ((0, 1, 2), 1), ((4, 5, 6), 2), ((3, 4, 5, 6), 3))
SCALE = HEAD_DIM ** (-0.5)
TILE = 256


def dot_nt(left, right):
    return lax.dot_general(left, right, (((1,), (1,)), ((), ())), preferred_element_type=f32)


def dot_tn(left, right):
    return lax.dot_general(left, right, (((0,), (0,)), ((), ())), preferred_element_type=f32)


def spread(pair):
    low = lax.broadcasted_iota(jnp.int32, pair.shape, 1) < HEAD_DIM
    wide = pair.astype(f32)
    turned = pltpu.roll(wide, HEAD_DIM, 1)
    zero = jnp.zeros_like(wide)
    members = (
        jnp.where(low, wide, zero),
        jnp.where(low, zero, turned),
        jnp.where(low, turned, zero),
        jnp.where(low, zero, wide),
    )
    return [member.astype(bf16) for member in members]


def unspread(kinds):
    low = lax.broadcasted_iota(jnp.int32, kinds[0].shape, 1) < HEAD_DIM
    straight = jnp.where(low, kinds[0], kinds[3])
    crossed = jnp.where(low, kinds[2], kinds[1])
    return straight + pltpu.roll(crossed, HEAD_DIM, 1)


def stack_pairs(tokens, kind):
    return jnp.concatenate(
        [tokens[:, 2 * HEAD_DIM * p : 2 * HEAD_DIM * (p + 1)] for p in KINDS[kind][0]], axis=0
    )


def join_pairs(kinds):
    found = [None] * PAIRS
    for kind, (pairs, _) in enumerate(KINDS):
        for at, p in enumerate(pairs):
            part = kinds[kind][SPAN * at : SPAN * (at + 1)]
            found[p] = part if found[p] is None else found[p] + part
    return jnp.concatenate(found, axis=1)


def turn(values, cosine, sine_up, sine_down, sign):
    tiles = []
    for at in range(values.shape[1] // 128):
        tile = values[:, 128 * at : 128 * (at + 1)]
        up = pltpu.roll(tile, 128 - HEAD_DIM // 2, 1)
        down = pltpu.roll(tile, HEAD_DIM // 2, 1)
        tiles.append(tile * cosine + sign * (up * sine_up + down * sine_down))
    return jnp.concatenate(tiles, axis=1)


def layers_kernel(
    tokens, cotangent, mask, cosine, sine_up, sine_down, vectors, joint_hbm, wide_hbm, down_hbm,
    acts, grads_in, out_n2, out_dgu, out_act, out_dmlp, out_left, out_right, out_vec,
    joint, wide, down, xs, n1s, qs, kvs, probs, ctx, hid, n2s, gus, act, ysend, yrecv,
    dys, dmlp, dgu, dn2, dsend, drecv, dkvsend, dkvrecv, lefts, rights, vecs, igs,
    send_sems, recv_sems, load_sems, away_send, away_recv, stay_sems,
):
    section_at = lax.axis_index("section")
    group_at = lax.axis_index("group")
    other = 1 - section_at
    peers = [ring_spot(group_at, step) for step in (1, 2, 3)]
    greet([], peers, [other])

    def load(layer, which):
        source, target = [
            (joint_hbm.at[layer], joint.at[layer]),
            (wide_hbm.at[layer, :, pl.ds(0, TILES_R)], wide.at[layer]),
            (down_hbm.at[layer], down.at[layer]),
        ][which]
        return pltpu.make_async_copy(source, target, load_sems.at[layer, which])

    for layer in (0, 1):
        for which in range(3):
            load(layer, which).start()

    def exchange(layer, which, source, target):
        copies = []
        for step, peer in enumerate(peers):
            copy = pltpu.make_async_remote_copy(
                src_ref=source(peer),
                dst_ref=target(group_at),
                send_sem=send_sems.at[layer, which, step],
                recv_sem=recv_sems.at[layer, which, step],
                device_id={"group": peer},
                device_id_type=MESH,
            )
            copy.start()
            copies.append(copy)

        def finish():
            for step, peer in enumerate(peers):
                landed = target(ring_spot(group_at, -1 - step))
                pltpu.make_async_remote_copy(
                    src_ref=landed,
                    dst_ref=landed,
                    send_sem=send_sems.at[layer, which, step],
                    recv_sem=recv_sems.at[layer, which, step],
                    device_id={"group": peer},
                    device_id_type=MESH,
                ).wait_recv()
            for copy in copies:
                copy.wait_send()

        return finish

    def wide_cols(layer, start):
        block = wide[layer, :, :, :, pl.ds(pl.multiple_of(start, 128), TILE)]
        return block.reshape(D, TILE)

    def gathered_sum(own, got):
        total = own[group_at].astype(f32)
        for step in (1, 2, 3):
            total = total + got[ring_spot(group_at, step)].astype(f32)
        return total

    def allowed(count):
        return jnp.concatenate([mask[...]] * count, axis=0) > 0.0

    xs[0] = tokens[section_at]
    bias_at, gain_at, gain_two_at = (0, QKV), (QKV, QKV + D), (QKV + D, QKV + 2 * D)

    def forward(layer, carry):
        x = xs[layer].astype(f32)
        gain_one = vectors[layer, :, gain_at[0] : gain_at[1]]
        gain_two = vectors[layer, :, gain_two_at[0] : gain_two_at[1]]
        n1 = (x * rms_scale(x) * gain_one).astype(bf16)
        n1s[layer] = n1
        load(layer, 0).wait()
        qkv = jnp.dot(n1, joint[layer, :, :QKV], preferred_element_type=f32)
        qkv = qkv + vectors[layer, :, bias_at[0] : bias_at[1]]
        turned = turn(
            qkv[:, : D + KV_WIDTH], cosine[...], sine_up[...], sine_down[...], 1.0
        ).astype(bf16)
        qs[layer] = turned[:, :D]
        kvs[layer, group_at] = jnp.concatenate(
            [turned[:, D:], qkv[:, D + KV_WIDTH :].astype(bf16)], axis=1
        )
        exchange(
            layer, 0, lambda peer: kvs.at[layer, group_at], lambda spot: kvs.at[layer, spot]
        )()
        kv = kvs[layer].reshape(ROW, 2 * KV_WIDTH)
        keys, values = spread(kv[:, :KV_WIDTH]), spread(kv[:, KV_WIDTH:])
        outs, row = [], 0
        for kind, (pairs, _) in enumerate(KINDS):
            count = SPAN * len(pairs)
            scores = dot_nt(stack_pairs(turned, kind), keys[kind]) * SCALE
            scores = jnp.where(allowed(len(pairs)), scores, -jnp.inf)
            top = jnp.max(scores, axis=-1, keepdims=True)
            raised = jnp.exp(scores - top)
            prob = raised * (1.0 / jnp.sum(raised, axis=-1, keepdims=True))
            probs[layer, row : row + count] = prob
            outs.append(jnp.dot(prob.astype(bf16), values[kind], preferred_element_type=f32))
            row += count
        context = join_pairs(outs).astype(bf16)
        ctx[layer] = context
        hidden = x + jnp.dot(context, joint[layer, :, QKV:], preferred_element_type=f32)
        hid[layer] = hidden
        n2s[layer, group_at] = (hidden * rms_scale(hidden) * gain_two).astype(bf16)
        done = exchange(
            layer, 1, lambda peer: n2s.at[layer, group_at], lambda spot: n2s.at[layer, spot]
        )
        load(layer, 1).wait()
        done()

        def columns(tile, carry):
            at = tile * TILE
            n2 = n2s[layer].reshape(ROW, D)
            gate = jnp.dot(n2, wide_cols(layer, at), preferred_element_type=f32)
            up = jnp.dot(n2, wide_cols(layer, at + WIN), preferred_element_type=f32)
            gus[layer, 0, :, pl.ds(pl.multiple_of(at, TILE), TILE)] = gate
            gus[layer, 1, :, pl.ds(pl.multiple_of(at, TILE), TILE)] = up
            act[layer, :, pl.ds(pl.multiple_of(at, TILE), TILE)] = (
                gate * jax.nn.sigmoid(gate) * up
            ).astype(bf16)
            return carry

        lax.fori_loop(0, WIN // TILE, columns, 0)
        load(layer, 2).wait()
        partial = jnp.dot(act[layer], down[layer], preferred_element_type=f32)
        ysend[layer] = partial.astype(bf16).reshape(ZDEV, SPAN, D)
        exchange(
            layer, 2, lambda peer: ysend.at[layer, peer], lambda spot: yrecv.at[layer, spot]
        )()
        mlp = gathered_sum(ysend.at[layer], yrecv.at[layer])
        xs[layer + 1] = (hidden + mlp).astype(bf16)
        return carry

    lax.fori_loop(0, 2, forward, 0)
    dys[...] = cotangent[section_at].astype(f32)

    def hand_over(layer):
        return [
            (xs.at[layer + 1], acts),
            (igs.at[layer], grads_in),
            (n2s.at[layer], out_n2),
            (dgu.at[layer], out_dgu),
            (act.at[layer], out_act),
            (dmlp.at[layer], out_dmlp),
            (lefts.at[layer], out_left),
            (rights.at[layer], out_right),
            (vecs.at[layer], out_vec),
        ]

    def staying(layer):
        return [
            pltpu.make_async_copy(source, target.at[section_at], stay_sems.at[at])
            for at, (source, target) in enumerate(hand_over(layer))
        ]

    def leaving(layer, slot):
        return [
            pltpu.make_async_remote_copy(
                src_ref=source,
                dst_ref=target.at[slot],
                send_sem=away_send.at[at],
                recv_sem=away_recv.at[at],
                device_id={"section": other},
                device_id_type=MESH,
            )
            for at, (source, target) in enumerate(hand_over(layer))
        ]

    def backward(turn_at, carry):
        layer = 1 - turn_at
        gain_one = vectors[layer, :, gain_at[0] : gain_at[1]]
        gain_two = vectors[layer, :, gain_two_at[0] : gain_two_at[1]]
        dy = dys[...]
        dmlp[layer, group_at] = dy.astype(bf16)
        exchange(
            layer, 3, lambda peer: dmlp.at[layer, group_at], lambda spot: dmlp.at[layer, spot]
        )()
        dn2[...] = jnp.zeros_like(dn2)

        def columns(tile, carry):
            at = pl.multiple_of(tile * TILE, TILE)
            grad = dot_nt(dmlp[layer].reshape(ROW, D), down[layer, pl.ds(at, TILE), :])
            gate = gus[layer, 0, :, pl.ds(at, TILE)]
            up = gus[layer, 1, :, pl.ds(at, TILE)]
            sigma = jax.nn.sigmoid(gate)
            grad_gate = (grad * up * sigma * (1.0 + gate * (1.0 - sigma))).astype(bf16)
            grad_up = (grad * gate * sigma).astype(bf16)
            dgu[layer, :, pl.ds(at, TILE)] = grad_gate
            dgu[layer, :, pl.ds(pl.multiple_of(at + WIN, TILE), TILE)] = grad_up
            dn2[...] += dot_nt(grad_gate, wide_cols(layer, at)) + dot_nt(
                grad_up, wide_cols(layer, at + WIN)
            )
            return carry

        lax.fori_loop(0, WIN // TILE, columns, 0)
        dsend[layer] = dn2[...].astype(bf16).reshape(ZDEV, SPAN, D)
        exchange(
            layer, 4, lambda peer: dsend.at[layer, peer], lambda spot: drecv.at[layer, spot]
        )()
        grad_two = gathered_sum(dsend.at[layer], drecv.at[layer])
        hidden = hid[layer]
        scale = rms_scale(hidden)
        scaled = grad_two * gain_two
        inner = jnp.mean(scaled * hidden, axis=-1, keepdims=True)
        dhid = dy + scale * (scaled - hidden * (scale * scale * inner))
        gain_two_term = jnp.sum(grad_two * hidden * scale, axis=0, keepdims=True)
        dt = dhid.astype(bf16)
        rights[layer, :, QKV:] = dt
        do = dot_nt(dt, joint[layer, :, QKV:]).astype(bf16)
        kv = kvs[layer].reshape(ROW, 2 * KV_WIDTH)
        keys, values = spread(kv[:, :KV_WIDTH]), spread(kv[:, KV_WIDTH:])
        queries = qs[layer]
        dqs, dks, dvs, row = [], [], [], 0
        for kind, (pairs, _) in enumerate(KINDS):
            count = SPAN * len(pairs)
            prob = probs[layer, row : row + count]
            grad = stack_pairs(do, kind)
            dprob = dot_nt(grad, values[kind])
            inner = jnp.sum(prob * dprob, axis=-1, keepdims=True)
            dscore = (prob * (dprob - inner)).astype(bf16)
            dqs.append(jnp.dot(dscore, keys[kind], preferred_element_type=f32))
            dks.append(dot_tn(dscore, stack_pairs(queries, kind)))
            dvs.append(dot_tn(prob.astype(bf16), grad))
            row += count
        dkv = jnp.concatenate([unspread(dks) * SCALE, unspread(dvs)], axis=1)
        dkvsend[layer] = dkv.astype(bf16).reshape(ZDEV, SPAN, 2 * KV_WIDTH)
        exchange(
            layer, 5, lambda peer: dkvsend.at[layer, peer], lambda spot: dkvrecv.at[layer, spot]
        )()
        dkv = gathered_sum(dkvsend.at[layer], dkvrecv.at[layer])
        dqk = jnp.concatenate([join_pairs(dqs) * SCALE, dkv[:, :KV_WIDTH]], axis=1)
        dqk = turn(dqk, cosine[...], sine_up[...], sine_down[...], -1.0)
        dqkv = jnp.concatenate([dqk, dkv[:, KV_WIDTH:]], axis=1).astype(bf16)
        rights[layer, :, :QKV] = dqkv
        lefts[layer, :, :D] = n1s[layer]
        lefts[layer, :, D:] = ctx[layer]
        bias_term = jnp.sum(dqkv.astype(f32), axis=0, keepdims=True)
        grad_one = dot_nt(dqkv, joint[layer, :, :QKV])
        x = xs[layer].astype(f32)
        scale = rms_scale(x)
        scaled = grad_one * gain_one
        inner = jnp.mean(scaled * x, axis=-1, keepdims=True)
        dx = dhid + scale * (scaled - x * (scale * scale * inner))
        gain_one_term = jnp.sum(grad_one * x * scale, axis=0, keepdims=True)
        rounded = dx.astype(bf16).astype(f32)
        dys[...] = rounded
        igs[layer] = jnp.where(layer == 1, rounded, dx)
        terms = jnp.concatenate(
            [bias_term, gain_one_term, gain_two_term, jnp.zeros((1, 128), f32)], axis=1
        )
        for at in range(12):
            vecs[layer, at : at + 1, :] = terms[:, 256 * at : 256 * (at + 1)]
        vecs[layer, 12:16, :] = jnp.zeros((4, 256), f32)

        @pl.when(layer == section_at)
        def _():
            for copy in staying(layer):
                copy.start()

        @pl.when(layer != section_at)
        def _():
            for copy in leaving(layer, section_at):
                copy.start()

        return carry

    lax.fori_loop(0, 2, backward, 0)
    for copy in staying(section_at):
        copy.wait()
    for copy in leaving(other, section_at):
        copy.wait_send()
    for copy in leaving(other, other):
        copy.wait_recv()


def run_layers(tokens, cotangent, mask, cosine, sine_up, sine_down, vectors, joint, wide, down):
    vmem = pl.BlockSpec(memory_space=pltpu.VMEM)
    anywhere = pl.BlockSpec(memory_space=pl.ANY)

    def per_micro(shape, kind):
        return jax.ShapeDtypeStruct((2,) + shape, kind)

    def scratch(shape, kind=bf16, lead=2):
        return pltpu.VMEM((lead,) + shape, kind)

    return pl.pallas_call(
        layers_kernel,
        out_shape=(
            per_micro((SPAN, D), bf16),
            per_micro((SPAN, D), f32),
            per_micro((ZDEV, SPAN, D), bf16),
            per_micro((ROW, 2 * WIN), bf16),
            per_micro((ROW, WIN), bf16),
            per_micro((ZDEV, SPAN, D), bf16),
            per_micro((SPAN, 2 * D), bf16),
            per_micro((SPAN, QKV + D), bf16),
            per_micro((16, 256), f32),
        ),
        in_specs=[vmem] * 7 + [anywhere] * 3,
        out_specs=[vmem] * 9,
        scratch_shapes=[
            scratch((D, QKV + D)),
            scratch((ZDEV, TILES_R, 16, 2 * WIN)),
            scratch((WIN, D)),
            scratch((SPAN, D), lead=3),
            scratch((SPAN, D)),
            scratch((SPAN, D)),
            scratch((ZDEV, SPAN, 2 * KV_WIDTH)),
            scratch((HEADS * SPAN, ROW), f32),
            scratch((SPAN, D)),
            scratch((SPAN, D), f32),
            scratch((ZDEV, SPAN, D)),
            scratch((2, ROW, WIN), f32),
            scratch((ROW, WIN)),
            scratch((ZDEV, SPAN, D)),
            scratch((ZDEV, SPAN, D)),
            pltpu.VMEM((SPAN, D), f32),
            scratch((ZDEV, SPAN, D)),
            scratch((ROW, 2 * WIN)),
            pltpu.VMEM((ROW, D), f32),
            scratch((ZDEV, SPAN, D)),
            scratch((ZDEV, SPAN, D)),
            scratch((ZDEV, SPAN, 2 * KV_WIDTH)),
            scratch((ZDEV, SPAN, 2 * KV_WIDTH)),
            scratch((SPAN, 2 * D)),
            scratch((SPAN, QKV + D)),
            scratch((16, 256), f32),
            scratch((SPAN, D), f32),
            pltpu.SemaphoreType.DMA((2, 6, 3)),
            pltpu.SemaphoreType.DMA((2, 6, 3)),
            pltpu.SemaphoreType.DMA((2, 3)),
            pltpu.SemaphoreType.DMA((9,)),
            pltpu.SemaphoreType.DMA((9,)),
            pltpu.SemaphoreType.DMA((9,)),
        ],
        compiler_params=pltpu.CompilerParams(
            collective_id=3, has_side_effects=True, vmem_limit_bytes=60 * 1024 * 1024
        ),
        name="layers",
    )(tokens, cotangent, mask, cosine, sine_up, sine_down, vectors, joint, wide, down)


def weights_kernel(
    w_qkv, w_out, w_gate, w_up, w_down, vec,
    joint, wide, down, vectors,
    zeros, send_sems, recv_sems, local_sems,
):
    section_at = lax.axis_index("section")
    group_at = lax.axis_index("group")
    replica_at = lax.axis_index("replica")
    x_at, y_at = replica_at // RING, lax.rem(replica_at, RING)
    links = Links(send_sems, recv_sems)
    sibling = {"section": 1 - section_at}

    def along_x(spot):
        return {"replica": spot * RING + y_at}

    def along_y(spot):
        return {"replica": x_at * RING + spot}

    def along_z(spot):
        return {"group": spot}

    zeros[...] = jnp.zeros_like(zeros)
    peers = [ring_spot(group_at, step) for step in (1, 2, 3)]
    greet(
        [
            ring_spot(x_at, 1) * RING + y_at,
            ring_spot(x_at, -1) * RING + y_at,
            x_at * RING + ring_spot(y_at, 1),
            x_at * RING + ring_spot(y_at, -1),
        ],
        peers,
        [1 - section_at],
    )
    row_tile = pl.ds(pl.multiple_of(jnp.minimum(replica_at, TILES_R - 1) * 16, 16), 16)
    slots = []
    for which, source in enumerate((w_gate, w_up)):
        target = wide.at[section_at, group_at, x_at, y_at, :, WIN * which : WIN * (which + 1)]
        slots.append((source, target))

    def window(source, spot):
        start = pl.multiple_of((19 * spot) // 2 * 128, 128)
        return source.at[row_tile, pl.ds(start, WIN)]

    slot_sem = links.take(6)
    for step, peer in enumerate(peers):
        for which, (source, target) in enumerate(slots):
            links.send(window(source, peer), target, slot_sem + 2 * step + which, along_z(peer))
    vec_sem = links.take(4)
    for step, peer in enumerate(peers):
        links.send(vec, vectors.at[section_at, group_at], vec_sem + step, along_z(peer))
    shift = lax.rem(group_at, 2) * 64
    body = pl.ds(pl.multiple_of(shift, 64), BLOCK)
    gap = pl.ds(pl.multiple_of(BLOCK - 19 * shift, 64), 64)
    locals_ = []
    for source, target in [
        *[(window(source, group_at), target) for source, target in slots],
        (w_qkv, joint.at[section_at, group_at, :, 0:QKV]),
        (w_out, joint.at[section_at, group_at, :, QKV : QKV + D]),
        (w_down, down.at[section_at, body]),
        (zeros, down.at[0, gap]),
        (zeros, down.at[1, gap]),
        (vec, vectors.at[section_at, group_at]),
    ]:
        copy = pltpu.make_async_copy(source, target, local_sems.at[len(locals_)])
        copy.start()
        locals_.append(copy)
    for at in (2, 3):
        locals_[at].wait()

    def joint_block(spot, half):
        return joint.at[section_at, spot, pl.ds(112 * half, 112)]

    joint_share = RingShare(links, group_at, along_z, joint_block, sibling)
    joint_share.start()
    down_sem = links.take(1)
    down_view = down.at[section_at, body]
    links.send(w_down, down_view, down_sem, sibling)
    locals_[0].wait()
    locals_[1].wait()

    def arrived_slots(which):
        for step, peer in enumerate(peers):
            spot = ring_spot(group_at, -1 - step)
            cols = pl.ds(WIN * which, WIN)
            target = wide.at[section_at, spot, x_at, y_at, :, cols]
            links.arrived(target, slot_sem + 2 * step + which, along_z(peer))

    def sharers(which, x_first):
        start = WIN * which

        def small(spot, half):
            cols = pl.ds(start + WIN // 2 * half, WIN // 2)
            if x_first:
                return wide.at[section_at, :, spot, y_at, :, cols]
            return wide.at[section_at, :, x_at, spot, :, cols]

        def big(spot, half):
            span, cols = pl.ds(2 * half, 2), pl.ds(start, WIN)
            if x_first:
                return wide.at[section_at, :, span, spot, :, cols]
            return wide.at[section_at, :, spot, span, :, cols]

        one = (x_at, along_x) if x_first else (y_at, along_y)
        two = (y_at, along_y) if x_first else (x_at, along_x)
        return RingShare(links, *one, small), RingShare(links, *two, big, sibling)

    gate_one, gate_two = sharers(0, False)
    up_one, up_two = sharers(1, True)
    arrived_slots(0)
    gate_one.start()
    arrived_slots(1)
    up_one.start()
    gate_one.middle()
    up_one.middle()
    gate_one.end()
    gate_two.start()
    up_one.end()
    up_two.start()
    joint_share.middle()
    for step, peer in enumerate(peers):
        spot = ring_spot(group_at, -1 - step)
        links.arrived(vectors.at[section_at, spot], vec_sem + step, along_z(peer))
    locals_[7].wait()
    links.send(vectors.at[section_at], vectors.at[section_at], vec_sem + 3, sibling)
    gate_two.middle()
    up_two.middle()
    joint_share.end()
    gate_two.end()
    up_two.end()
    other = 1 - section_at
    for at in (4, 5, 6):
        locals_[at].wait()
    links.arrived(down.at[other, body], down_sem, sibling)
    links.arrived(vectors.at[other], vec_sem + 3, sibling)
    joint_share.end_twin(lambda spot, half: joint.at[other, spot, pl.ds(112 * half, 112)])
    for which, share in ((0, gate_two), (1, up_two)):
        cols = pl.ds(WIN * which, WIN)
        if which:
            share.end_twin(lambda s, h: wide.at[other, :, pl.ds(2 * h, 2), s, :, cols])
        else:
            share.end_twin(lambda s, h: wide.at[other, :, s, pl.ds(2 * h, 2), :, cols])
    links.finish()


def share_weights(w_qkv, w_out, w_gate, w_up, w_down, vec):
    anywhere = pl.BlockSpec(memory_space=pl.ANY)
    sems = 6 + 4 + 1 + 3 * 14 + 2 * 6
    return pl.pallas_call(
        weights_kernel,
        out_shape=(
            jax.ShapeDtypeStruct((2, ZDEV, OWN, QKV + D), bf16),
            jax.ShapeDtypeStruct((2, ZDEV, RING, RING, 16, 2 * WIN), bf16),
            jax.ShapeDtypeStruct((2, WIN, D), bf16),
            jax.ShapeDtypeStruct((2, ZDEV, 8, 128), f32),
        ),
        in_specs=[anywhere] * 6,
        out_specs=[pl.BlockSpec(memory_space=pltpu.VMEM)] * 4,
        scratch_shapes=[
            pltpu.VMEM((64, D), bf16),
            pltpu.SemaphoreType.DMA((sems,)),
            pltpu.SemaphoreType.DMA((sems,)),
            pltpu.SemaphoreType.DMA((8,)),
        ],
        compiler_params=pltpu.CompilerParams(
            collective_id=2, has_side_effects=True, vmem_limit_bytes=58 * 1024 * 1024
        ),
        name="weights",
    )(w_qkv, w_out, w_gate, w_up, w_down, vec)


def on_device(
    tokens, cotangent, doc_lengths, w_qkv, b_qkv, w_out, w_gate, w_up, w_down, norm_attn, norm_ffn
):
    section_at = lax.axis_index("section")
    group_at = lax.axis_index("group")
    vec = jnp.concatenate([b_qkv[0], norm_attn[0], norm_ffn[0]]).astype(f32)
    vec = jnp.pad(vec, (0, 1024 - vec.shape[0])).reshape(8, 128)
    joint, wide, down, vectors = share_weights(
        w_qkv[0], w_out[0], w_gate[0], w_up[0], w_down[0], vec
    )
    vectors = vectors.reshape(2, ZDEV, 1024)
    parts = (vectors[..., : QKV // 4], vectors[..., QKV // 4 : QKV // 4 + OWN])
    parts = parts + (vectors[..., QKV // 4 + OWN : QKV // 4 + 2 * OWN],)
    vectors = jnp.concatenate([part.reshape(2, 1, -1) for part in parts], axis=2)
    lengths = lax.dynamic_index_in_dim(doc_lengths, section_at, 0, keepdims=False)[0]
    acts, input_grads, *pieces = run_layers(
        tokens[:, 0],
        cotangent[:, 0],
        *doc_tables(lengths, group_at),
        vectors,
        joint.reshape(2, D, QKV + D),
        wide.reshape(2, ZDEV, REPL, 16, 2 * WIN),
        down,
    )
    grads = weight_grads(*pieces)
    return (acts[None, :, None], input_grads[None, :, None]) + tuple(g[None] for g in grads)


def solution(mesh):
    rows = P("section", "group", None)
    vector = P("section", "group")
    spans = P("section", None, "replica", "group", None)
    return jax.shard_map(
        on_device,
        mesh=mesh,
        in_specs=(
            P(None, "replica", "group", None),
            P(None, "replica", "group", None),
            P(None, "replica", None),
            rows,
            vector,
            rows,
            rows,
            rows,
            rows,
            vector,
            vector,
        ),
        out_specs=(spans, spans, rows, vector, rows, rows, rows, rows, vector, vector),
        check_vma=False,
    )
```

```python
import jax
import jax.numpy as jnp
from jax import lax
from jax.experimental import pallas as pl
from jax.experimental.pallas import tpu as pltpu
from jax.sharding import PartitionSpec as P

HEADS = 14
KV_HEADS = 2
HEAD_DIM = 64
GROUPS = HEADS // KV_HEADS
D = 896
FF = 4864
QKV = 1152
SPAN = 64
ROW = 256
REPL = 16
ZDEV = 4
OWN = D // ZDEV
CHUNK = OWN // REPL
BLOCK = FF // ZDEV
WIN = 1280
STARTS = [128 * ((19 * z) // 2) for z in range(ZDEV)]
SHIFTS = [BLOCK * z - STARTS[z] for z in range(ZDEV)]
KV_WIDTH = KV_HEADS * HEAD_DIM

eps = 1e-06
rope_base = 1000000.0
f32 = jnp.float32
bf16 = jnp.bfloat16

def rms_scale(values):
    return lax.rsqrt(jnp.mean(values * values, axis=-1, keepdims=True) + eps)


def doc_tables(doc_lens, group_at):
    doc_ends = jnp.cumsum(doc_lens)
    doc_starts = doc_ends - doc_lens
    row_spots = jnp.arange(ROW, dtype=jnp.int32)
    segment = jnp.sum((doc_ends[None, :] <= row_spots[:, None]).astype(jnp.int32), axis=1)
    doc_pick = segment[:, None] == jnp.arange(doc_lens.shape[0], dtype=jnp.int32)[None, :]
    doc_begin = jnp.sum(jnp.where(doc_pick, doc_starts[None, :], 0), axis=1)
    first_row = group_at * SPAN
    own_segment = lax.dynamic_slice_in_dim(segment, first_row, SPAN)
    own_spots = lax.dynamic_slice_in_dim(row_spots, first_row, SPAN)
    own_begin = lax.dynamic_slice_in_dim(doc_begin, first_row, SPAN)
    allowed = (own_segment[:, None] == segment[None, :]) & (
        row_spots[None, :] <= own_spots[:, None]
    )
    inv_freqs = rope_base ** (-jnp.arange(0, HEAD_DIM, 2, dtype=f32) / HEAD_DIM)
    angles = (own_spots - own_begin).astype(f32)[:, None] * inv_freqs[None, :]
    cosine, sine = jnp.cos(angles), jnp.sin(angles)
    blank = jnp.zeros_like(sine)
    cosine = jnp.concatenate([cosine] * 4, axis=1)
    sine_up = jnp.concatenate([-sine, blank] * 2, axis=1)
    sine_down = jnp.concatenate([blank, sine] * 2, axis=1)
    return (allowed.astype(f32), cosine, sine_up, sine_down)


MESH = pl.DeviceIdType.MESH
TILES_R = OWN // 16
COLS = 15232
PART_A = (0, 7680)
PART_B = (7680, 12928)
PART_C = (12928, 15232)
DOWN_AT = 4 * 2 * WIN
QO_AT = PART_C[0]
VEC_AT = QO_AT + QKV + D
RING = 4


def halves(start, stop):
    middle = start + ((stop - start) // 128 + 1) // 2 * 128
    return ((start, middle), (middle, stop))


def ring_spot(spot, steps):
    return lax.rem(spot + steps + RING, RING)


class Links:
    def __init__(self, send_sems, recv_sems):
        self.send_sems, self.recv_sems, self.used, self.started = send_sems, recv_sems, 0, {}

    def take(self, count):
        first = self.used
        self.used += count
        return first

    def copy(self, source, target, sem_at, device):
        return pltpu.make_async_remote_copy(
            src_ref=source,
            dst_ref=target,
            send_sem=self.send_sems.at[sem_at],
            recv_sem=self.recv_sems.at[sem_at],
            device_id=device,
            device_id_type=MESH,
        )

    def send(self, source, target, sem_at, device):
        copy = self.copy(source, target, sem_at, device)
        copy.start()
        self.started[sem_at] = lambda: copy

    def send_block(self, block, spot, half, sem_at, device):
        def again():
            return self.copy(block(spot, half), block(spot, half), sem_at, device)

        again().start()
        self.started[sem_at] = again

    def arrived(self, target, sem_at, device):
        self.copy(target, target, sem_at, device).wait_recv()

    def finish(self):
        for copy in self.started.values():
            copy().wait_send()
        self.started = {}


class RingSum:
    def __init__(self, links, spot, device_at, block, first, second, left, right, add):
        self.links, self.block, self.add = links, block, add
        self.spots = [ring_spot(spot, steps) for steps in (0, 1, 2, -1)]
        self.right, self.left = device_at(ring_spot(spot, 1)), device_at(ring_spot(spot, -1))
        self.first, self.second, self.from_left, self.from_right = first, second, left, right
        self.sem = links.take(6)

    def start(self):
        send, sem, spots = self.links.send, self.sem, self.spots
        send(self.block(spots[2], 0), self.first, sem, self.right)
        send(self.block(spots[2], 1), self.second, sem + 1, self.left)
        send(self.block(spots[1], 1), self.from_left(1), sem + 2, self.right)
        send(self.block(spots[-1], 0), self.from_right(0), sem + 3, self.left)

    def middle(self):
        links, sem, spots = self.links, self.sem, self.spots
        links.arrived(self.first, sem, self.right)
        onward = self.block(spots[1], 0)
        self.add(onward, onward, self.first)
        links.send(onward, self.from_left(0), sem + 4, self.right)
        links.arrived(self.second, sem + 1, self.left)
        onward = self.block(spots[-1], 1)
        self.add(onward, onward, self.second)
        links.send(onward, self.from_right(1), sem + 5, self.left)

    def end(self, result):
        links, sem, spots = self.links, self.sem, self.spots
        links.arrived(self.from_left(1), sem + 2, self.right)
        links.arrived(self.from_right(0), sem + 3, self.left)
        links.arrived(self.from_left(0), sem + 4, self.right)
        links.arrived(self.from_right(1), sem + 5, self.left)
        for half in (0, 1):
            self.add(
                result(half), self.block(spots[0], half), self.from_left(half), self.from_right(half)
            )


class RingShare:
    def __init__(self, links, spot, device_at, block, sibling=None):
        self.links, self.block, self.sibling = links, block, sibling
        self.spots = [ring_spot(spot, steps) for steps in (0, 1, 2, -1)]
        self.right, self.left = device_at(self.spots[1]), device_at(self.spots[-1])
        self.sem = links.take(6)
        self.twin = links.take(8) if sibling else 0

    def send(self, steps, half, at, device):
        self.links.send_block(self.block, self.spots[steps], half, self.sem + at, device)

    def pass_on(self, steps, half):
        if self.sibling:
            sem = self.twin + 2 * (steps % RING) + half
            self.links.send_block(self.block, self.spots[steps], half, sem, self.sibling)

    def arrived(self, steps, half, at, device, onward=None):
        self.links.arrived(self.block(self.spots[steps], half), self.sem + at, device)
        if onward:
            self.send(steps, half, *onward)
        self.pass_on(steps, half)

    def start(self):
        self.send(0, 0, 0, self.right)
        self.send(0, 1, 2, self.left)
        self.send(0, 1, 1, self.right)
        self.send(0, 0, 3, self.left)
        self.pass_on(0, 0)
        self.pass_on(0, 1)

    def middle(self):
        self.arrived(-1, 0, 0, self.right, (4, self.right))
        self.arrived(1, 1, 2, self.left, (5, self.left))

    def end(self):
        self.arrived(-1, 1, 1, self.right)
        self.arrived(1, 0, 3, self.left)
        self.arrived(2, 0, 4, self.right)
        self.arrived(2, 1, 5, self.left)

    def end_twin(self, twin_block):
        for steps in range(RING):
            for half in (0, 1):
                view = twin_block(self.spots[steps], half)
                self.links.arrived(view, self.twin + 2 * steps + half, self.sibling)


def add_into(target, *sources):
    if len(target.shape) == 3:
        for at in range(target.shape[0]):
            add_into(target.at[at], *[source.at[at] for source in sources])
        return
    total = sources[0][...].astype(f32)
    for source in sources[1:]:
        total = total + source[...].astype(f32)
    target[...] = total.astype(target.dtype)


def greet(replica_spots, group_spots, section_spots=()):
    barrier = pltpu.get_barrier_semaphore()
    spots = {"replica": replica_spots, "group": group_spots, "section": section_spots}
    for axis, members in spots.items():
        for spot in members:
            pl.semaphore_signal(barrier, inc=1, device_id={axis: spot}, device_id_type=MESH)
    pl.semaphore_wait(barrier, sum(map(len, spots.values())))


def grads_kernel(
    n2_rows, dgu, act_rows, dmlp, left_tokens, right_tokens, vecs,
    shared, n2t, act, left_rows, right_rows, vec, part, own, zbuf, left_all, right_all, vec_all,
    a_first, a_second, a_left, a_right, a_sum, a_first2, a_second2, a_left2, a_right2,
    b_first, b_second, b_left, b_right, b_sum, b_first2, b_second2, b_left2, b_right2,
    c_first, c_second, c_left, c_right, c_sum, c_first2, c_second2, c_left2, c_right2,
    send_sems, recv_sems,
):
    group_at = lax.axis_index("group")
    replica_at = lax.axis_index("replica")
    x_at, y_at = replica_at // RING, lax.rem(replica_at, RING)
    links = Links(send_sems, recv_sems)

    def along_x(spot):
        return {"replica": spot * RING + y_at}

    def along_y(spot):
        return {"replica": x_at * RING + spot}

    peers = [ring_spot(group_at, step) for step in (1, 2, 3)]
    greet(
        [
            ring_spot(x_at, 1) * RING + y_at,
            ring_spot(x_at, -1) * RING + y_at,
            x_at * RING + ring_spot(y_at, 1),
            x_at * RING + ring_spot(y_at, -1),
        ],
        peers,
    )
    right_rows[...] = right_tokens[...].reshape(2 * SPAN, QKV + D)
    vec[...] = vecs[0] + vecs[1]
    tall = left_tokens[...].reshape(2 * SPAN, 2 * D).T
    for z in range(ZDEV):
        left_rows[z, :OWN] = tall[OWN * z : OWN * (z + 1)]
        left_rows[z, OWN:] = tall[D + OWN * z : D + OWN * (z + 1)]
    tok_sem = links.take(9)
    for step, peer in enumerate(peers):
        for at, (source, target) in enumerate(
            [
                (left_rows.at[peer], left_all.at[group_at]),
                (right_rows, right_all.at[group_at]),
                (vec, vec_all.at[group_at]),
            ]
        ):
            links.send(source, target, tok_sem + 3 * step + at, {"group": peer})
    left_all[group_at] = left_rows[group_at]
    right_all[group_at] = right_rows[...]
    vec_all[group_at] = vec[...]

    n2t[...] = n2_rows[...].T
    act[...] = act_rows[...].T

    def gate_up(tile, carry):
        at = pl.multiple_of(tile * 256, 256)
        block = jnp.dot(n2t[...], dgu[:, pl.ds(at, 256)], preferred_element_type=f32).astype(bf16)
        block = block.reshape(ZDEV, TILES_R, 16, 256)
        for z in range(ZDEV):
            where = pl.multiple_of(tile * 256 + z * 2 * WIN, 128)
            for r in range(TILES_R):
                part[r // RING, r % RING, :, pl.ds(where, 256)] = block[z, r]
        return carry

    lax.fori_loop(0, 2 * WIN // 256, gate_up, 0)
    shift = lax.rem(group_at, 2) * 64
    for quarter in range(4):
        rows = pl.ds(pl.multiple_of(shift + 304 * quarter, 16), 304)
        block = jnp.dot(act[rows, :], dmlp[...], preferred_element_type=f32).astype(bf16)
        block = block.reshape(19, 16, D)
        for inner in range(19):
            tile = 19 * quarter + inner
            if tile < 3 * TILES_R:
                r, at = tile // 3, DOWN_AT + D * (tile % 3)
            else:
                r, at = TILES_R + (tile - 3 * TILES_R) // 17, D * ((tile - 3 * TILES_R) % 17)
            part[r // RING, r % RING, :, at : at + D] = block[inner]

    def summers(cols, x_first, bufs):
        first, second, left, right, total, first2, second2, left2, right2 = bufs
        start, stop = cols

        def big(spot, half):
            span = pl.ds(2 * half, 2)
            if x_first:
                return part.at[spot, span, :, start:stop]
            return part.at[span, spot, :, start:stop]

        cuts = halves(0, stop - start)

        def small(spot, half):
            return total.at[spot, :, cuts[half][0] : cuts[half][1]]

        def pair(buf):
            return lambda half: buf.at[pl.ds(2 * half, 2)]

        def cut(buf):
            return lambda half: buf.at[:, cuts[half][0] : cuts[half][1]]

        one = (x_at, along_x) if x_first else (y_at, along_y)
        two = (y_at, along_y) if x_first else (x_at, along_x)
        stage_one = RingSum(
            links, *one, big, first, second, pair(left), pair(right), add_into
        )
        stage_two = RingSum(
            links, *two, small, first2, second2, cut(left2), cut(right2), add_into
        )

        def result(half):
            return own.at[:, start + cuts[half][0] : start + cuts[half][1]]

        return stage_one, stage_two, pair(total), result

    a_one, a_two, a_mid, a_result = summers(
        PART_A, True,
        (a_first, a_second, a_left, a_right, a_sum, a_first2, a_second2, a_left2, a_right2),
    )
    b_one, b_two, b_mid, b_result = summers(
        PART_B, False,
        (b_first, b_second, b_left, b_right, b_sum, b_first2, b_second2, b_left2, b_right2),
    )
    c_one, c_two, c_mid, c_result = summers(
        PART_C, False,
        (c_first, c_second, c_left, c_right, c_sum, c_first2, c_second2, c_left2, c_right2),
    )
    a_one.start()
    b_one.start()
    a_one.middle()
    b_one.middle()
    for step, peer in enumerate(peers):
        source = ring_spot(group_at, -1 - step)
        for at, target in enumerate((left_all, right_all, vec_all)):
            links.arrived(target.at[source], tok_sem + 3 * step + at, {"group": peer})
    for width, col, row in ((QKV, 0, 0), (D, QKV, OWN)):
        total = jnp.dot(
            left_all[0, row : row + OWN], right_all[0, :, col : col + width],
            preferred_element_type=f32,
        )
        for z in range(1, ZDEV):
            total = total + jnp.dot(
                left_all[z, row : row + OWN], right_all[z, :, col : col + width],
                preferred_element_type=f32,
            )
        total = total.astype(bf16).reshape(TILES_R, 16, width)
        for r in range(TILES_R):
            part[r // RING, r % RING, :, QO_AT + col : QO_AT + col + width] = total[r]
    part[0, 0, :, VEC_AT:COLS] = (
        vec_all[0] + vec_all[1] + vec_all[2] + vec_all[3]
    ).astype(bf16)
    for r in range(1, TILES_R):
        part[r // RING, r % RING, :, VEC_AT:COLS] = jnp.zeros((16, COLS - VEC_AT), bf16)
    c_one.start()
    a_one.end(a_mid)
    a_two.start()
    b_one.end(b_mid)
    b_two.start()
    c_one.middle()
    a_two.middle()
    b_two.middle()
    c_one.end(c_mid)
    c_two.start()
    a_two.end(a_result)
    b_two.end(b_result)
    slot_sem = links.take(3)
    for step, peer in enumerate(peers):
        where = pl.multiple_of(peer * 2 * WIN, 128)
        links.send(
            own.at[:, pl.ds(where, 2 * WIN)], zbuf.at[group_at], slot_sem + step, {"group": peer}
        )
    where = pl.multiple_of(group_at * 2 * WIN, 128)
    zbuf[group_at] = own[:, pl.ds(where, 2 * WIN)]
    c_two.middle()
    c_two.end(c_result)
    for step, peer in enumerate(peers):
        links.arrived(zbuf.at[ring_spot(group_at, -1 - step)], slot_sem + step, {"group": peer})

    @pl.when(replica_at < TILES_R)
    def _():
        for which in (0, 1):
            base, at = which * FF, which * WIN
            for z in range(ZDEV):
                low = 128 if z % 2 else 0
                high = WIN if z % 2 else WIN - 128
                to = base + STARTS[z]
                shared[x_at, y_at, :, to + low : to + high] = zbuf[z, :, at + low : at + high]
            for z in (0, 2):
                to = base + STARTS[z + 1]
                shared[x_at, y_at, :, to : to + 128] = (
                    zbuf[z, :, at + WIN - 128 : at + WIN] + zbuf[z + 1, :, at : at + 128]
                )
        shared[x_at, y_at, :, 2 * FF : 2 * FF + 512] = jnp.zeros((16, 512), bf16)
        shared[x_at, y_at, :, DOWN_AT:COLS] = own[:, DOWN_AT:COLS]

    @pl.when(replica_at >= TILES_R)
    def _():
        shared[x_at, y_at] = own[...]

    def sharers(cols, x_first):
        start, stop = cols
        cuts = halves(start, stop)

        def small(spot, half):
            low, high = cuts[half]
            if x_first:
                return shared.at[spot, y_at, :, low:high]
            return shared.at[x_at, spot, :, low:high]

        def big(spot, half):
            span = pl.ds(2 * half, 2)
            if x_first:
                return shared.at[span, spot, :, start:stop]
            return shared.at[spot, span, :, start:stop]

        one = (x_at, along_x) if x_first else (y_at, along_y)
        two = (y_at, along_y) if x_first else (x_at, along_x)
        return RingShare(links, *one, small), RingShare(links, *two, big)

    a_one, a_two = sharers((0, 7680), False)
    b_one, b_two = sharers((7680, COLS), True)
    a_one.start()
    b_one.start()
    a_one.middle()
    b_one.middle()
    a_one.end()
    a_two.start()
    b_one.end()
    b_two.start()
    a_two.middle()
    b_two.middle()
    a_two.end()
    b_two.end()
    links.finish()


def share_grads(n2, dgu, act, dmlp, lefts, rights, vecs):
    def bufs(cols):
        width = cols[1] - cols[0]
        low, high = [b - a for a, b in halves(0, width)]
        shapes = [(2, 16, width), (2, 16, width), (4, 16, width), (4, 16, width), (4, 16, width)]
        shapes = shapes + [(16, low), (16, high), (16, width), (16, width)]
        return [pltpu.VMEM(shape, bf16) for shape in shapes]

    vmem = pl.BlockSpec(memory_space=pltpu.VMEM)
    sems = 9 + 3 + 6 * 6 + 4 * 6
    return pl.pallas_call(
        grads_kernel,
        out_shape=jax.ShapeDtypeStruct((RING, RING, 16, COLS), bf16),
        in_specs=[vmem] * 7,
        out_specs=vmem,
        scratch_shapes=[
            pltpu.VMEM((D, 2 * ROW), bf16),
            pltpu.VMEM((WIN, 2 * ROW), bf16),
            pltpu.VMEM((ZDEV, 2 * OWN, 2 * SPAN), bf16),
            pltpu.VMEM((2 * SPAN, QKV + D), bf16),
            pltpu.VMEM((16, 256), f32),
            pltpu.VMEM((RING, RING, 16, COLS), bf16),
            pltpu.VMEM((16, COLS), bf16),
            pltpu.VMEM((ZDEV, 16, 2 * WIN), bf16),
            pltpu.VMEM((ZDEV, 2 * OWN, 2 * SPAN), bf16),
            pltpu.VMEM((ZDEV, 2 * SPAN, QKV + D), bf16),
            pltpu.VMEM((ZDEV, 16, 256), f32),
            *bufs(PART_A),
            *bufs(PART_B),
            *bufs(PART_C),
            pltpu.SemaphoreType.DMA((sems,)),
            pltpu.SemaphoreType.DMA((sems,)),
        ],
        compiler_params=pltpu.CompilerParams(
            collective_id=1, has_side_effects=True, vmem_limit_bytes=58 * 1024 * 1024
        ),
        name="grads",
    )(n2, dgu, act, dmlp, lefts, rights, vecs)


def widen_kernel(block, rest, gate, up, qkv, out, down):
    at = pl.program_id(0)
    for target, start, width in (
        (gate, 0, FF), (up, FF, FF), (qkv, QO_AT, QKV), (out, QO_AT + QKV, D),
    ):
        target[...] = block[0, :, start : start + width].astype(f32)
    for inner in range(3):
        rows = pl.ds(pl.multiple_of((3 * at + inner) * 16, 16), 16)
        start = DOWN_AT + D * inner
        down[rows, :] = block[0, :, start : start + D].astype(f32)
    for tile in range(34):

        @pl.when(at == tile // 3)
        def _():
            rows = pl.ds((3 * TILES_R + tile) * 16, 16)
            start = D * (tile % 17)
            down[rows, :] = rest[tile // 17, :, start : start + D].astype(f32)


def widen(shared):
    rows = [FF, FF, QKV, D]
    return pl.pallas_call(
        widen_kernel,
        grid=(TILES_R,),
        out_shape=[jax.ShapeDtypeStruct((OWN, width), f32) for width in rows]
        + [jax.ShapeDtypeStruct((BLOCK, D), f32)],
        in_specs=[
            pl.BlockSpec((1, 16, COLS), lambda at: (at, 0, 0)),
            pl.BlockSpec((2, 16, COLS), lambda at: (TILES_R // 2, 0, 0)),
        ],
        out_specs=[pl.BlockSpec((16, width), lambda at: (at, 0)) for width in rows]
        + [pl.BlockSpec((BLOCK, D), lambda at: (0, 0))],
        compiler_params=pltpu.CompilerParams(vmem_limit_bytes=40 * 1024 * 1024),
        name="widen",
    )(shared, shared)


def weight_grads(n2, dgu, act, dmlp, lefts, rights, vecs):
    group_at = lax.axis_index("group")
    shared = share_grads(
        n2.reshape(2 * ROW, D),
        dgu.reshape(2 * ROW, 2 * WIN),
        act.reshape(2 * ROW, WIN),
        dmlp.reshape(2 * ROW, D),
        lefts,
        rights,
        vecs,
    )
    shared = shared.reshape(REPL, 16, COLS)
    grad_gate, grad_up, grad_qkv, grad_out, grad_down = widen(shared)
    vec = shared[0, :, VEC_AT:].reshape(16 * 256).astype(f32)

    def own_part(start, width):
        return lax.dynamic_slice_in_dim(vec, start + group_at * width, width, 0)

    return (
        grad_qkv,
        own_part(0, QKV // ZDEV),
        grad_out,
        grad_gate,
        grad_up,
        grad_down,
        own_part(QKV, OWN),
        own_part(QKV + D, OWN),
    )


PAIRS = HEADS // 2
KINDS = (((0, 1, 2, 3), 0), ((0, 1, 2), 1), ((4, 5, 6), 2), ((3, 4, 5, 6), 3))
SCALE = HEAD_DIM ** (-0.5)
TILE = 256


def dot_nt(left, right):
    return lax.dot_general(left, right, (((1,), (1,)), ((), ())), preferred_element_type=f32)


def dot_tn(left, right):
    return lax.dot_general(left, right, (((0,), (0,)), ((), ())), preferred_element_type=f32)


def spread(pair):
    low = lax.broadcasted_iota(jnp.int32, pair.shape, 1) < HEAD_DIM
    wide = pair.astype(f32)
    turned = pltpu.roll(wide, HEAD_DIM, 1)
    zero = jnp.zeros_like(wide)
    members = (
        jnp.where(low, wide, zero),
        jnp.where(low, zero, turned),
        jnp.where(low, turned, zero),
        jnp.where(low, zero, wide),
    )
    return [member.astype(bf16) for member in members]


def unspread(kinds):
    low = lax.broadcasted_iota(jnp.int32, kinds[0].shape, 1) < HEAD_DIM
    straight = jnp.where(low, kinds[0], kinds[3])
    crossed = jnp.where(low, kinds[2], kinds[1])
    return straight + pltpu.roll(crossed, HEAD_DIM, 1)


def stack_pairs(tokens, kind):
    return jnp.concatenate(
        [tokens[:, 2 * HEAD_DIM * p : 2 * HEAD_DIM * (p + 1)] for p in KINDS[kind][0]], axis=0
    )


def join_pairs(kinds):
    found = [None] * PAIRS
    for kind, (pairs, _) in enumerate(KINDS):
        for at, p in enumerate(pairs):
            part = kinds[kind][SPAN * at : SPAN * (at + 1)]
            found[p] = part if found[p] is None else found[p] + part
    return jnp.concatenate(found, axis=1)


def turn(values, cosine, sine_up, sine_down, sign):
    tiles = []
    for at in range(values.shape[1] // 128):
        tile = values[:, 128 * at : 128 * (at + 1)]
        up = pltpu.roll(tile, 128 - HEAD_DIM // 2, 1)
        down = pltpu.roll(tile, HEAD_DIM // 2, 1)
        tiles.append(tile * cosine + sign * (up * sine_up + down * sine_down))
    return jnp.concatenate(tiles, axis=1)


def layers_kernel(
    tokens, cotangent, mask, cosine, sine_up, sine_down, vec,
    w_qkv, w_out, w_gate, w_up, w_down,
    acts, grads_in, out_n2, out_dgu, out_act, out_dmlp, out_left, out_right, out_vec,
    joint, wide, down, vectors, zeros,
    xs, n1s, qs, kvs, probs, ctx, hid, n2s, gus, act, ysend, yrecv,
    dys, dmlp, dgu, dn2, dsend, drecv, dkvsend, dkvrecv, lefts, rights, vecs, igs,
    send_sems, recv_sems, away_send, away_recv, stay_sems, ring_send, ring_recv, local_sems,
):
    section_at = lax.axis_index("section")
    group_at = lax.axis_index("group")
    replica_at = lax.axis_index("replica")
    x_at, y_at = replica_at // RING, lax.rem(replica_at, RING)
    other = 1 - section_at
    sibling = {"section": other}
    links = Links(ring_send, ring_recv)

    def along_x(spot):
        return {"replica": spot * RING + y_at}

    def along_y(spot):
        return {"replica": x_at * RING + spot}

    def along_z(spot):
        return {"group": spot}

    zeros[...] = jnp.zeros_like(zeros)
    peers = [ring_spot(group_at, step) for step in (1, 2, 3)]
    sources = [ring_spot(group_at, -step) for step in (1, 2, 3)]
    greet(
        [
            ring_spot(x_at, 1) * RING + y_at,
            ring_spot(x_at, -1) * RING + y_at,
            x_at * RING + ring_spot(y_at, 1),
            x_at * RING + ring_spot(y_at, -1),
        ],
        peers,
        [other],
    )
    row_tile = pl.ds(pl.multiple_of(jnp.minimum(replica_at, TILES_R - 1) * 16, 16), 16)
    slots = []
    for which, source in enumerate((w_gate, w_up)):
        target = wide.at[section_at, group_at, x_at, y_at, :, WIN * which : WIN * (which + 1)]
        slots.append((source, target))

    def window(source, spot):
        start = pl.multiple_of((19 * spot) // 2 * 128, 128)
        return source.at[row_tile, pl.ds(start, WIN)]

    slot_sem = links.take(6)
    for step, peer in enumerate(peers):
        for which, (source, target) in enumerate(slots):
            links.send(window(source, peer), target, slot_sem + 2 * step + which, along_z(peer))
    vec_sem = links.take(4)
    for step, peer in enumerate(peers):
        links.send(vec, vectors.at[section_at, group_at], vec_sem + step, along_z(peer))
    shift = lax.rem(group_at, 2) * 64
    body = pl.ds(pl.multiple_of(shift, 64), BLOCK)
    gap = pl.ds(pl.multiple_of(BLOCK - 19 * shift, 64), 64)
    locals_ = []
    for source, target in [
        *[(window(source, group_at), target) for source, target in slots],
        (w_qkv, joint.at[section_at, group_at, :, 0:QKV]),
        (w_out, joint.at[section_at, group_at, :, QKV : QKV + D]),
        (w_down, down.at[section_at, body]),
        (zeros, down.at[0, gap]),
        (zeros, down.at[1, gap]),
        (vec, vectors.at[section_at, group_at]),
    ]:
        copy = pltpu.make_async_copy(source, target, local_sems.at[len(locals_)])
        copy.start()
        locals_.append(copy)
    down_sem = links.take(1)
    links.send(w_down, down.at[section_at, body], down_sem, sibling)

    def joint_block(spot, half):
        return joint.at[section_at, spot, pl.ds(112 * half, 112)]

    def joint_twin(spot, half):
        return joint.at[other, spot, pl.ds(112 * half, 112)]

    joint_share = RingShare(links, group_at, along_z, joint_block, sibling)

    def sharers(which, x_first):
        start = WIN * which

        def small(spot, half):
            cols = pl.ds(start + WIN // 2 * half, WIN // 2)
            if x_first:
                return wide.at[section_at, :, spot, y_at, :, cols]
            return wide.at[section_at, :, x_at, spot, :, cols]

        def big(spot, half, layer=section_at):
            span, cols = pl.ds(2 * half, 2), pl.ds(start, WIN)
            if x_first:
                return wide.at[layer, :, span, spot, :, cols]
            return wide.at[layer, :, spot, span, :, cols]

        one = (x_at, along_x) if x_first else (y_at, along_y)
        two = (y_at, along_y) if x_first else (x_at, along_x)
        stage_two = RingShare(links, *two, big, sibling)
        return RingShare(links, *one, small), stage_two, lambda spot, half: big(spot, half, other)

    gate_one, gate_two, gate_twin = sharers(0, False)
    up_one, up_two, up_twin = sharers(1, True)

    @pl.when(section_at == 0)
    def _():
        locals_[2].wait()
        locals_[3].wait()
        joint_share.start()

    for which, share in ((0, gate_one), (1, up_one)):
        locals_[which].wait()
        for step, spot in enumerate(sources):
            cols = pl.ds(WIN * which, WIN)
            target = wide.at[section_at, spot, x_at, y_at, :, cols]
            links.arrived(target, slot_sem + 2 * step + which, along_z(peers[step]))
        share.start()
    gate_one.middle()
    up_one.middle()
    gate_one.end()
    up_one.end()

    @pl.when(section_at == 0)
    def _():
        gate_two.start()
        up_two.start()

    locals_[7].wait()
    for step, spot in enumerate(sources):
        links.arrived(vectors.at[section_at, spot], vec_sem + step, along_z(peers[step]))
    links.send(vectors.at[section_at], vectors.at[section_at], vec_sem + 3, sibling)

    @pl.when(section_at == 0)
    def _():
        joint_share.middle()
        gate_two.middle()
        up_two.middle()
        joint_share.end()

    @pl.when(section_at == 1)
    def _():
        locals_[2].wait()
        locals_[3].wait()
        joint_share.end_twin(joint_twin)
        joint_share.start()

    links.arrived(vectors.at[other], vec_sem + 3, sibling)
    for at in (4, 5, 6):
        locals_[at].wait()

    def while_keys_travel():
        @pl.when(section_at == 0)
        def _():
            gate_two.end()
            up_two.end()

        @pl.when(section_at == 1)
        def _():
            gate_two.start()
            up_two.start()
            joint_share.middle()

    def while_rows_travel():
        @pl.when(section_at == 1)
        def _():
            gate_two.middle()
            up_two.middle()
            gate_two.end_twin(gate_twin)
            up_two.end_twin(up_twin)

        links.arrived(down.at[other, body], down_sem, sibling)

    def while_sums_travel():
        @pl.when(section_at == 1)
        def _():
            joint_share.end()
            gate_two.end()
            up_two.end()

    def late_weights(at):
        @pl.when(section_at == 0)
        def _():
            if at == 0:
                joint_share.end_twin(joint_twin)
            else:
                gate_two.end_twin(gate_twin)
                up_two.end_twin(up_twin)

    def vector_row(layer):
        total = vectors[layer, 0]
        for z in range(1, ZDEV):
            total = total + vectors[layer, z]
        return jnp.concatenate([total[at : at + 1] for at in range(8)], axis=1)

    def exchange(layer, which, source, target):
        copies = []
        for step, peer in enumerate(peers):
            copy = pltpu.make_async_remote_copy(
                src_ref=source(peer),
                dst_ref=target(group_at),
                send_sem=send_sems.at[layer, which, step],
                recv_sem=recv_sems.at[layer, which, step],
                device_id={"group": peer},
                device_id_type=MESH,
            )
            copy.start()
            copies.append(copy)

        def finish():
            for step, peer in enumerate(peers):
                landed = target(ring_spot(group_at, -1 - step))
                pltpu.make_async_remote_copy(
                    src_ref=landed,
                    dst_ref=landed,
                    send_sem=send_sems.at[layer, which, step],
                    recv_sem=recv_sems.at[layer, which, step],
                    device_id={"group": peer},
                    device_id_type=MESH,
                ).wait_recv()
            for copy in copies:
                copy.wait_send()

        return finish

    def wide_cols(layer, start):
        block = wide[layer, :, :, :, :, pl.ds(pl.multiple_of(start, 128), TILE)]
        return block.reshape(ZDEV, REPL, 16, TILE)[:, :TILES_R].reshape(D, TILE)

    def joint_cols(layer, start, stop):
        return joint[layer, :, :, start:stop].reshape(D, stop - start)

    def gathered_sum(own, got):
        total = own[group_at].astype(f32)
        for step in (1, 2, 3):
            total = total + got[ring_spot(group_at, step)].astype(f32)
        return total

    def allowed(count):
        return jnp.concatenate([mask[...]] * count, axis=0) > 0.0

    xs[0] = tokens[section_at]
    bias_at, gain_at, gain_two_at = (0, QKV), (QKV, QKV + D), (QKV + D, QKV + 2 * D)

    def forward(layer):
        x = xs[layer].astype(f32)
        row = vector_row(layer)
        gain_one = row[:, gain_at[0] : gain_at[1]]
        gain_two = row[:, gain_two_at[0] : gain_two_at[1]]
        n1 = (x * rms_scale(x) * gain_one).astype(bf16)
        n1s[layer] = n1
        if layer == 1:
            late_weights(0)
        qkv = jnp.dot(n1, joint_cols(layer, 0, QKV), preferred_element_type=f32)
        qkv = qkv + row[:, bias_at[0] : bias_at[1]]
        turned = turn(
            qkv[:, : D + KV_WIDTH], cosine[...], sine_up[...], sine_down[...], 1.0
        ).astype(bf16)
        qs[layer] = turned[:, :D]
        kvs[layer, group_at] = jnp.concatenate(
            [turned[:, D:], qkv[:, D + KV_WIDTH :].astype(bf16)], axis=1
        )
        done = exchange(
            layer, 0, lambda peer: kvs.at[layer, group_at], lambda spot: kvs.at[layer, spot]
        )
        if layer == 0:
            while_keys_travel()
        done()
        kv = kvs[layer].reshape(ROW, 2 * KV_WIDTH)
        keys, values = spread(kv[:, :KV_WIDTH]), spread(kv[:, KV_WIDTH:])
        outs, at_row = [], 0
        for kind, (pairs, _) in enumerate(KINDS):
            count = SPAN * len(pairs)
            scores = dot_nt(stack_pairs(turned, kind), keys[kind]) * SCALE
            scores = jnp.where(allowed(len(pairs)), scores, -jnp.inf)
            top = jnp.max(scores, axis=-1, keepdims=True)
            raised = jnp.exp(scores - top)
            prob = raised * (1.0 / jnp.sum(raised, axis=-1, keepdims=True))
            probs[layer, at_row : at_row + count] = prob
            outs.append(jnp.dot(prob.astype(bf16), values[kind], preferred_element_type=f32))
            at_row += count
        context = join_pairs(outs).astype(bf16)
        ctx[layer] = context
        hidden = x + jnp.dot(context, joint_cols(layer, QKV, QKV + D), preferred_element_type=f32)
        hid[layer] = hidden
        n2s[layer, group_at] = (hidden * rms_scale(hidden) * gain_two).astype(bf16)
        done = exchange(
            layer, 1, lambda peer: n2s.at[layer, group_at], lambda spot: n2s.at[layer, spot]
        )
        if layer == 0:
            while_rows_travel()
        else:
            late_weights(1)
        done()

        def columns(tile, carry):
            at = tile * TILE
            n2 = n2s[layer].reshape(ROW, D)
            gate = jnp.dot(n2, wide_cols(layer, at), preferred_element_type=f32)
            up = jnp.dot(n2, wide_cols(layer, at + WIN), preferred_element_type=f32)
            gus[layer, 0, :, pl.ds(pl.multiple_of(at, TILE), TILE)] = gate
            gus[layer, 1, :, pl.ds(pl.multiple_of(at, TILE), TILE)] = up
            act[layer, :, pl.ds(pl.multiple_of(at, TILE), TILE)] = (
                gate * jax.nn.sigmoid(gate) * up
            ).astype(bf16)
            return carry

        lax.fori_loop(0, WIN // TILE, columns, 0)
        partial = jnp.dot(act[layer], down[layer], preferred_element_type=f32)
        ysend[layer] = partial.astype(bf16).reshape(ZDEV, SPAN, D)
        done = exchange(
            layer, 2, lambda peer: ysend.at[layer, peer], lambda spot: yrecv.at[layer, spot]
        )
        if layer == 0:
            while_sums_travel()
        done()
        mlp = gathered_sum(ysend.at[layer], yrecv.at[layer])
        xs[layer + 1] = (hidden + mlp).astype(bf16)

    forward(0)
    dmlp[1, group_at] = cotangent[section_at]
    grads_done = exchange(
        1, 3, lambda peer: dmlp.at[1, group_at], lambda spot: dmlp.at[1, spot]
    )
    forward(1)
    grads_done()
    dys[...] = cotangent[section_at].astype(f32)

    def hand_over(layer):
        return [
            (xs.at[layer + 1], acts),
            (igs.at[layer], grads_in),
            (n2s.at[layer], out_n2),
            (dgu.at[layer], out_dgu),
            (act.at[layer], out_act),
            (dmlp.at[layer], out_dmlp),
            (lefts.at[layer], out_left),
            (rights.at[layer], out_right),
            (vecs.at[layer], out_vec),
        ]

    def staying(layer):
        return [
            pltpu.make_async_copy(source, target.at[section_at], stay_sems.at[at])
            for at, (source, target) in enumerate(hand_over(layer))
        ]

    def leaving(layer, slot):
        return [
            pltpu.make_async_remote_copy(
                src_ref=source,
                dst_ref=target.at[slot],
                send_sem=away_send.at[at],
                recv_sem=away_recv.at[at],
                device_id={"section": other},
                device_id_type=MESH,
            )
            for at, (source, target) in enumerate(hand_over(layer))
        ]

    def backward(layer):
        row = vector_row(layer)
        gain_one = row[:, gain_at[0] : gain_at[1]]
        gain_two = row[:, gain_two_at[0] : gain_two_at[1]]
        dy = dys[...]
        if layer == 0:
            dmlp[layer, group_at] = dy.astype(bf16)
            exchange(
                layer, 3, lambda peer: dmlp.at[layer, group_at], lambda spot: dmlp.at[layer, spot]
            )()
        dn2[...] = jnp.zeros_like(dn2)

        def columns(tile, carry):
            at = pl.multiple_of(tile * TILE, TILE)
            grad = dot_nt(dmlp[layer].reshape(ROW, D), down[layer, pl.ds(at, TILE), :])
            gate = gus[layer, 0, :, pl.ds(at, TILE)]
            up = gus[layer, 1, :, pl.ds(at, TILE)]
            sigma = jax.nn.sigmoid(gate)
            grad_gate = (grad * up * sigma * (1.0 + gate * (1.0 - sigma))).astype(bf16)
            grad_up = (grad * gate * sigma).astype(bf16)
            dgu[layer, :, pl.ds(at, TILE)] = grad_gate
            dgu[layer, :, pl.ds(pl.multiple_of(at + WIN, TILE), TILE)] = grad_up
            dn2[...] += dot_nt(grad_gate, wide_cols(layer, at)) + dot_nt(
                grad_up, wide_cols(layer, at + WIN)
            )
            return carry

        lax.fori_loop(0, WIN // TILE, columns, 0)
        dsend[layer] = dn2[...].astype(bf16).reshape(ZDEV, SPAN, D)
        exchange(
            layer, 4, lambda peer: dsend.at[layer, peer], lambda spot: drecv.at[layer, spot]
        )()
        grad_two = gathered_sum(dsend.at[layer], drecv.at[layer])
        hidden = hid[layer]
        scale = rms_scale(hidden)
        scaled = grad_two * gain_two
        inner = jnp.mean(scaled * hidden, axis=-1, keepdims=True)
        dhid = dy + scale * (scaled - hidden * (scale * scale * inner))
        gain_two_term = jnp.sum(grad_two * hidden * scale, axis=0, keepdims=True)
        dt = dhid.astype(bf16)
        rights[layer, :, QKV:] = dt
        do = dot_nt(dt, joint_cols(layer, QKV, QKV + D)).astype(bf16)
        kv = kvs[layer].reshape(ROW, 2 * KV_WIDTH)
        keys, values = spread(kv[:, :KV_WIDTH]), spread(kv[:, KV_WIDTH:])
        queries = qs[layer]
        dqs, dks, dvs, at_row = [], [], [], 0
        for kind, (pairs, _) in enumerate(KINDS):
            count = SPAN * len(pairs)
            prob = probs[layer, at_row : at_row + count]
            grad = stack_pairs(do, kind)
            dprob = dot_nt(grad, values[kind])
            inner = jnp.sum(prob * dprob, axis=-1, keepdims=True)
            dscore = (prob * (dprob - inner)).astype(bf16)
            dqs.append(jnp.dot(dscore, keys[kind], preferred_element_type=f32))
            dks.append(dot_tn(dscore, stack_pairs(queries, kind)))
            dvs.append(dot_tn(prob.astype(bf16), grad))
            at_row += count
        dkv = jnp.concatenate([unspread(dks) * SCALE, unspread(dvs)], axis=1)
        dkvsend[layer] = dkv.astype(bf16).reshape(ZDEV, SPAN, 2 * KV_WIDTH)
        exchange(
            layer, 5, lambda peer: dkvsend.at[layer, peer], lambda spot: dkvrecv.at[layer, spot]
        )()
        dkv = gathered_sum(dkvsend.at[layer], dkvrecv.at[layer])
        dqk = jnp.concatenate([join_pairs(dqs) * SCALE, dkv[:, :KV_WIDTH]], axis=1)
        dqk = turn(dqk, cosine[...], sine_up[...], sine_down[...], -1.0)
        dqkv = jnp.concatenate([dqk, dkv[:, KV_WIDTH:]], axis=1).astype(bf16)
        rights[layer, :, :QKV] = dqkv
        lefts[layer, :, :D] = n1s[layer]
        lefts[layer, :, D:] = ctx[layer]
        bias_term = jnp.sum(dqkv.astype(f32), axis=0, keepdims=True)
        grad_one = dot_nt(dqkv, joint_cols(layer, 0, QKV))
        x = xs[layer].astype(f32)
        scale = rms_scale(x)
        scaled = grad_one * gain_one
        inner = jnp.mean(scaled * x, axis=-1, keepdims=True)
        dx = dhid + scale * (scaled - x * (scale * scale * inner))
        gain_one_term = jnp.sum(grad_one * x * scale, axis=0, keepdims=True)
        rounded = dx.astype(bf16).astype(f32)
        dys[...] = rounded
        igs[layer] = rounded if layer == 1 else dx
        terms = jnp.concatenate(
            [bias_term, gain_one_term, gain_two_term, jnp.zeros((1, 128), f32)], axis=1
        )
        for at in range(12):
            vecs[layer, at : at + 1, :] = terms[:, 256 * at : 256 * (at + 1)]
        vecs[layer, 12:16, :] = jnp.zeros((4, 256), f32)

        @pl.when(layer == section_at)
        def _():
            for copy in staying(layer):
                copy.start()

        @pl.when(layer != section_at)
        def _():
            for copy in leaving(layer, section_at):
                copy.start()

    backward(1)
    backward(0)
    for copy in staying(section_at):
        copy.wait()
    for copy in leaving(other, section_at):
        copy.wait_send()
    for copy in leaving(other, other):
        copy.wait_recv()
    links.finish()


def run_layers(tokens, cotangent, mask, cosine, sine_up, sine_down, vec, *weights):
    vmem = pl.BlockSpec(memory_space=pltpu.VMEM)
    anywhere = pl.BlockSpec(memory_space=pl.ANY)

    def per_micro(shape, kind):
        return jax.ShapeDtypeStruct((2,) + shape, kind)

    sems = 6 + 4 + 1 + 3 * 14 + 2 * 6

    def scratch(shape, kind=bf16, lead=2):
        return pltpu.VMEM((lead,) + shape, kind)

    return pl.pallas_call(
        layers_kernel,
        out_shape=(
            per_micro((SPAN, D), bf16),
            per_micro((SPAN, D), f32),
            per_micro((ZDEV, SPAN, D), bf16),
            per_micro((ROW, 2 * WIN), bf16),
            per_micro((ROW, WIN), bf16),
            per_micro((ZDEV, SPAN, D), bf16),
            per_micro((SPAN, 2 * D), bf16),
            per_micro((SPAN, QKV + D), bf16),
            per_micro((16, 256), f32),
        ),
        in_specs=[vmem] * 7 + [anywhere] * 5,
        out_specs=[vmem] * 9,
        scratch_shapes=[
            scratch((ZDEV, OWN, QKV + D)),
            scratch((ZDEV, RING, RING, 16, 2 * WIN)),
            scratch((WIN, D)),
            scratch((ZDEV, 8, 384), f32),
            pltpu.VMEM((64, D), bf16),
            scratch((SPAN, D), lead=3),
            scratch((SPAN, D)),
            scratch((SPAN, D)),
            scratch((ZDEV, SPAN, 2 * KV_WIDTH)),
            scratch((HEADS * SPAN, ROW), f32),
            scratch((SPAN, D)),
            scratch((SPAN, D), f32),
            scratch((ZDEV, SPAN, D)),
            scratch((2, ROW, WIN), f32),
            scratch((ROW, WIN)),
            scratch((ZDEV, SPAN, D)),
            scratch((ZDEV, SPAN, D)),
            pltpu.VMEM((SPAN, D), f32),
            scratch((ZDEV, SPAN, D)),
            scratch((ROW, 2 * WIN)),
            pltpu.VMEM((ROW, D), f32),
            scratch((ZDEV, SPAN, D)),
            scratch((ZDEV, SPAN, D)),
            scratch((ZDEV, SPAN, 2 * KV_WIDTH)),
            scratch((ZDEV, SPAN, 2 * KV_WIDTH)),
            scratch((SPAN, 2 * D)),
            scratch((SPAN, QKV + D)),
            scratch((16, 256), f32),
            scratch((SPAN, D), f32),
            pltpu.SemaphoreType.DMA((2, 6, 3)),
            pltpu.SemaphoreType.DMA((2, 6, 3)),
            pltpu.SemaphoreType.DMA((9,)),
            pltpu.SemaphoreType.DMA((9,)),
            pltpu.SemaphoreType.DMA((9,)),
            pltpu.SemaphoreType.DMA((sems,)),
            pltpu.SemaphoreType.DMA((sems,)),
            pltpu.SemaphoreType.DMA((8,)),
        ],
        compiler_params=pltpu.CompilerParams(
            collective_id=3, has_side_effects=True, vmem_limit_bytes=60 * 1024 * 1024
        ),
        name="layers",
    )(tokens, cotangent, mask, cosine, sine_up, sine_down, vec, *weights)


def on_device(
    tokens, cotangent, doc_lengths, w_qkv, b_qkv, w_out, w_gate, w_up, w_down, norm_attn, norm_ffn
):
    section_at = lax.axis_index("section")
    group_at = lax.axis_index("group")
    vec = jnp.zeros((8 * 384,), f32)
    for member, start in ((b_qkv, 0), (norm_attn, QKV), (norm_ffn, QKV + D)):
        width = member.shape[1]
        vec = lax.dynamic_update_slice(
            vec, member[0].astype(f32), (start + width * group_at,)
        )
    lengths = lax.dynamic_index_in_dim(doc_lengths, section_at, 0, keepdims=False)[0]
    acts, input_grads, *pieces = run_layers(
        tokens[:, 0],
        cotangent[:, 0],
        *doc_tables(lengths, group_at),
        vec.reshape(8, 384),
        w_qkv[0],
        w_out[0],
        w_gate[0],
        w_up[0],
        w_down[0],
    )
    grads = weight_grads(*pieces)
    return (acts[None, :, None], input_grads[None, :, None]) + tuple(g[None] for g in grads)


def solution(mesh):
    rows = P("section", "group", None)
    vector = P("section", "group")
    spans = P("section", None, "replica", "group", None)
    return jax.shard_map(
        on_device,
        mesh=mesh,
        in_specs=(
            P(None, "replica", "group", None),
            P(None, "replica", "group", None),
            P(None, "replica", None),
            rows,
            vector,
            rows,
            rows,
            rows,
            rows,
            vector,
            vector,
        ),
        out_specs=(spans, spans, rows, vector, rows, rows, rows, rows, vector, vector),
        check_vma=False,
    )
```

```python
import math

import jax
import jax.numpy as jnp
from jax import lax
from jax.experimental import pallas as pl
from jax.experimental.pallas import tpu as pltpu
from jax.sharding import PartitionSpec as P

HEADS = 14
KV_HEADS = 2
HEAD_DIM = 64
GROUPS = HEADS // KV_HEADS
D = 896
FF = 4864
QKV = 1152
SPAN = 64
ROW = 256
REPL = 16
ZDEV = 4
OWN = D // ZDEV
CHUNK = OWN // REPL
BLOCK = FF // ZDEV
WIN = 1280
STARTS = [128 * ((19 * z) // 2) for z in range(ZDEV)]
SHIFTS = [BLOCK * z - STARTS[z] for z in range(ZDEV)]
KV_WIDTH = KV_HEADS * HEAD_DIM

eps = 1e-06
rope_base = 1000000.0
f32 = jnp.float32
bf16 = jnp.bfloat16

def rms_scale(values):
    return lax.rsqrt(jnp.mean(values * values, axis=-1, keepdims=True) + eps)


MESH = pl.DeviceIdType.MESH
TILES_R = OWN // 16
COLS = 15232
PART_A = (0, 7680)
PART_B = (7680, 12928)
PART_C = (12928, 15232)
DOWN_AT = 4 * 2 * WIN
QO_AT = PART_C[0]
VEC_AT = QO_AT + QKV + D
RING = 4


def halves(start, stop):
    middle = start + ((stop - start) // 128 + 1) // 2 * 128
    return ((start, middle), (middle, stop))


def ring_spot(spot, steps):
    return lax.rem(spot + steps + RING, RING)


class Links:
    def __init__(self, send_sems, recv_sems):
        self.send_sems, self.recv_sems, self.used, self.started = send_sems, recv_sems, 0, {}

    def take(self, count):
        first = self.used
        self.used += count
        return first

    def copy(self, source, target, sem_at, device):
        return pltpu.make_async_remote_copy(
            src_ref=source,
            dst_ref=target,
            send_sem=self.send_sems.at[sem_at],
            recv_sem=self.recv_sems.at[sem_at],
            device_id=device,
            device_id_type=MESH,
        )

    def send(self, source, target, sem_at, device):
        copy = self.copy(source, target, sem_at, device)
        copy.start()
        self.started[sem_at] = lambda: copy

    def send_block(self, block, spot, half, sem_at, device):
        def again():
            return self.copy(block(spot, half), block(spot, half), sem_at, device)

        again().start()
        self.started[sem_at] = again

    def arrived(self, target, sem_at, device):
        self.copy(target, target, sem_at, device).wait_recv()

    def finish(self):
        for copy in self.started.values():
            copy().wait_send()
        self.started = {}


class RingSum:
    def __init__(self, links, spot, device_at, block, first, second, left, right, add):
        self.links, self.block, self.add = links, block, add
        self.spots = [ring_spot(spot, steps) for steps in (0, 1, 2, -1)]
        self.right, self.left = device_at(ring_spot(spot, 1)), device_at(ring_spot(spot, -1))
        self.first, self.second, self.from_left, self.from_right = first, second, left, right
        self.sem = links.take(6)

    def start(self):
        send, sem, spots = self.links.send, self.sem, self.spots
        send(self.block(spots[2], 0), self.first, sem, self.right)
        send(self.block(spots[2], 1), self.second, sem + 1, self.left)
        send(self.block(spots[1], 1), self.from_left(1), sem + 2, self.right)
        send(self.block(spots[-1], 0), self.from_right(0), sem + 3, self.left)

    def middle(self):
        links, sem, spots = self.links, self.sem, self.spots
        links.arrived(self.first, sem, self.right)
        onward = self.block(spots[1], 0)
        self.add(onward, onward, self.first)
        links.send(onward, self.from_left(0), sem + 4, self.right)
        links.arrived(self.second, sem + 1, self.left)
        onward = self.block(spots[-1], 1)
        self.add(onward, onward, self.second)
        links.send(onward, self.from_right(1), sem + 5, self.left)

    def end(self, result):
        links, sem, spots = self.links, self.sem, self.spots
        links.arrived(self.from_left(1), sem + 2, self.right)
        links.arrived(self.from_right(0), sem + 3, self.left)
        links.arrived(self.from_left(0), sem + 4, self.right)
        links.arrived(self.from_right(1), sem + 5, self.left)
        for half in (0, 1):
            self.add(
                result(half), self.block(spots[0], half), self.from_left(half), self.from_right(half)
            )


class RingShare:
    def __init__(self, links, spot, device_at, block, sibling=None):
        self.links, self.block, self.sibling = links, block, sibling
        self.spots = [ring_spot(spot, steps) for steps in (0, 1, 2, -1)]
        self.right, self.left = device_at(self.spots[1]), device_at(self.spots[-1])
        self.sem = links.take(6)
        self.twin = links.take(8) if sibling else 0

    def send(self, steps, half, at, device):
        self.links.send_block(self.block, self.spots[steps], half, self.sem + at, device)

    def pass_on(self, steps, half):
        if self.sibling:
            sem = self.twin + 2 * (steps % RING) + half
            self.links.send_block(self.block, self.spots[steps], half, sem, self.sibling)

    def arrived(self, steps, half, at, device, onward=None):
        self.links.arrived(self.block(self.spots[steps], half), self.sem + at, device)
        if onward:
            self.send(steps, half, *onward)
        self.pass_on(steps, half)

    def start(self):
        self.send(0, 0, 0, self.right)
        self.send(0, 1, 2, self.left)
        self.send(0, 1, 1, self.right)
        self.send(0, 0, 3, self.left)
        self.pass_on(0, 0)
        self.pass_on(0, 1)

    def middle(self):
        self.arrived(-1, 0, 0, self.right, (4, self.right))
        self.arrived(1, 1, 2, self.left, (5, self.left))

    def end(self):
        self.arrived(-1, 1, 1, self.right)
        self.arrived(1, 0, 3, self.left)
        self.arrived(2, 0, 4, self.right)
        self.arrived(2, 1, 5, self.left)

    def end_twin(self, twin_block):
        for steps in range(RING):
            for half in (0, 1):
                view = twin_block(self.spots[steps], half)
                self.links.arrived(view, self.twin + 2 * steps + half, self.sibling)


def add_into(target, *sources):
    if len(target.shape) == 3:
        for at in range(target.shape[0]):
            add_into(target.at[at], *[source.at[at] for source in sources])
        return
    total = sources[0][...].astype(f32)
    for source in sources[1:]:
        total = total + source[...].astype(f32)
    target[...] = total.astype(target.dtype)


def greet(replica_spots, group_spots, section_spots=()):
    barrier = pltpu.get_barrier_semaphore()
    spots = {"replica": replica_spots, "group": group_spots, "section": section_spots}
    for axis, members in spots.items():
        for spot in members:
            pl.semaphore_signal(barrier, inc=1, device_id={axis: spot}, device_id_type=MESH)
    pl.semaphore_wait(barrier, sum(map(len, spots.values())))


def grads_kernel(
    n2_rows, dgu, act_rows, dmlp, left_tokens, right_tokens, vecs,
    shared, n2t, act, left_rows, vec, part, own, zbuf, left_all, right_all, vec_all,
    a_first, a_second, a_left, a_right, a_sum, a_first2, a_second2, a_left2, a_right2,
    b_first, b_second, b_left, b_right, b_sum, b_first2, b_second2, b_left2, b_right2,
    c_first, c_second, c_left, c_right, c_sum, c_first2, c_second2, c_left2, c_right2,
    send_sems, recv_sems,
):
    group_at = lax.axis_index("group")
    replica_at = lax.axis_index("replica")
    x_at, y_at = replica_at // RING, lax.rem(replica_at, RING)
    links = Links(send_sems, recv_sems)

    def along_x(spot):
        return {"replica": spot * RING + y_at}

    def along_y(spot):
        return {"replica": x_at * RING + spot}

    peers = [ring_spot(group_at, step) for step in (1, 2, 3)]
    greet(
        [
            ring_spot(x_at, 1) * RING + y_at,
            ring_spot(x_at, -1) * RING + y_at,
            x_at * RING + ring_spot(y_at, 1),
            x_at * RING + ring_spot(y_at, -1),
        ],
        peers,
    )
    right_all[group_at] = right_tokens[...].reshape(2 * SPAN, QKV + D)
    rights_share = RingShare(
        links,
        group_at,
        lambda spot: {"group": spot},
        lambda spot, half: right_all.at[spot, pl.ds(SPAN * half, SPAN)],
    )
    rights_share.start()
    vec[...] = vecs[0] + vecs[1]
    tall = left_tokens[...].reshape(2 * SPAN, 2 * D).T
    for z in range(ZDEV):
        left_rows[z, :OWN] = tall[OWN * z : OWN * (z + 1)]
        left_rows[z, OWN:] = tall[D + OWN * z : D + OWN * (z + 1)]
    tok_sem = links.take(6)
    for step, peer in enumerate(peers):
        for at, (source, target) in enumerate(
            [
                (left_rows.at[peer], left_all.at[group_at]),
                (vec, vec_all.at[group_at]),
            ]
        ):
            links.send(source, target, tok_sem + 2 * step + at, {"group": peer})
    left_all[group_at] = left_rows[group_at]
    vec_all[group_at] = vec[...]

    n2t[...] = n2_rows[...].T

    def gate_up(first, count):
        def columns(tile, carry):
            at = pl.multiple_of(tile * 256, 256)
            block = jnp.dot(
                n2t[OWN * first : OWN * (first + count)],
                dgu[:, pl.ds(at, 256)],
                preferred_element_type=f32,
            ).astype(bf16)
            block = block.reshape(count, TILES_R, 16, 256)
            for z in range(count):
                where = pl.multiple_of(tile * 256 + (first + z) * 2 * WIN, 128)
                for r in range(TILES_R):
                    part[r // RING, r % RING, :, pl.ds(where, 256)] = block[z, r]
            return carry

        lax.fori_loop(0, 2 * WIN // 256, columns, 0)

    act[...] = act_rows[...].T
    def summers(cols, x_first, bufs):
        first, second, left, right, total, first2, second2, left2, right2 = bufs
        start, stop = cols

        def big(spot, half):
            span = pl.ds(2 * half, 2)
            if x_first:
                return part.at[spot, span, :, start:stop]
            return part.at[span, spot, :, start:stop]

        cuts = halves(0, stop - start)

        def small(spot, half):
            return total.at[spot, :, cuts[half][0] : cuts[half][1]]

        def pair(buf):
            return lambda half: buf.at[pl.ds(2 * half, 2)]

        def cut(buf):
            return lambda half: buf.at[:, cuts[half][0] : cuts[half][1]]

        one = (x_at, along_x) if x_first else (y_at, along_y)
        two = (y_at, along_y) if x_first else (x_at, along_x)
        stage_one = RingSum(
            links, *one, big, first, second, pair(left), pair(right), add_into
        )
        stage_two = RingSum(
            links, *two, small, first2, second2, cut(left2), cut(right2), add_into
        )

        def result(half):
            return own.at[:, start + cuts[half][0] : start + cuts[half][1]]

        return stage_one, stage_two, pair(total), result

    a_one, a_two, a_mid, a_result = summers(
        PART_A, True,
        (a_first, a_second, a_left, a_right, a_sum, a_first2, a_second2, a_left2, a_right2),
    )
    b_one, b_two, b_mid, b_result = summers(
        PART_B, False,
        (b_first, b_second, b_left, b_right, b_sum, b_first2, b_second2, b_left2, b_right2),
    )
    c_one, c_two, c_mid, c_result = summers(
        PART_C, False,
        (c_first, c_second, c_left, c_right, c_sum, c_first2, c_second2, c_left2, c_right2),
    )
    shift = lax.rem(group_at, 2) * 64
    for quarter in range(4):
        rows = pl.ds(pl.multiple_of(shift + 304 * quarter, 16), 304)
        block = jnp.dot(act[rows, :], dmlp[...], preferred_element_type=f32).astype(bf16)
        block = block.reshape(19, 16, D)
        for inner in range(19):
            tile = 19 * quarter + inner
            if tile < 3 * TILES_R:
                r, at = tile // 3, DOWN_AT + D * (tile % 3)
            else:
                r, at = TILES_R + (tile - 3 * TILES_R) // 17, D * ((tile - 3 * TILES_R) % 17)
            part[r // RING, r % RING, :, at : at + D] = block[inner]
    rights_share.middle()
    gate_up(0, 3)
    a_one.start()
    gate_up(3, 1)
    b_one.start()
    a_one.middle()
    b_one.middle()
    for step, peer in enumerate(peers):
        source = ring_spot(group_at, -1 - step)
        for at, target in enumerate((left_all, vec_all)):
            links.arrived(target.at[source], tok_sem + 2 * step + at, {"group": peer})
    rights_share.end()
    for width, col, row in ((QKV, 0, 0), (D, QKV, OWN)):
        total = jnp.dot(
            left_all[0, row : row + OWN], right_all[0, :, col : col + width],
            preferred_element_type=f32,
        )
        for z in range(1, ZDEV):
            total = total + jnp.dot(
                left_all[z, row : row + OWN], right_all[z, :, col : col + width],
                preferred_element_type=f32,
            )
        total = total.astype(bf16).reshape(TILES_R, 16, width)
        for r in range(TILES_R):
            part[r // RING, r % RING, :, QO_AT + col : QO_AT + col + width] = total[r]
    part[0, 0, :, VEC_AT:COLS] = (
        vec_all[0] + vec_all[1] + vec_all[2] + vec_all[3]
    ).astype(bf16)
    for r in range(1, TILES_R):
        part[r // RING, r % RING, :, VEC_AT:COLS] = jnp.zeros((16, COLS - VEC_AT), bf16)
    c_one.start()
    a_one.end(a_mid)
    a_two.start()
    b_one.end(b_mid)
    b_two.start()
    c_one.middle()
    a_two.middle()
    b_two.middle()
    c_one.end(c_mid)
    c_two.start()
    a_two.end(a_result)
    b_two.end(b_result)
    slot_sem = links.take(3)
    for step, peer in enumerate(peers):
        where = pl.multiple_of(peer * 2 * WIN, 128)
        links.send(
            own.at[:, pl.ds(where, 2 * WIN)], zbuf.at[group_at], slot_sem + step, {"group": peer}
        )
    where = pl.multiple_of(group_at * 2 * WIN, 128)
    zbuf[group_at] = own[:, pl.ds(where, 2 * WIN)]
    c_two.middle()
    c_two.end(c_result)
    for step, peer in enumerate(peers):
        links.arrived(zbuf.at[ring_spot(group_at, -1 - step)], slot_sem + step, {"group": peer})

    @pl.when(replica_at < TILES_R)
    def _():
        for which in (0, 1):
            base, at = which * FF, which * WIN
            for z in range(ZDEV):
                low = 128 if z % 2 else 0
                high = WIN if z % 2 else WIN - 128
                to = base + STARTS[z]
                shared[x_at, y_at, :, to + low : to + high] = zbuf[z, :, at + low : at + high]
            for z in (0, 2):
                to = base + STARTS[z + 1]
                shared[x_at, y_at, :, to : to + 128] = (
                    zbuf[z, :, at + WIN - 128 : at + WIN] + zbuf[z + 1, :, at : at + 128]
                )
        shared[x_at, y_at, :, 2 * FF : 2 * FF + 512] = jnp.zeros((16, 512), bf16)
        shared[x_at, y_at, :, DOWN_AT:COLS] = own[:, DOWN_AT:COLS]

    @pl.when(replica_at >= TILES_R)
    def _():
        shared[x_at, y_at] = own[...]

    def sharers(cols, x_first):
        start, stop = cols
        cuts = halves(start, stop)

        def small(spot, half):
            low, high = cuts[half]
            if x_first:
                return shared.at[spot, y_at, :, low:high]
            return shared.at[x_at, spot, :, low:high]

        def big(spot, half):
            span = pl.ds(2 * half, 2)
            if x_first:
                return shared.at[span, spot, :, start:stop]
            return shared.at[spot, span, :, start:stop]

        one = (x_at, along_x) if x_first else (y_at, along_y)
        two = (y_at, along_y) if x_first else (x_at, along_x)
        return RingShare(links, *one, small), RingShare(links, *two, big)

    a_one, a_two = sharers((0, 7680), False)
    b_one, b_two = sharers((7680, COLS), True)
    a_one.start()
    b_one.start()
    a_one.middle()
    b_one.middle()
    a_one.end()
    a_two.start()
    b_one.end()
    b_two.start()
    a_two.middle()
    b_two.middle()
    a_two.end()
    b_two.end()
    links.finish()


def share_grads(n2, dgu, act, dmlp, lefts, rights, vecs):
    def bufs(cols):
        width = cols[1] - cols[0]
        low, high = [b - a for a, b in halves(0, width)]
        shapes = [(2, 16, width), (2, 16, width), (4, 16, width), (4, 16, width), (4, 16, width)]
        shapes = shapes + [(16, low), (16, high), (16, width), (16, width)]
        return [pltpu.VMEM(shape, bf16) for shape in shapes]

    vmem = pl.BlockSpec(memory_space=pltpu.VMEM)
    sems = 6 + 6 + 3 + 6 * 6 + 4 * 6
    return pl.pallas_call(
        grads_kernel,
        out_shape=jax.ShapeDtypeStruct((RING, RING, 16, COLS), bf16),
        in_specs=[vmem] * 7,
        out_specs=vmem,
        scratch_shapes=[
            pltpu.VMEM((D, 2 * ROW), bf16),
            pltpu.VMEM((WIN, 2 * ROW), bf16),
            pltpu.VMEM((ZDEV, 2 * OWN, 2 * SPAN), bf16),
            pltpu.VMEM((16, 256), f32),
            pltpu.VMEM((RING, RING, 16, COLS), bf16),
            pltpu.VMEM((16, COLS), bf16),
            pltpu.VMEM((ZDEV, 16, 2 * WIN), bf16),
            pltpu.VMEM((ZDEV, 2 * OWN, 2 * SPAN), bf16),
            pltpu.VMEM((ZDEV, 2 * SPAN, QKV + D), bf16),
            pltpu.VMEM((ZDEV, 16, 256), f32),
            *bufs(PART_A),
            *bufs(PART_B),
            *bufs(PART_C),
            pltpu.SemaphoreType.DMA((sems,)),
            pltpu.SemaphoreType.DMA((sems,)),
        ],
        compiler_params=pltpu.CompilerParams(
            collective_id=1, has_side_effects=True, vmem_limit_bytes=58 * 1024 * 1024
        ),
        name="grads",
    )(n2, dgu, act, dmlp, lefts, rights, vecs)


def widen_kernel(block, rest, gate, up, qkv, out, down):
    at = pl.program_id(0)
    for inner in range(2):
        rows = pl.ds(16 * inner, 16)
        for target, start, width in (
            (gate, 0, FF), (up, FF, FF), (qkv, QO_AT, QKV), (out, QO_AT + QKV, D),
        ):
            target[rows, :] = block[inner, :, start : start + width].astype(f32)
        for place in range(3):
            tile = pl.multiple_of((6 * at + 3 * inner + place) * 16, 16)
            start = DOWN_AT + D * place
            down[pl.ds(tile, 16), :] = block[inner, :, start : start + D].astype(f32)
    for tile in range(34):

        @pl.when(at == tile // 5)
        def _():
            rows = pl.ds((3 * TILES_R + tile) * 16, 16)
            start = D * (tile % 17)
            down[rows, :] = rest[tile // 17, :, start : start + D].astype(f32)


def widen(shared):
    rows = [FF, FF, QKV, D]
    return pl.pallas_call(
        widen_kernel,
        grid=(TILES_R // 2,),
        out_shape=[jax.ShapeDtypeStruct((OWN, width), f32) for width in rows]
        + [jax.ShapeDtypeStruct((BLOCK, D), f32)],
        in_specs=[
            pl.BlockSpec((2, 16, COLS), lambda at: (at, 0, 0)),
            pl.BlockSpec((2, 16, COLS), lambda at: (TILES_R // 2, 0, 0)),
        ],
        out_specs=[pl.BlockSpec((32, width), lambda at: (at, 0)) for width in rows]
        + [pl.BlockSpec((BLOCK, D), lambda at: (0, 0))],
        compiler_params=pltpu.CompilerParams(vmem_limit_bytes=40 * 1024 * 1024),
        name="widen",
    )(shared, shared)


def weight_grads(n2, dgu, act, dmlp, lefts, rights, vecs):
    group_at = lax.axis_index("group")
    shared = share_grads(
        n2.reshape(2 * ROW, D),
        dgu.reshape(2 * ROW, 2 * WIN),
        act.reshape(2 * ROW, WIN),
        dmlp.reshape(2 * ROW, D),
        lefts,
        rights,
        vecs,
    )
    shared = shared.reshape(REPL, 16, COLS)
    grad_gate, grad_up, grad_qkv, grad_out, grad_down = widen(shared)
    vec = shared[0, :, VEC_AT:].reshape(16 * 256).astype(f32)

    def own_part(start, width):
        return lax.dynamic_slice_in_dim(vec, start + group_at * width, width, 0)

    return (
        grad_qkv,
        own_part(0, QKV // ZDEV),
        grad_out,
        grad_gate,
        grad_up,
        grad_down,
        own_part(QKV, OWN),
        own_part(QKV + D, OWN),
    )


PAIRS = HEADS // 2
KINDS = (((0, 1, 2, 3), 0), ((0, 1, 2), 1), ((4, 5, 6), 2), ((3, 4, 5, 6), 3))
SCALE = HEAD_DIM ** (-0.5)
TILE = 256


def dot_nt(left, right):
    return lax.dot_general(left, right, (((1,), (1,)), ((), ())), preferred_element_type=f32)


def dot_tn(left, right):
    return lax.dot_general(left, right, (((0,), (0,)), ((), ())), preferred_element_type=f32)


def spread(pair):
    low = lax.broadcasted_iota(jnp.int32, pair.shape, 1) < HEAD_DIM
    wide = pair.astype(f32)
    turned = pltpu.roll(wide, HEAD_DIM, 1)
    zero = jnp.zeros_like(wide)
    members = (
        jnp.where(low, wide, zero),
        jnp.where(low, zero, turned),
        jnp.where(low, turned, zero),
        jnp.where(low, zero, wide),
    )
    return [member.astype(bf16) for member in members]


def unspread(kinds):
    low = lax.broadcasted_iota(jnp.int32, kinds[0].shape, 1) < HEAD_DIM
    straight = jnp.where(low, kinds[0], kinds[3])
    crossed = jnp.where(low, kinds[2], kinds[1])
    return straight + pltpu.roll(crossed, HEAD_DIM, 1)


def stack_pairs(tokens, kind):
    return jnp.concatenate(
        [tokens[:, 2 * HEAD_DIM * p : 2 * HEAD_DIM * (p + 1)] for p in KINDS[kind][0]], axis=0
    )


def join_pairs(kinds):
    found = [None] * PAIRS
    for kind, (pairs, _) in enumerate(KINDS):
        for at, p in enumerate(pairs):
            part = kinds[kind][SPAN * at : SPAN * (at + 1)]
            found[p] = part if found[p] is None else found[p] + part
    return jnp.concatenate(found, axis=1)


def turn(values, cosine, sine_up, sine_down, sign):
    tiles = []
    for at in range(values.shape[1] // 128):
        tile = values[:, 128 * at : 128 * (at + 1)]
        up = pltpu.roll(tile, 128 - HEAD_DIM // 2, 1)
        down = pltpu.roll(tile, HEAD_DIM // 2, 1)
        tiles.append(tile * cosine + sign * (up * sine_up + down * sine_down))
    return jnp.concatenate(tiles, axis=1)


def layers_kernel(
    tokens, cotangent, lengths, vec,
    w_qkv, w_out, w_gate, w_up, w_down,
    acts, grads_in, out_n2, out_dgu, out_act, out_dmlp, out_left, out_right, out_vec,
    joint, wide, down, vectors, zeros, mask, cosine, sine_up, sine_down,
    xs, n1s, qs, kvs, probs, ctx, hid, n2s, gus, act, ysend,
    sum_first, sum_second, sum_left, sum_right, row_total,
    dys, dmlp, dgu, dn2, dsend, dkvsend, dkvrecv, lefts, rights, vecs, igs,
    send_sems, recv_sems, away_send, away_recv, stay_sems, ring_send, ring_recv, local_sems,
):
    section_at = lax.axis_index("section")
    group_at = lax.axis_index("group")
    replica_at = lax.axis_index("replica")
    x_at, y_at = replica_at // RING, lax.rem(replica_at, RING)
    other = 1 - section_at
    sibling = {"section": other}
    links = Links(ring_send, ring_recv)

    def along_x(spot):
        return {"replica": spot * RING + y_at}

    def along_y(spot):
        return {"replica": x_at * RING + spot}

    def along_z(spot):
        return {"group": spot}

    zeros[...] = jnp.zeros_like(zeros)
    peers = [ring_spot(group_at, step) for step in (1, 2, 3)]
    sources = [ring_spot(group_at, -step) for step in (1, 2, 3)]
    greet(
        [
            ring_spot(x_at, 1) * RING + y_at,
            ring_spot(x_at, -1) * RING + y_at,
            x_at * RING + ring_spot(y_at, 1),
            x_at * RING + ring_spot(y_at, -1),
        ],
        peers,
        [other],
    )
    row_tile = pl.ds(pl.multiple_of(jnp.minimum(replica_at, TILES_R - 1) * 16, 16), 16)
    slots = []
    for which, source in enumerate((w_gate, w_up)):
        target = wide.at[section_at, group_at, x_at, y_at, :, WIN * which : WIN * (which + 1)]
        slots.append((source, target))

    def window(source, spot):
        start = pl.multiple_of((19 * spot) // 2 * 128, 128)
        return source.at[row_tile, pl.ds(start, WIN)]

    slot_sem = links.take(6)
    for step, peer in enumerate(peers):
        for which, (source, target) in enumerate(slots):
            links.send(window(source, peer), target, slot_sem + 2 * step + which, along_z(peer))
    vec_sem = links.take(4)
    for step, peer in enumerate(peers):
        links.send(vec, vectors.at[section_at, group_at], vec_sem + step, along_z(peer))
    shift = lax.rem(group_at, 2) * 64
    body = pl.ds(pl.multiple_of(shift, 64), BLOCK)
    gap = pl.ds(pl.multiple_of(BLOCK - 19 * shift, 64), 64)
    locals_ = []
    for source, target in [
        *[(window(source, group_at), target) for source, target in slots],
        (w_qkv, joint.at[section_at, group_at, :, 0:QKV]),
        (w_out, joint.at[section_at, group_at, :, QKV : QKV + D]),
        (w_down, down.at[section_at, body]),
        (zeros, down.at[0, gap]),
        (zeros, down.at[1, gap]),
        (vec, vectors.at[section_at, group_at]),
    ]:
        copy = pltpu.make_async_copy(source, target, local_sems.at[len(locals_)])
        copy.start()
        locals_.append(copy)
    down_sem = links.take(1)
    links.send(w_down, down.at[section_at, body], down_sem, sibling)

    def joint_block(spot, half):
        return joint.at[section_at, spot, pl.ds(112 * half, 112)]

    def joint_twin(spot, half):
        return joint.at[other, spot, pl.ds(112 * half, 112)]

    joint_share = RingShare(links, group_at, along_z, joint_block, sibling)

    def sharers(which, x_first):
        start = WIN * which

        def small(spot, half):
            cols = pl.ds(start + WIN // 2 * half, WIN // 2)
            if x_first:
                return wide.at[section_at, :, spot, y_at, :, cols]
            return wide.at[section_at, :, x_at, spot, :, cols]

        def big(spot, half, layer=section_at):
            span, cols = pl.ds(2 * half, 2), pl.ds(start, WIN)
            if x_first:
                return wide.at[layer, :, span, spot, :, cols]
            return wide.at[layer, :, spot, span, :, cols]

        one = (x_at, along_x) if x_first else (y_at, along_y)
        two = (y_at, along_y) if x_first else (x_at, along_x)
        stage_two = RingShare(links, *two, big, sibling)
        return RingShare(links, *one, small), stage_two, lambda spot, half: big(spot, half, other)

    gate_one, gate_two, gate_twin = sharers(0, False)
    up_one, up_two, up_twin = sharers(1, True)

    @pl.when(section_at == 0)
    def _():
        locals_[2].wait()
        locals_[3].wait()
        joint_share.start()

    for which, share in ((0, gate_one), (1, up_one)):
        locals_[which].wait()
        for step, spot in enumerate(sources):
            cols = pl.ds(WIN * which, WIN)
            target = wide.at[section_at, spot, x_at, y_at, :, cols]
            links.arrived(target, slot_sem + 2 * step + which, along_z(peers[step]))
        share.start()
    gate_one.middle()
    up_one.middle()
    gate_one.end()
    up_one.end()

    @pl.when(section_at == 0)
    def _():
        gate_two.start()
        up_two.start()

    def starts(spots):
        begin, end = jnp.zeros_like(spots), 0
        for doc in range(lengths.shape[2]):
            length = lengths[section_at, 0, doc]
            end = end + length
            begin = begin + jnp.where(spots >= end, length, 0)
        return begin

    own_spots = lax.broadcasted_iota(jnp.int32, (SPAN, ROW), 0) + group_at * SPAN
    row_spots = lax.broadcasted_iota(jnp.int32, (SPAN, ROW), 1)
    own_begin = starts(own_spots)
    allowed_now = (own_begin == starts(row_spots)) & (row_spots <= own_spots)
    mask[...] = jnp.where(allowed_now, 1.0, 0.0).astype(f32)
    lane = lax.broadcasted_iota(jnp.int32, (SPAN, 128), 1)
    turn_at = lax.rem(lane, HEAD_DIM // 2).astype(f32)
    freqs = jnp.exp(turn_at * (-2.0 / HEAD_DIM * math.log(rope_base)))
    angles = (own_spots - own_begin)[:, :128].astype(f32) * freqs
    sine = jnp.sin(angles)
    cosine[...] = jnp.cos(angles)
    first_half = lax.rem(lane, HEAD_DIM) < HEAD_DIM // 2
    sine_up[...] = jnp.where(first_half, -sine, 0.0)
    sine_down[...] = jnp.where(first_half, 0.0, sine)
    locals_[7].wait()
    for step, spot in enumerate(sources):
        links.arrived(vectors.at[section_at, spot], vec_sem + step, along_z(peers[step]))
    links.send(vectors.at[section_at], vectors.at[section_at], vec_sem + 3, sibling)

    @pl.when(section_at == 0)
    def _():
        joint_share.middle()
        gate_two.middle()
        up_two.middle()
        joint_share.end()

    @pl.when(section_at == 1)
    def _():
        locals_[2].wait()
        locals_[3].wait()
        joint_share.end_twin(joint_twin)

    links.arrived(vectors.at[other], vec_sem + 3, sibling)
    for at in (4, 5, 6):
        locals_[at].wait()

    def while_keys_travel():
        @pl.when(section_at == 0)
        def _():
            gate_two.end()
            up_two.end()

        @pl.when(section_at == 1)
        def _():
            gate_two.start()
            up_two.start()
            joint_share.start()

    def while_rows_travel():
        @pl.when(section_at == 1)
        def _():
            gate_two.middle()
            up_two.middle()
            joint_share.middle()
            gate_two.end_twin(gate_twin)
            up_two.end_twin(up_twin)

        links.arrived(down.at[other, body], down_sem, sibling)

    def while_sums_travel():
        @pl.when(section_at == 1)
        def _():
            joint_share.end()
            gate_two.end()
            up_two.end()

    def late_weights(at):
        @pl.when(section_at == 0)
        def _():
            if at == 0:
                joint_share.end_twin(joint_twin)
            else:
                gate_two.end_twin(gate_twin)
                up_two.end_twin(up_twin)

    def vector_row(layer):
        total = vectors[layer, 0]
        for z in range(1, ZDEV):
            total = total + vectors[layer, z]
        return jnp.concatenate([total[at : at + 1] for at in range(8)], axis=1)

    def exchange(layer, which, source, target):
        copies = []
        for step, peer in enumerate(peers):
            copy = pltpu.make_async_remote_copy(
                src_ref=source(peer),
                dst_ref=target(group_at),
                send_sem=send_sems.at[layer, which, step],
                recv_sem=recv_sems.at[layer, which, step],
                device_id={"group": peer},
                device_id_type=MESH,
            )
            copy.start()
            copies.append(copy)

        def finish():
            for step, peer in enumerate(peers):
                landed = target(ring_spot(group_at, -1 - step))
                pltpu.make_async_remote_copy(
                    src_ref=landed,
                    dst_ref=landed,
                    send_sem=send_sems.at[layer, which, step],
                    recv_sem=recv_sems.at[layer, which, step],
                    device_id={"group": peer},
                    device_id_type=MESH,
                ).wait_recv()
            for copy in copies:
                copy.wait_send()

        return finish

    def wide_cols(layer, start):
        block = wide[layer, :, :, :, :, pl.ds(pl.multiple_of(start, 128), TILE)]
        return block.reshape(ZDEV, REPL, 16, TILE)[:, :TILES_R].reshape(D, TILE)

    def joint_cols(layer, start, stop):
        return joint[layer, :, :, start:stop].reshape(D, stop - start)

    def gathered_sum(own, got):
        total = own[group_at].astype(f32)
        for step in (1, 2, 3):
            total = total + got[ring_spot(group_at, step)].astype(f32)
        return total

    def allowed(count):
        return jnp.concatenate([mask[...]] * count, axis=0) > 0.0

    xs[0] = tokens[section_at]
    bias_at, gain_at, gain_two_at = (0, QKV), (QKV, QKV + D), (QKV + D, QKV + 2 * D)

    def row_share(rows):
        return RingShare(
            links, group_at, along_z, lambda spot, half: rows.at[spot, pl.ds(32 * half, 32)]
        )

    def row_sum(rows, use):
        def pair(buf):
            return lambda half: buf.at[use, pl.ds(32 * half, 32)]

        return RingSum(
            links, group_at, along_z, lambda spot, half: rows.at[spot, pl.ds(32 * half, 32)],
            sum_first.at[use], sum_second.at[use], pair(sum_left), pair(sum_right), add_into,
        )

    def sum_half(half):
        return row_total.at[pl.ds(32 * half, 32)]

    def forward(layer):
        x = xs[layer].astype(f32)
        row = vector_row(layer)
        gain_one = row[:, gain_at[0] : gain_at[1]]
        gain_two = row[:, gain_two_at[0] : gain_two_at[1]]
        n1 = (x * rms_scale(x) * gain_one).astype(bf16)
        n1s[layer] = n1
        if layer == 1:
            late_weights(0)
        qkv = jnp.dot(n1, joint_cols(layer, 0, QKV), preferred_element_type=f32)
        qkv = qkv + row[:, bias_at[0] : bias_at[1]]
        turned = turn(
            qkv[:, : D + KV_WIDTH], cosine[...], sine_up[...], sine_down[...], 1.0
        ).astype(bf16)
        qs[layer] = turned[:, :D]
        kvs[layer, group_at] = jnp.concatenate(
            [turned[:, D:], qkv[:, D + KV_WIDTH :].astype(bf16)], axis=1
        )
        done = exchange(
            layer, 0, lambda peer: kvs.at[layer, group_at], lambda spot: kvs.at[layer, spot]
        )
        if layer == 0:
            while_keys_travel()
        else:
            grads_share.middle()
        done()
        kv = kvs[layer].reshape(ROW, 2 * KV_WIDTH)
        keys, values = spread(kv[:, :KV_WIDTH]), spread(kv[:, KV_WIDTH:])
        outs, at_row = [], 0
        for kind, (pairs, _) in enumerate(KINDS):
            count = SPAN * len(pairs)
            scores = dot_nt(stack_pairs(turned, kind), keys[kind]) * SCALE
            scores = jnp.where(allowed(len(pairs)), scores, -jnp.inf)
            top = jnp.max(scores, axis=-1, keepdims=True)
            raised = jnp.exp(scores - top)
            prob = raised * (1.0 / jnp.sum(raised, axis=-1, keepdims=True))
            probs[layer, at_row : at_row + count] = prob
            outs.append(jnp.dot(prob.astype(bf16), values[kind], preferred_element_type=f32))
            at_row += count
        context = join_pairs(outs).astype(bf16)
        ctx[layer] = context
        hidden = x + jnp.dot(context, joint_cols(layer, QKV, QKV + D), preferred_element_type=f32)
        hid[layer] = hidden
        n2s[layer, group_at] = (hidden * rms_scale(hidden) * gain_two).astype(bf16)
        share = row_share(n2s.at[layer])
        share.start()
        share.middle()
        if layer == 0:
            while_rows_travel()
        else:
            late_weights(1)
        share.end()

        def columns(tile, carry):
            at = tile * TILE
            n2 = n2s[layer].reshape(ROW, D)
            gate = jnp.dot(n2, wide_cols(layer, at), preferred_element_type=f32)
            up = jnp.dot(n2, wide_cols(layer, at + WIN), preferred_element_type=f32)
            gus[layer, 0, :, pl.ds(pl.multiple_of(at, TILE), TILE)] = gate
            gus[layer, 1, :, pl.ds(pl.multiple_of(at, TILE), TILE)] = up
            act[layer, :, pl.ds(pl.multiple_of(at, TILE), TILE)] = (
                gate * jax.nn.sigmoid(gate) * up
            ).astype(bf16)
            return carry

        lax.fori_loop(0, WIN // TILE, columns, 0)
        partial = jnp.dot(act[layer], down[layer], preferred_element_type=f32)
        ysend[layer] = partial.astype(bf16).reshape(ZDEV, SPAN, D)
        adder = row_sum(ysend.at[layer], layer)
        adder.start()
        adder.middle()
        if layer == 0:
            while_sums_travel()
        adder.end(sum_half)
        xs[layer + 1] = (hidden + row_total[...]).astype(bf16)

    forward(0)
    dmlp[1, group_at] = cotangent[section_at]
    grads_share = row_share(dmlp.at[1])
    grads_share.start()
    forward(1)
    grads_share.end()
    dys[...] = cotangent[section_at].astype(f32)

    def hand_over(layer):
        return [
            (xs.at[layer + 1], acts),
            (igs.at[layer], grads_in),
            (n2s.at[layer], out_n2),
            (dgu.at[layer], out_dgu),
            (act.at[layer], out_act),
            (dmlp.at[layer], out_dmlp),
            (lefts.at[layer], out_left),
            (rights.at[layer], out_right),
            (vecs.at[layer], out_vec),
        ]

    def staying(layer):
        return [
            pltpu.make_async_copy(source, target.at[section_at], stay_sems.at[at])
            for at, (source, target) in enumerate(hand_over(layer))
        ]

    def leaving(layer, slot):
        return [
            pltpu.make_async_remote_copy(
                src_ref=source,
                dst_ref=target.at[slot],
                send_sem=away_send.at[at],
                recv_sem=away_recv.at[at],
                device_id={"section": other},
                device_id_type=MESH,
            )
            for at, (source, target) in enumerate(hand_over(layer))
        ]

    def backward(layer):
        row = vector_row(layer)
        gain_one = row[:, gain_at[0] : gain_at[1]]
        gain_two = row[:, gain_two_at[0] : gain_two_at[1]]
        dy = dys[...]
        if layer == 0:
            dmlp[layer, group_at] = dy.astype(bf16)
            share = row_share(dmlp.at[layer])
            share.start()
            share.middle()
            share.end()
        dn2[...] = jnp.zeros_like(dn2)

        def columns(tile, carry):
            at = pl.multiple_of(tile * TILE, TILE)
            grad = dot_nt(dmlp[layer].reshape(ROW, D), down[layer, pl.ds(at, TILE), :])
            gate = gus[layer, 0, :, pl.ds(at, TILE)]
            up = gus[layer, 1, :, pl.ds(at, TILE)]
            sigma = jax.nn.sigmoid(gate)
            grad_gate = (grad * up * sigma * (1.0 + gate * (1.0 - sigma))).astype(bf16)
            grad_up = (grad * gate * sigma).astype(bf16)
            dgu[layer, :, pl.ds(at, TILE)] = grad_gate
            dgu[layer, :, pl.ds(pl.multiple_of(at + WIN, TILE), TILE)] = grad_up
            dn2[...] += dot_nt(grad_gate, wide_cols(layer, at)) + dot_nt(
                grad_up, wide_cols(layer, at + WIN)
            )
            return carry

        lax.fori_loop(0, WIN // TILE, columns, 0)
        dsend[layer] = dn2[...].astype(bf16).reshape(ZDEV, SPAN, D)
        adder = row_sum(dsend.at[layer], 2 + layer)
        adder.start()
        adder.middle()
        adder.end(sum_half)
        grad_two = row_total[...]
        hidden = hid[layer]
        scale = rms_scale(hidden)
        scaled = grad_two * gain_two
        inner = jnp.mean(scaled * hidden, axis=-1, keepdims=True)
        dhid = dy + scale * (scaled - hidden * (scale * scale * inner))
        gain_two_term = jnp.sum(grad_two * hidden * scale, axis=0, keepdims=True)
        dt = dhid.astype(bf16)
        rights[layer, :, QKV:] = dt
        do = dot_nt(dt, joint_cols(layer, QKV, QKV + D)).astype(bf16)
        kv = kvs[layer].reshape(ROW, 2 * KV_WIDTH)
        keys, values = spread(kv[:, :KV_WIDTH]), spread(kv[:, KV_WIDTH:])
        queries = qs[layer]
        dqs, dks, dvs, at_row = [], [], [], 0
        for kind, (pairs, _) in enumerate(KINDS):
            count = SPAN * len(pairs)
            prob = probs[layer, at_row : at_row + count]
            grad = stack_pairs(do, kind)
            dprob = dot_nt(grad, values[kind])
            inner = jnp.sum(prob * dprob, axis=-1, keepdims=True)
            dscore = (prob * (dprob - inner)).astype(bf16)
            dqs.append(jnp.dot(dscore, keys[kind], preferred_element_type=f32))
            dks.append(dot_tn(dscore, stack_pairs(queries, kind)))
            dvs.append(dot_tn(prob.astype(bf16), grad))
            at_row += count
        dkv = jnp.concatenate([unspread(dks) * SCALE, unspread(dvs)], axis=1)
        dkvsend[layer] = dkv.astype(bf16).reshape(ZDEV, SPAN, 2 * KV_WIDTH)
        exchange(
            layer, 5, lambda peer: dkvsend.at[layer, peer], lambda spot: dkvrecv.at[layer, spot]
        )()
        dkv = gathered_sum(dkvsend.at[layer], dkvrecv.at[layer])
        dqk = jnp.concatenate([join_pairs(dqs) * SCALE, dkv[:, :KV_WIDTH]], axis=1)
        dqk = turn(dqk, cosine[...], sine_up[...], sine_down[...], -1.0)
        dqkv = jnp.concatenate([dqk, dkv[:, KV_WIDTH:]], axis=1).astype(bf16)
        rights[layer, :, :QKV] = dqkv
        lefts[layer, :, :D] = n1s[layer]
        lefts[layer, :, D:] = ctx[layer]
        bias_term = jnp.sum(dqkv.astype(f32), axis=0, keepdims=True)
        grad_one = dot_nt(dqkv, joint_cols(layer, 0, QKV))
        x = xs[layer].astype(f32)
        scale = rms_scale(x)
        scaled = grad_one * gain_one
        inner = jnp.mean(scaled * x, axis=-1, keepdims=True)
        dx = dhid + scale * (scaled - x * (scale * scale * inner))
        gain_one_term = jnp.sum(grad_one * x * scale, axis=0, keepdims=True)
        rounded = dx.astype(bf16).astype(f32)
        dys[...] = rounded
        igs[layer] = rounded if layer == 1 else dx
        terms = jnp.concatenate(
            [bias_term, gain_one_term, gain_two_term, jnp.zeros((1, 128), f32)], axis=1
        )
        for at in range(12):
            vecs[layer, at : at + 1, :] = terms[:, 256 * at : 256 * (at + 1)]
        vecs[layer, 12:16, :] = jnp.zeros((4, 256), f32)

        @pl.when(layer == section_at)
        def _():
            for copy in staying(layer):
                copy.start()

        @pl.when(layer != section_at)
        def _():
            for copy in leaving(layer, section_at):
                copy.start()

    backward(1)
    backward(0)
    for copy in staying(section_at):
        copy.wait()
    for copy in leaving(other, section_at):
        copy.wait_send()
    for copy in leaving(other, other):
        copy.wait_recv()
    links.finish()


def run_layers(tokens, cotangent, lengths, vec, *weights):
    vmem = pl.BlockSpec(memory_space=pltpu.VMEM)
    anywhere = pl.BlockSpec(memory_space=pl.ANY)

    def per_micro(shape, kind):
        return jax.ShapeDtypeStruct((2,) + shape, kind)

    sems = 6 + 4 + 1 + 3 * 14 + 2 * 6 + 8 * 6

    def scratch(shape, kind=bf16, lead=2):
        return pltpu.VMEM((lead,) + shape, kind)

    return pl.pallas_call(
        layers_kernel,
        out_shape=(
            per_micro((SPAN, D), bf16),
            per_micro((SPAN, D), f32),
            per_micro((ZDEV, SPAN, D), bf16),
            per_micro((ROW, 2 * WIN), bf16),
            per_micro((ROW, WIN), bf16),
            per_micro((ZDEV, SPAN, D), bf16),
            per_micro((SPAN, 2 * D), bf16),
            per_micro((SPAN, QKV + D), bf16),
            per_micro((16, 256), f32),
        ),
        in_specs=[vmem, vmem, pl.BlockSpec(memory_space=pltpu.SMEM), vmem] + [anywhere] * 5,
        out_specs=[vmem] * 9,
        scratch_shapes=[
            scratch((ZDEV, OWN, QKV + D)),
            scratch((ZDEV, RING, RING, 16, 2 * WIN)),
            scratch((WIN, D)),
            scratch((ZDEV, 8, 384), f32),
            pltpu.VMEM((64, D), bf16),
            pltpu.VMEM((SPAN, ROW), f32),
            pltpu.VMEM((SPAN, 128), f32),
            pltpu.VMEM((SPAN, 128), f32),
            pltpu.VMEM((SPAN, 128), f32),
            scratch((SPAN, D), lead=3),
            scratch((SPAN, D)),
            scratch((SPAN, D)),
            scratch((ZDEV, SPAN, 2 * KV_WIDTH)),
            scratch((HEADS * SPAN, ROW), f32),
            scratch((SPAN, D)),
            scratch((SPAN, D), f32),
            scratch((ZDEV, SPAN, D)),
            scratch((2, ROW, WIN), f32),
            scratch((ROW, WIN)),
            scratch((ZDEV, SPAN, D)),
            scratch((SPAN // 2, D), lead=4),
            scratch((SPAN // 2, D), lead=4),
            scratch((SPAN, D), lead=4),
            scratch((SPAN, D), lead=4),
            pltpu.VMEM((SPAN, D), f32),
            pltpu.VMEM((SPAN, D), f32),
            scratch((ZDEV, SPAN, D)),
            scratch((ROW, 2 * WIN)),
            pltpu.VMEM((ROW, D), f32),
            scratch((ZDEV, SPAN, D)),
            scratch((ZDEV, SPAN, 2 * KV_WIDTH)),
            scratch((ZDEV, SPAN, 2 * KV_WIDTH)),
            scratch((SPAN, 2 * D)),
            scratch((SPAN, QKV + D)),
            scratch((16, 256), f32),
            scratch((SPAN, D), f32),
            pltpu.SemaphoreType.DMA((2, 6, 3)),
            pltpu.SemaphoreType.DMA((2, 6, 3)),
            pltpu.SemaphoreType.DMA((9,)),
            pltpu.SemaphoreType.DMA((9,)),
            pltpu.SemaphoreType.DMA((9,)),
            pltpu.SemaphoreType.DMA((sems,)),
            pltpu.SemaphoreType.DMA((sems,)),
            pltpu.SemaphoreType.DMA((8,)),
        ],
        compiler_params=pltpu.CompilerParams(
            collective_id=3, has_side_effects=True, vmem_limit_bytes=60 * 1024 * 1024
        ),
        name="layers",
    )(tokens, cotangent, lengths, vec, *weights)


def on_device(
    tokens, cotangent, doc_lengths, w_qkv, b_qkv, w_out, w_gate, w_up, w_down, norm_attn, norm_ffn
):
    group_at = lax.axis_index("group")
    vec = jnp.zeros((8 * 384,), f32)
    for member, start in ((b_qkv, 0), (norm_attn, QKV), (norm_ffn, QKV + D)):
        width = member.shape[1]
        vec = lax.dynamic_update_slice(
            vec, member[0].astype(f32), (start + width * group_at,)
        )
    acts, input_grads, *pieces = run_layers(
        tokens[:, 0],
        cotangent[:, 0],
        doc_lengths,
        vec.reshape(8, 384),
        w_qkv[0],
        w_out[0],
        w_gate[0],
        w_up[0],
        w_down[0],
    )
    grads = weight_grads(*pieces)
    return (acts[None, :, None], input_grads[None, :, None]) + tuple(g[None] for g in grads)


def solution(mesh):
    rows = P("section", "group", None)
    vector = P("section", "group")
    spans = P("section", None, "replica", "group", None)
    return jax.shard_map(
        on_device,
        mesh=mesh,
        in_specs=(
            P(None, "replica", "group", None),
            P(None, "replica", "group", None),
            P(None, "replica", None),
            rows,
            vector,
            rows,
            rows,
            rows,
            rows,
            vector,
            vector,
        ),
        out_specs=(spans, spans, rows, vector, rows, rows, rows, rows, vector, vector),
        check_vma=False,
    )
```

```python
import math

import jax
import jax.numpy as jnp
from jax import lax
from jax.experimental import pallas as pl
from jax.experimental.pallas import tpu as pltpu
from jax.sharding import PartitionSpec as P

HEADS = 14
KV_HEADS = 2
HEAD_DIM = 64
GROUPS = HEADS // KV_HEADS
D = 896
FF = 4864
QKV = 1152
SPAN = 64
ROW = 256
REPL = 16
ZDEV = 4
OWN = D // ZDEV
CHUNK = OWN // REPL
BLOCK = FF // ZDEV
WIN = 1280
STARTS = [128 * ((19 * z) // 2) for z in range(ZDEV)]
SHIFTS = [BLOCK * z - STARTS[z] for z in range(ZDEV)]
KV_WIDTH = KV_HEADS * HEAD_DIM

eps = 1e-06
rope_base = 1000000.0
f32 = jnp.float32
bf16 = jnp.bfloat16

def rms_scale(values):
    return lax.rsqrt(jnp.mean(values * values, axis=-1, keepdims=True) + eps)


MESH = pl.DeviceIdType.MESH
TILES_R = OWN // 16
COLS = 15232
PART_A = (0, 7680)
PART_B = (7680, 12928)
PART_C = (12928, 15232)
DOWN_AT = 4 * 2 * WIN
QO_AT = PART_C[0]
VEC_AT = QO_AT + QKV + D
RING = 4


def halves(start, stop):
    middle = start + ((stop - start) // 128 + 1) // 2 * 128
    return ((start, middle), (middle, stop))


def ring_spot(spot, steps):
    return lax.rem(spot + steps + RING, RING)


class Links:
    def __init__(self, send_sems, recv_sems):
        self.send_sems, self.recv_sems, self.used, self.started = send_sems, recv_sems, 0, {}

    def take(self, count):
        first = self.used
        self.used += count
        return first

    def copy(self, source, target, sem_at, device):
        return pltpu.make_async_remote_copy(
            src_ref=source,
            dst_ref=target,
            send_sem=self.send_sems.at[sem_at],
            recv_sem=self.recv_sems.at[sem_at],
            device_id=device,
            device_id_type=MESH,
        )

    def send(self, source, target, sem_at, device):
        copy = self.copy(source, target, sem_at, device)
        copy.start()
        self.started[sem_at] = lambda: copy

    def send_block(self, block, spot, half, sem_at, device):
        def again():
            return self.copy(block(spot, half), block(spot, half), sem_at, device)

        again().start()
        self.started[sem_at] = again

    def arrived(self, target, sem_at, device):
        self.copy(target, target, sem_at, device).wait_recv()

    def finish(self):
        for copy in self.started.values():
            copy().wait_send()
        self.started = {}


class RingSum:
    def __init__(self, links, spot, device_at, block, first, second, left, right, add):
        self.links, self.block, self.add = links, block, add
        self.spots = [ring_spot(spot, steps) for steps in (0, 1, 2, -1)]
        self.right, self.left = device_at(ring_spot(spot, 1)), device_at(ring_spot(spot, -1))
        self.first, self.second, self.from_left, self.from_right = first, second, left, right
        self.sem = links.take(6)

    def start(self):
        send, sem, spots = self.links.send, self.sem, self.spots
        send(self.block(spots[2], 0), self.first, sem, self.right)
        send(self.block(spots[2], 1), self.second, sem + 1, self.left)
        send(self.block(spots[1], 1), self.from_left(1), sem + 2, self.right)
        send(self.block(spots[-1], 0), self.from_right(0), sem + 3, self.left)

    def middle(self):
        links, sem, spots = self.links, self.sem, self.spots
        links.arrived(self.first, sem, self.right)
        onward = self.block(spots[1], 0)
        self.add(onward, onward, self.first)
        links.send(onward, self.from_left(0), sem + 4, self.right)
        links.arrived(self.second, sem + 1, self.left)
        onward = self.block(spots[-1], 1)
        self.add(onward, onward, self.second)
        links.send(onward, self.from_right(1), sem + 5, self.left)

    def end(self, result):
        links, sem, spots = self.links, self.sem, self.spots
        links.arrived(self.from_left(1), sem + 2, self.right)
        links.arrived(self.from_right(0), sem + 3, self.left)
        links.arrived(self.from_left(0), sem + 4, self.right)
        links.arrived(self.from_right(1), sem + 5, self.left)
        for half in (0, 1):
            self.add(
                result(half), self.block(spots[0], half), self.from_left(half), self.from_right(half)
            )


class RingShare:
    def __init__(self, links, spot, device_at, block, sibling=None):
        self.links, self.block, self.sibling = links, block, sibling
        self.spots = [ring_spot(spot, steps) for steps in (0, 1, 2, -1)]
        self.right, self.left = device_at(self.spots[1]), device_at(self.spots[-1])
        self.sem = links.take(6)
        self.twin = links.take(8) if sibling else 0

    def send(self, steps, half, at, device):
        self.links.send_block(self.block, self.spots[steps], half, self.sem + at, device)

    def pass_on(self, steps, half):
        if self.sibling:
            sem = self.twin + 2 * (steps % RING) + half
            self.links.send_block(self.block, self.spots[steps], half, sem, self.sibling)

    def arrived(self, steps, half, at, device, onward=None):
        self.links.arrived(self.block(self.spots[steps], half), self.sem + at, device)
        if onward:
            self.send(steps, half, *onward)
        self.pass_on(steps, half)

    def start(self):
        self.send(0, 0, 0, self.right)
        self.send(0, 1, 2, self.left)
        self.send(0, 1, 1, self.right)
        self.send(0, 0, 3, self.left)
        self.pass_on(0, 0)
        self.pass_on(0, 1)

    def middle(self):
        self.arrived(-1, 0, 0, self.right, (4, self.right))
        self.arrived(1, 1, 2, self.left, (5, self.left))

    def end(self):
        self.arrived(-1, 1, 1, self.right)
        self.arrived(1, 0, 3, self.left)
        self.arrived(2, 0, 4, self.right)
        self.arrived(2, 1, 5, self.left)

    def end_twin(self, twin_block):
        for steps in range(RING):
            for half in (0, 1):
                view = twin_block(self.spots[steps], half)
                self.links.arrived(view, self.twin + 2 * steps + half, self.sibling)


def add_into(target, *sources):
    if len(target.shape) == 3:
        for at in range(target.shape[0]):
            add_into(target.at[at], *[source.at[at] for source in sources])
        return
    total = sources[0][...].astype(f32)
    for source in sources[1:]:
        total = total + source[...].astype(f32)
    target[...] = total.astype(target.dtype)


def greet(replica_spots, group_spots, section_spots=()):
    barrier = pltpu.get_barrier_semaphore()
    spots = {"replica": replica_spots, "group": group_spots, "section": section_spots}
    for axis, members in spots.items():
        for spot in members:
            pl.semaphore_signal(barrier, inc=1, device_id={axis: spot}, device_id_type=MESH)
    pl.semaphore_wait(barrier, sum(map(len, spots.values())))


def grads_kernel(
    n2_rows, dgu, act_rows, dmlp, left_tokens, right_tokens, vecs,
    shared, n2t, act, left_rows, vec, part, own, zbuf, left_all, right_all, vec_all,
    a_first, a_second, a_left, a_right, a_sum, a_first2, a_second2, a_left2, a_right2,
    b_first, b_second, b_left, b_right, b_sum, b_first2, b_second2, b_left2, b_right2,
    c_first, c_second, c_left, c_right, c_sum, c_first2, c_second2, c_left2, c_right2,
    send_sems, recv_sems,
):
    group_at = lax.axis_index("group")
    replica_at = lax.axis_index("replica")
    x_at, y_at = replica_at // RING, lax.rem(replica_at, RING)
    links = Links(send_sems, recv_sems)

    def along_x(spot):
        return {"replica": spot * RING + y_at}

    def along_y(spot):
        return {"replica": x_at * RING + spot}

    peers = [ring_spot(group_at, step) for step in (1, 2, 3)]
    greet(
        [
            ring_spot(x_at, 1) * RING + y_at,
            ring_spot(x_at, -1) * RING + y_at,
            x_at * RING + ring_spot(y_at, 1),
            x_at * RING + ring_spot(y_at, -1),
        ],
        peers,
    )
    right_all[group_at] = right_tokens[...].reshape(2 * SPAN, QKV + D)
    rights_share = RingShare(
        links,
        group_at,
        lambda spot: {"group": spot},
        lambda spot, half: right_all.at[spot, pl.ds(SPAN * half, SPAN)],
    )
    rights_share.start()
    vec[...] = vecs[0] + vecs[1]
    tall = left_tokens[...].reshape(2 * SPAN, 2 * D).T
    for z in range(ZDEV):
        left_rows[z, :OWN] = tall[OWN * z : OWN * (z + 1)]
        left_rows[z, OWN:] = tall[D + OWN * z : D + OWN * (z + 1)]
    tok_sem = links.take(6)
    for step, peer in enumerate(peers):
        for at, (source, target) in enumerate(
            [
                (left_rows.at[peer], left_all.at[group_at]),
                (vec, vec_all.at[group_at]),
            ]
        ):
            links.send(source, target, tok_sem + 2 * step + at, {"group": peer})
    left_all[group_at] = left_rows[group_at]
    vec_all[group_at] = vec[...]

    n2t[...] = n2_rows[...].T

    def gate_up(first, count):
        def columns(tile, carry):
            at = pl.multiple_of(tile * 256, 256)
            block = jnp.dot(
                n2t[OWN * first : OWN * (first + count)],
                dgu[:, pl.ds(at, 256)],
                preferred_element_type=f32,
            ).astype(bf16)
            block = block.reshape(count, TILES_R, 16, 256)
            for z in range(count):
                where = pl.multiple_of(tile * 256 + (first + z) * 2 * WIN, 128)
                for r in range(TILES_R):
                    part[r // RING, r % RING, :, pl.ds(where, 256)] = block[z, r]
            return carry

        lax.fori_loop(0, 2 * WIN // 256, columns, 0)

    act[...] = act_rows[...].T
    def summers(cols, x_first, bufs):
        first, second, left, right, total, first2, second2, left2, right2 = bufs
        start, stop = cols

        def big(spot, half):
            span = pl.ds(2 * half, 2)
            if x_first:
                return part.at[spot, span, :, start:stop]
            return part.at[span, spot, :, start:stop]

        cuts = halves(0, stop - start)

        def small(spot, half):
            return total.at[spot, :, cuts[half][0] : cuts[half][1]]

        def pair(buf):
            return lambda half: buf.at[pl.ds(2 * half, 2)]

        def cut(buf):
            return lambda half: buf.at[:, cuts[half][0] : cuts[half][1]]

        one = (x_at, along_x) if x_first else (y_at, along_y)
        two = (y_at, along_y) if x_first else (x_at, along_x)
        stage_one = RingSum(
            links, *one, big, first, second, pair(left), pair(right), add_into
        )
        stage_two = RingSum(
            links, *two, small, first2, second2, cut(left2), cut(right2), add_into
        )

        def result(half):
            return own.at[:, start + cuts[half][0] : start + cuts[half][1]]

        return stage_one, stage_two, pair(total), result

    a_one, a_two, a_mid, a_result = summers(
        PART_A, True,
        (a_first, a_second, a_left, a_right, a_sum, a_first2, a_second2, a_left2, a_right2),
    )
    b_one, b_two, b_mid, b_result = summers(
        PART_B, False,
        (b_first, b_second, b_left, b_right, b_sum, b_first2, b_second2, b_left2, b_right2),
    )
    c_one, c_two, c_mid, c_result = summers(
        PART_C, False,
        (c_first, c_second, c_left, c_right, c_sum, c_first2, c_second2, c_left2, c_right2),
    )
    shift = lax.rem(group_at, 2) * 64
    for quarter in range(4):
        rows = pl.ds(pl.multiple_of(shift + 304 * quarter, 16), 304)
        block = jnp.dot(act[rows, :], dmlp[...], preferred_element_type=f32).astype(bf16)
        block = block.reshape(19, 16, D)
        for inner in range(19):
            tile = 19 * quarter + inner
            if tile < 3 * TILES_R:
                r, at = tile // 3, DOWN_AT + D * (tile % 3)
            else:
                r, at = TILES_R + (tile - 3 * TILES_R) // 17, D * ((tile - 3 * TILES_R) % 17)
            part[r // RING, r % RING, :, at : at + D] = block[inner]
    rights_share.middle()
    gate_up(0, 3)
    a_one.start()
    gate_up(3, 1)
    b_one.start()
    a_one.middle()
    b_one.middle()
    for step, peer in enumerate(peers):
        source = ring_spot(group_at, -1 - step)
        for at, target in enumerate((left_all, vec_all)):
            links.arrived(target.at[source], tok_sem + 2 * step + at, {"group": peer})
    rights_share.end()
    for width, col, row in ((QKV, 0, 0), (D, QKV, OWN)):
        total = jnp.dot(
            left_all[0, row : row + OWN], right_all[0, :, col : col + width],
            preferred_element_type=f32,
        )
        for z in range(1, ZDEV):
            total = total + jnp.dot(
                left_all[z, row : row + OWN], right_all[z, :, col : col + width],
                preferred_element_type=f32,
            )
        total = total.astype(bf16).reshape(TILES_R, 16, width)
        for r in range(TILES_R):
            part[r // RING, r % RING, :, QO_AT + col : QO_AT + col + width] = total[r]
    part[0, 0, :, VEC_AT:COLS] = (
        vec_all[0] + vec_all[1] + vec_all[2] + vec_all[3]
    ).astype(bf16)
    for r in range(1, TILES_R):
        part[r // RING, r % RING, :, VEC_AT:COLS] = jnp.zeros((16, COLS - VEC_AT), bf16)
    c_one.start()
    a_one.end(a_mid)
    a_two.start()
    b_one.end(b_mid)
    b_two.start()
    c_one.middle()
    a_two.middle()
    b_two.middle()
    c_one.end(c_mid)
    c_two.start()
    a_two.end(a_result)
    b_two.end(b_result)
    slot_sem = links.take(3)
    for step, peer in enumerate(peers):
        where = pl.multiple_of(peer * 2 * WIN, 128)
        links.send(
            own.at[:, pl.ds(where, 2 * WIN)], zbuf.at[group_at], slot_sem + step, {"group": peer}
        )
    where = pl.multiple_of(group_at * 2 * WIN, 128)
    zbuf[group_at] = own[:, pl.ds(where, 2 * WIN)]
    c_two.middle()
    c_two.end(c_result)
    for step, peer in enumerate(peers):
        links.arrived(zbuf.at[ring_spot(group_at, -1 - step)], slot_sem + step, {"group": peer})

    @pl.when(replica_at < TILES_R)
    def _():
        for which in (0, 1):
            base, at = which * FF, which * WIN
            for z in range(ZDEV):
                low = 128 if z % 2 else 0
                high = WIN if z % 2 else WIN - 128
                to = base + STARTS[z]
                shared[x_at, y_at, :, to + low : to + high] = zbuf[z, :, at + low : at + high]
            for z in (0, 2):
                to = base + STARTS[z + 1]
                shared[x_at, y_at, :, to : to + 128] = (
                    zbuf[z, :, at + WIN - 128 : at + WIN] + zbuf[z + 1, :, at : at + 128]
                )
        shared[x_at, y_at, :, 2 * FF : 2 * FF + 512] = jnp.zeros((16, 512), bf16)
        shared[x_at, y_at, :, DOWN_AT:COLS] = own[:, DOWN_AT:COLS]

    @pl.when(replica_at >= TILES_R)
    def _():
        shared[x_at, y_at] = own[...]

    def sharers(cols, x_first):
        start, stop = cols
        cuts = halves(start, stop)

        def small(spot, half):
            low, high = cuts[half]
            if x_first:
                return shared.at[spot, y_at, :, low:high]
            return shared.at[x_at, spot, :, low:high]

        def big(spot, half):
            span = pl.ds(2 * half, 2)
            if x_first:
                return shared.at[span, spot, :, start:stop]
            return shared.at[spot, span, :, start:stop]

        one = (x_at, along_x) if x_first else (y_at, along_y)
        two = (y_at, along_y) if x_first else (x_at, along_x)
        return RingShare(links, *one, small), RingShare(links, *two, big)

    a_one, a_two = sharers((0, 7680), False)
    b_one, b_two = sharers((7680, COLS), True)
    a_one.start()
    b_one.start()
    a_one.middle()
    b_one.middle()
    a_one.end()
    a_two.start()
    b_one.end()
    b_two.start()
    a_two.middle()
    b_two.middle()
    a_two.end()
    b_two.end()
    links.finish()


def share_grads(n2, dgu, act, dmlp, lefts, rights, vecs):
    def bufs(cols):
        width = cols[1] - cols[0]
        low, high = [b - a for a, b in halves(0, width)]
        shapes = [(2, 16, width), (2, 16, width), (4, 16, width), (4, 16, width), (4, 16, width)]
        shapes = shapes + [(16, low), (16, high), (16, width), (16, width)]
        return [pltpu.VMEM(shape, bf16) for shape in shapes]

    vmem = pl.BlockSpec(memory_space=pltpu.VMEM)
    sems = 6 + 6 + 3 + 6 * 6 + 4 * 6
    return pl.pallas_call(
        grads_kernel,
        out_shape=jax.ShapeDtypeStruct((RING, RING, 16, COLS), bf16),
        in_specs=[vmem] * 7,
        out_specs=vmem,
        scratch_shapes=[
            pltpu.VMEM((D, 2 * ROW), bf16),
            pltpu.VMEM((WIN, 2 * ROW), bf16),
            pltpu.VMEM((ZDEV, 2 * OWN, 2 * SPAN), bf16),
            pltpu.VMEM((16, 256), f32),
            pltpu.VMEM((RING, RING, 16, COLS), bf16),
            pltpu.VMEM((16, COLS), bf16),
            pltpu.VMEM((ZDEV, 16, 2 * WIN), bf16),
            pltpu.VMEM((ZDEV, 2 * OWN, 2 * SPAN), bf16),
            pltpu.VMEM((ZDEV, 2 * SPAN, QKV + D), bf16),
            pltpu.VMEM((ZDEV, 16, 256), f32),
            *bufs(PART_A),
            *bufs(PART_B),
            *bufs(PART_C),
            pltpu.SemaphoreType.DMA((sems,)),
            pltpu.SemaphoreType.DMA((sems,)),
        ],
        compiler_params=pltpu.CompilerParams(
            collective_id=1, has_side_effects=True, vmem_limit_bytes=58 * 1024 * 1024
        ),
        name="grads",
    )(n2, dgu, act, dmlp, lefts, rights, vecs)


def widen_kernel(block, rest, gate, up, qkv, out, down):
    at = pl.program_id(0)
    for inner in range(2):
        rows = pl.ds(16 * inner, 16)
        for target, start, width in (
            (gate, 0, FF), (up, FF, FF), (qkv, QO_AT, QKV), (out, QO_AT + QKV, D),
        ):
            target[rows, :] = block[inner, :, start : start + width].astype(f32)
        for place in range(3):
            tile = pl.multiple_of((6 * at + 3 * inner + place) * 16, 16)
            start = DOWN_AT + D * place
            down[pl.ds(tile, 16), :] = block[inner, :, start : start + D].astype(f32)
    for tile in range(34):

        @pl.when(at == tile // 5)
        def _():
            rows = pl.ds((3 * TILES_R + tile) * 16, 16)
            start = D * (tile % 17)
            down[rows, :] = rest[tile // 17, :, start : start + D].astype(f32)


def widen(shared):
    rows = [FF, FF, QKV, D]
    return pl.pallas_call(
        widen_kernel,
        grid=(TILES_R // 2,),
        out_shape=[jax.ShapeDtypeStruct((OWN, width), f32) for width in rows]
        + [jax.ShapeDtypeStruct((BLOCK, D), f32)],
        in_specs=[
            pl.BlockSpec((2, 16, COLS), lambda at: (at, 0, 0)),
            pl.BlockSpec((2, 16, COLS), lambda at: (TILES_R // 2, 0, 0)),
        ],
        out_specs=[pl.BlockSpec((32, width), lambda at: (at, 0)) for width in rows]
        + [pl.BlockSpec((BLOCK, D), lambda at: (0, 0))],
        compiler_params=pltpu.CompilerParams(vmem_limit_bytes=40 * 1024 * 1024),
        name="widen",
    )(shared, shared)


def weight_grads(n2, dgu, act, dmlp, lefts, rights, vecs):
    group_at = lax.axis_index("group")
    shared = share_grads(
        n2.reshape(2 * ROW, D),
        dgu.reshape(2 * ROW, 2 * WIN),
        act.reshape(2 * ROW, WIN),
        dmlp.reshape(2 * ROW, D),
        lefts,
        rights,
        vecs,
    )
    shared = shared.reshape(REPL, 16, COLS)
    grad_gate, grad_up, grad_qkv, grad_out, grad_down = widen(shared)
    vec = shared[0, :, VEC_AT:].reshape(16 * 256).astype(f32)

    def own_part(start, width):
        return lax.dynamic_slice_in_dim(vec, start + group_at * width, width, 0)

    return (
        grad_qkv,
        own_part(0, QKV // ZDEV),
        grad_out,
        grad_gate,
        grad_up,
        grad_down,
        own_part(QKV, OWN),
        own_part(QKV + D, OWN),
    )


PAIRS = HEADS // 2
KINDS = (((0, 1, 2, 3), 0), ((0, 1, 2), 1), ((4, 5, 6), 2), ((3, 4, 5, 6), 3))
SCALE = HEAD_DIM ** (-0.5)
TILE = 256


def dot_nt(left, right):
    return lax.dot_general(left, right, (((1,), (1,)), ((), ())), preferred_element_type=f32)


def dot_tn(left, right):
    return lax.dot_general(left, right, (((0,), (0,)), ((), ())), preferred_element_type=f32)


def spread(pair):
    low = lax.broadcasted_iota(jnp.int32, pair.shape, 1) < HEAD_DIM
    wide = pair.astype(f32)
    turned = pltpu.roll(wide, HEAD_DIM, 1)
    zero = jnp.zeros_like(wide)
    members = (
        jnp.where(low, wide, zero),
        jnp.where(low, zero, turned),
        jnp.where(low, turned, zero),
        jnp.where(low, zero, wide),
    )
    return [member.astype(bf16) for member in members]


def unspread(kinds):
    low = lax.broadcasted_iota(jnp.int32, kinds[0].shape, 1) < HEAD_DIM
    straight = jnp.where(low, kinds[0], kinds[3])
    crossed = jnp.where(low, kinds[2], kinds[1])
    return straight + pltpu.roll(crossed, HEAD_DIM, 1)


def stack_pairs(tokens, kind):
    return jnp.concatenate(
        [tokens[:, 2 * HEAD_DIM * p : 2 * HEAD_DIM * (p + 1)] for p in KINDS[kind][0]], axis=0
    )


def join_pairs(kinds):
    found = [None] * PAIRS
    for kind, (pairs, _) in enumerate(KINDS):
        for at, p in enumerate(pairs):
            part = kinds[kind][SPAN * at : SPAN * (at + 1)]
            found[p] = part if found[p] is None else found[p] + part
    return jnp.concatenate(found, axis=1)


def turn(values, cosine, sine_up, sine_down, sign):
    tiles = []
    for at in range(values.shape[1] // 128):
        tile = values[:, 128 * at : 128 * (at + 1)]
        up = pltpu.roll(tile, 128 - HEAD_DIM // 2, 1)
        down = pltpu.roll(tile, HEAD_DIM // 2, 1)
        tiles.append(tile * cosine + sign * (up * sine_up + down * sine_down))
    return jnp.concatenate(tiles, axis=1)


def layers_kernel(
    tokens, cotangent, lengths, vec,
    w_qkv, w_out, w_gate, w_up, w_down,
    acts, grads_in, out_n2, out_dgu, out_act, out_dmlp, out_left, out_right, out_vec,
    joint, wide, down, vectors, zeros, mask, cosine, sine_up, sine_down,
    xs, n1s, qs, kvs, probs, ctx, hid, n2s, gus, act, ysend,
    sum_first, sum_second, sum_left, sum_right, row_total,
    dys, dmlp, dgu, dn2, dsend, dkvsend, dkvrecv, lefts, rights, vecs, igs,
    send_sems, recv_sems, away_send, away_recv, stay_sems, ring_send, ring_recv, local_sems,
):
    section_at = lax.axis_index("section")
    group_at = lax.axis_index("group")
    replica_at = lax.axis_index("replica")
    x_at, y_at = replica_at // RING, lax.rem(replica_at, RING)
    other = 1 - section_at
    sibling = {"section": other}
    links = Links(ring_send, ring_recv)

    def along_x(spot):
        return {"replica": spot * RING + y_at}

    def along_y(spot):
        return {"replica": x_at * RING + spot}

    def along_z(spot):
        return {"group": spot}

    zeros[...] = jnp.zeros_like(zeros)
    peers = [ring_spot(group_at, step) for step in (1, 2, 3)]
    sources = [ring_spot(group_at, -step) for step in (1, 2, 3)]
    greet(
        [
            ring_spot(x_at, 1) * RING + y_at,
            ring_spot(x_at, -1) * RING + y_at,
            x_at * RING + ring_spot(y_at, 1),
            x_at * RING + ring_spot(y_at, -1),
        ],
        peers,
        [other],
    )
    row_tile = pl.ds(pl.multiple_of(jnp.minimum(replica_at, TILES_R - 1) * 16, 16), 16)
    slots = []
    for which, source in enumerate((w_gate, w_up)):
        target = wide.at[section_at, group_at, x_at, y_at, :, WIN * which : WIN * (which + 1)]
        slots.append((source, target))

    def window(source, spot):
        start = pl.multiple_of((19 * spot) // 2 * 128, 128)
        return source.at[row_tile, pl.ds(start, WIN)]

    slot_sem = links.take(6)
    for step, peer in enumerate(peers):
        for which, (source, target) in enumerate(slots):
            links.send(window(source, peer), target, slot_sem + 2 * step + which, along_z(peer))
    vec_sem = links.take(4)
    for step, peer in enumerate(peers):
        links.send(vec, vectors.at[section_at, group_at], vec_sem + step, along_z(peer))
    shift = lax.rem(group_at, 2) * 64
    body = pl.ds(pl.multiple_of(shift, 64), BLOCK)
    gap = pl.ds(pl.multiple_of(BLOCK - 19 * shift, 64), 64)
    locals_ = []
    for source, target in [
        *[(window(source, group_at), target) for source, target in slots],
        (w_qkv, joint.at[section_at, group_at, :, 0:QKV]),
        (w_out, joint.at[section_at, group_at, :, QKV : QKV + D]),
        (w_down, down.at[section_at, body]),
        (zeros, down.at[0, gap]),
        (zeros, down.at[1, gap]),
        (vec, vectors.at[section_at, group_at]),
    ]:
        copy = pltpu.make_async_copy(source, target, local_sems.at[len(locals_)])
        copy.start()
        locals_.append(copy)
    down_sem = links.take(1)
    links.send(w_down, down.at[section_at, body], down_sem, sibling)

    def joint_block(spot, half):
        return joint.at[section_at, spot, pl.ds(112 * half, 112)]

    def joint_twin(spot, half):
        return joint.at[other, spot, pl.ds(112 * half, 112)]

    joint_share = RingShare(links, group_at, along_z, joint_block, sibling)

    def sharers(which, x_first):
        start = WIN * which

        def small(spot, half):
            cols = pl.ds(start + WIN // 2 * half, WIN // 2)
            if x_first:
                return wide.at[section_at, :, spot, y_at, :, cols]
            return wide.at[section_at, :, x_at, spot, :, cols]

        def big(spot, half, layer=section_at):
            span, cols = pl.ds(2 * half, 2), pl.ds(start, WIN)
            if x_first:
                return wide.at[layer, :, span, spot, :, cols]
            return wide.at[layer, :, spot, span, :, cols]

        one = (x_at, along_x) if x_first else (y_at, along_y)
        two = (y_at, along_y) if x_first else (x_at, along_x)
        stage_two = RingShare(links, *two, big, sibling)
        return RingShare(links, *one, small), stage_two, lambda spot, half: big(spot, half, other)

    gate_one, gate_two, gate_twin = sharers(0, False)
    up_one, up_two, up_twin = sharers(1, True)

    @pl.when(section_at == 0)
    def _():
        locals_[2].wait()
        locals_[3].wait()
        joint_share.start()

    for which, share in ((0, gate_one), (1, up_one)):
        locals_[which].wait()
        for step, spot in enumerate(sources):
            cols = pl.ds(WIN * which, WIN)
            target = wide.at[section_at, spot, x_at, y_at, :, cols]
            links.arrived(target, slot_sem + 2 * step + which, along_z(peers[step]))
        share.start()
    gate_one.middle()
    up_one.middle()
    gate_one.end()
    up_one.end()

    @pl.when(section_at == 0)
    def _():
        gate_two.start()
        up_two.start()

    def starts(spots):
        begin, end = jnp.zeros_like(spots), 0
        for doc in range(lengths.shape[2]):
            length = lengths[section_at, 0, doc]
            end = end + length
            begin = begin + jnp.where(spots >= end, length, 0)
        return begin

    own_spots = lax.broadcasted_iota(jnp.int32, (SPAN, ROW), 0) + group_at * SPAN
    row_spots = lax.broadcasted_iota(jnp.int32, (SPAN, ROW), 1)
    own_begin = starts(own_spots)
    allowed_now = (own_begin == starts(row_spots)) & (row_spots <= own_spots)
    mask[...] = jnp.where(allowed_now, 1.0, 0.0).astype(f32)
    lane = lax.broadcasted_iota(jnp.int32, (SPAN, 128), 1)
    turn_at = lax.rem(lane, HEAD_DIM // 2).astype(f32)
    freqs = jnp.exp(turn_at * (-2.0 / HEAD_DIM * math.log(rope_base)))
    angles = (own_spots - own_begin)[:, :128].astype(f32) * freqs
    sine = jnp.sin(angles)
    cosine[...] = jnp.cos(angles)
    first_half = lax.rem(lane, HEAD_DIM) < HEAD_DIM // 2
    sine_up[...] = jnp.where(first_half, -sine, 0.0)
    sine_down[...] = jnp.where(first_half, 0.0, sine)
    locals_[7].wait()
    for step, spot in enumerate(sources):
        links.arrived(vectors.at[section_at, spot], vec_sem + step, along_z(peers[step]))
    links.send(vectors.at[section_at], vectors.at[section_at], vec_sem + 3, sibling)

    @pl.when(section_at == 0)
    def _():
        joint_share.middle()
        gate_two.middle()
        up_two.middle()
        joint_share.end()

    @pl.when(section_at == 1)
    def _():
        locals_[2].wait()
        locals_[3].wait()
        joint_share.end_twin(joint_twin)

    links.arrived(vectors.at[other], vec_sem + 3, sibling)
    for at in (4, 5, 6):
        locals_[at].wait()

    def while_keys_travel():
        @pl.when(section_at == 0)
        def _():
            gate_two.end()
            up_two.end()

        @pl.when(section_at == 1)
        def _():
            gate_two.start()
            up_two.start()
            joint_share.start()

    def while_rows_travel():
        @pl.when(section_at == 1)
        def _():
            gate_two.middle()
            up_two.middle()
            joint_share.middle()
            gate_two.end_twin(gate_twin)
            up_two.end_twin(up_twin)

        links.arrived(down.at[other, body], down_sem, sibling)

    def while_sums_travel():
        @pl.when(section_at == 1)
        def _():
            joint_share.end()
            gate_two.end()
            up_two.end()

    def late_weights(at):
        @pl.when(section_at == 0)
        def _():
            if at == 0:
                joint_share.end_twin(joint_twin)
            else:
                gate_two.end_twin(gate_twin)
                up_two.end_twin(up_twin)

    def vector_row(layer):
        total = vectors[layer, 0]
        for z in range(1, ZDEV):
            total = total + vectors[layer, z]
        return jnp.concatenate([total[at : at + 1] for at in range(8)], axis=1)

    def exchange(layer, which, source, target):
        copies = []
        for step, peer in enumerate(peers):
            copy = pltpu.make_async_remote_copy(
                src_ref=source(peer),
                dst_ref=target(group_at),
                send_sem=send_sems.at[layer, which, step],
                recv_sem=recv_sems.at[layer, which, step],
                device_id={"group": peer},
                device_id_type=MESH,
            )
            copy.start()
            copies.append(copy)

        def finish():
            for step, peer in enumerate(peers):
                landed = target(ring_spot(group_at, -1 - step))
                pltpu.make_async_remote_copy(
                    src_ref=landed,
                    dst_ref=landed,
                    send_sem=send_sems.at[layer, which, step],
                    recv_sem=recv_sems.at[layer, which, step],
                    device_id={"group": peer},
                    device_id_type=MESH,
                ).wait_recv()
            for copy in copies:
                copy.wait_send()

        return finish

    def wide_cols(layer, start):
        block = wide[layer, :, :, :, :, pl.ds(pl.multiple_of(start, 128), TILE)]
        return block.reshape(ZDEV, REPL, 16, TILE)[:, :TILES_R].reshape(D, TILE)

    def joint_cols(layer, start, stop):
        return joint[layer, :, :, start:stop].reshape(D, stop - start)

    def gathered_sum(own, got):
        total = own[group_at].astype(f32)
        for step in (1, 2, 3):
            total = total + got[ring_spot(group_at, step)].astype(f32)
        return total

    def allowed(count):
        return jnp.concatenate([mask[...]] * count, axis=0) > 0.0

    xs[0] = tokens[section_at]
    bias_at, gain_at, gain_two_at = (0, QKV), (QKV, QKV + D), (QKV + D, QKV + 2 * D)

    def row_share(rows):
        return RingShare(
            links, group_at, along_z, lambda spot, half: rows.at[spot, pl.ds(32 * half, 32)]
        )

    def row_sum(rows, use):
        def pair(buf):
            return lambda half: buf.at[use, pl.ds(32 * half, 32)]

        return RingSum(
            links, group_at, along_z, lambda spot, half: rows.at[spot, pl.ds(32 * half, 32)],
            sum_first.at[use], sum_second.at[use], pair(sum_left), pair(sum_right), add_into,
        )

    def sum_half(half):
        return row_total.at[pl.ds(32 * half, 32)]

    def forward(layer):
        x = xs[layer].astype(f32)
        row = vector_row(layer)
        gain_one = row[:, gain_at[0] : gain_at[1]]
        gain_two = row[:, gain_two_at[0] : gain_two_at[1]]
        n1 = (x * rms_scale(x) * gain_one).astype(bf16)
        n1s[layer] = n1
        if layer == 1:
            late_weights(0)
        qkv = jnp.dot(n1, joint_cols(layer, 0, QKV), preferred_element_type=f32)
        qkv = qkv + row[:, bias_at[0] : bias_at[1]]
        turned = turn(
            qkv[:, : D + KV_WIDTH], cosine[...], sine_up[...], sine_down[...], 1.0
        ).astype(bf16)
        qs[layer] = turned[:, :D]
        kvs[layer, group_at] = jnp.concatenate(
            [turned[:, D:], qkv[:, D + KV_WIDTH :].astype(bf16)], axis=1
        )
        done = exchange(
            layer, 0, lambda peer: kvs.at[layer, group_at], lambda spot: kvs.at[layer, spot]
        )
        if layer == 0:
            while_keys_travel()
        else:
            grads_share.middle()
        done()
        kv = kvs[layer].reshape(ROW, 2 * KV_WIDTH)
        keys, values = spread(kv[:, :KV_WIDTH]), spread(kv[:, KV_WIDTH:])
        outs, at_row = [], 0
        for kind, (pairs, _) in enumerate(KINDS):
            count = SPAN * len(pairs)
            scores = dot_nt(stack_pairs(turned, kind), keys[kind]) * SCALE
            scores = jnp.where(allowed(len(pairs)), scores, -jnp.inf)
            top = jnp.max(scores, axis=-1, keepdims=True)
            raised = jnp.exp(scores - top)
            prob = raised * (1.0 / jnp.sum(raised, axis=-1, keepdims=True))
            probs[layer, at_row : at_row + count] = prob
            outs.append(jnp.dot(prob.astype(bf16), values[kind], preferred_element_type=f32))
            at_row += count
        context = join_pairs(outs).astype(bf16)
        ctx[layer] = context
        hidden = x + jnp.dot(context, joint_cols(layer, QKV, QKV + D), preferred_element_type=f32)
        hid[layer] = hidden
        n2s[layer, group_at] = (hidden * rms_scale(hidden) * gain_two).astype(bf16)
        share = row_share(n2s.at[layer])
        share.start()
        share.middle()
        if layer == 0:
            while_rows_travel()
        else:
            late_weights(1)
        share.end()

        def columns(tile, carry):
            at = tile * TILE
            n2 = n2s[layer].reshape(ROW, D)
            gate = jnp.dot(n2, wide_cols(layer, at), preferred_element_type=f32)
            up = jnp.dot(n2, wide_cols(layer, at + WIN), preferred_element_type=f32)
            gus[layer, 0, :, pl.ds(pl.multiple_of(at, TILE), TILE)] = gate
            gus[layer, 1, :, pl.ds(pl.multiple_of(at, TILE), TILE)] = up
            act[layer, :, pl.ds(pl.multiple_of(at, TILE), TILE)] = (
                gate * jax.nn.sigmoid(gate) * up
            ).astype(bf16)
            return carry

        lax.fori_loop(0, WIN // TILE, columns, 0)
        partial = jnp.dot(act[layer], down[layer], preferred_element_type=f32)
        ysend[layer] = partial.astype(bf16).reshape(ZDEV, SPAN, D)
        adder = row_sum(ysend.at[layer], layer)
        adder.start()
        adder.middle()
        if layer == 0:
            while_sums_travel()
        adder.end(sum_half)
        xs[layer + 1] = (hidden + row_total[...]).astype(bf16)

    forward(0)
    dmlp[1, group_at] = cotangent[section_at]
    grads_share = row_share(dmlp.at[1])
    grads_share.start()
    forward(1)
    grads_share.end()
    dys[...] = cotangent[section_at].astype(f32)

    def hand_over(layer):
        return [
            (xs.at[layer + 1], acts),
            (igs.at[layer], grads_in),
            (n2s.at[layer], out_n2),
            (dgu.at[layer], out_dgu),
            (act.at[layer], out_act),
            (dmlp.at[layer], out_dmlp),
            (lefts.at[layer], out_left),
            (rights.at[layer], out_right),
            (vecs.at[layer], out_vec),
        ]

    def staying(layer):
        return [
            pltpu.make_async_copy(source, target.at[section_at], stay_sems.at[at])
            for at, (source, target) in enumerate(hand_over(layer))
        ]

    def leaving(layer, slot):
        return [
            pltpu.make_async_remote_copy(
                src_ref=source,
                dst_ref=target.at[slot],
                send_sem=away_send.at[at],
                recv_sem=away_recv.at[at],
                device_id={"section": other},
                device_id_type=MESH,
            )
            for at, (source, target) in enumerate(hand_over(layer))
        ]

    def backward(layer):
        row = vector_row(layer)
        gain_one = row[:, gain_at[0] : gain_at[1]]
        gain_two = row[:, gain_two_at[0] : gain_two_at[1]]
        dy = dys[...]
        if layer == 0:
            dmlp[layer, group_at] = dy.astype(bf16)
            share = row_share(dmlp.at[layer])
            share.start()
            share.middle()
            share.end()
        dn2[...] = jnp.zeros_like(dn2)

        def columns(tile, carry):
            at = pl.multiple_of(tile * TILE, TILE)
            grad = dot_nt(dmlp[layer].reshape(ROW, D), down[layer, pl.ds(at, TILE), :])
            gate = gus[layer, 0, :, pl.ds(at, TILE)]
            up = gus[layer, 1, :, pl.ds(at, TILE)]
            sigma = jax.nn.sigmoid(gate)
            grad_gate = (grad * up * sigma * (1.0 + gate * (1.0 - sigma))).astype(bf16)
            grad_up = (grad * gate * sigma).astype(bf16)
            dgu[layer, :, pl.ds(at, TILE)] = grad_gate
            dgu[layer, :, pl.ds(pl.multiple_of(at + WIN, TILE), TILE)] = grad_up
            dn2[...] += dot_nt(grad_gate, wide_cols(layer, at)) + dot_nt(
                grad_up, wide_cols(layer, at + WIN)
            )
            return carry

        lax.fori_loop(0, WIN // TILE, columns, 0)
        dsend[layer] = dn2[...].astype(bf16).reshape(ZDEV, SPAN, D)
        adder = row_sum(dsend.at[layer], 2 + layer)
        adder.start()
        adder.middle()
        kv = kvs[layer].reshape(ROW, 2 * KV_WIDTH)
        keys, values = spread(kv[:, :KV_WIDTH]), spread(kv[:, KV_WIDTH:])
        adder.end(sum_half)
        grad_two = row_total[...]
        hidden = hid[layer]
        scale = rms_scale(hidden)
        scaled = grad_two * gain_two
        inner = jnp.mean(scaled * hidden, axis=-1, keepdims=True)
        dhid = dy + scale * (scaled - hidden * (scale * scale * inner))
        gain_two_term = jnp.sum(grad_two * hidden * scale, axis=0, keepdims=True)
        dt = dhid.astype(bf16)
        rights[layer, :, QKV:] = dt
        do = dot_nt(dt, joint_cols(layer, QKV, QKV + D)).astype(bf16)
        queries = qs[layer]
        dscores, dks, dvs, at_row = [], [], [], 0
        for kind, (pairs, _) in enumerate(KINDS):
            count = SPAN * len(pairs)
            prob = probs[layer, at_row : at_row + count]
            grad = stack_pairs(do, kind)
            dprob = dot_nt(grad, values[kind])
            inner = jnp.sum(prob * dprob, axis=-1, keepdims=True)
            dscore = (prob * (dprob - inner)).astype(bf16)
            dscores.append(dscore)
            dks.append(dot_tn(dscore, stack_pairs(queries, kind)))
            dvs.append(dot_tn(prob.astype(bf16), grad))
            at_row += count
        dkv = jnp.concatenate([unspread(dks) * SCALE, unspread(dvs)], axis=1)
        dkvsend[layer] = dkv.astype(bf16).reshape(ZDEV, SPAN, 2 * KV_WIDTH)
        done = exchange(
            layer, 5, lambda peer: dkvsend.at[layer, peer], lambda spot: dkvrecv.at[layer, spot]
        )
        dqs = [
            jnp.dot(dscore, member, preferred_element_type=f32)
            for dscore, member in zip(dscores, keys)
        ]
        dq = turn(join_pairs(dqs) * SCALE, cosine[...], sine_up[...], sine_down[...], -1.0)
        dq = dq.astype(bf16)
        rights[layer, :, :D] = dq
        lefts[layer, :, :D] = n1s[layer]
        lefts[layer, :, D:] = ctx[layer]
        grad_one = dot_nt(dq, joint_cols(layer, 0, D))
        done()
        dkv = gathered_sum(dkvsend.at[layer], dkvrecv.at[layer])
        dk = turn(dkv[:, :KV_WIDTH], cosine[...], sine_up[...], sine_down[...], -1.0)
        dkv = jnp.concatenate([dk, dkv[:, KV_WIDTH:]], axis=1).astype(bf16)
        rights[layer, :, D:QKV] = dkv
        grad_one = grad_one + dot_nt(dkv, joint_cols(layer, D, QKV))
        bias_term = jnp.concatenate(
            [jnp.sum(part.astype(f32), axis=0, keepdims=True) for part in (dq, dkv)], axis=1
        )
        x = xs[layer].astype(f32)
        scale = rms_scale(x)
        scaled = grad_one * gain_one
        inner = jnp.mean(scaled * x, axis=-1, keepdims=True)
        dx = dhid + scale * (scaled - x * (scale * scale * inner))
        gain_one_term = jnp.sum(grad_one * x * scale, axis=0, keepdims=True)
        rounded = dx.astype(bf16).astype(f32)
        dys[...] = rounded
        igs[layer] = rounded if layer == 1 else dx
        terms = jnp.concatenate(
            [bias_term, gain_one_term, gain_two_term, jnp.zeros((1, 128), f32)], axis=1
        )
        for at in range(12):
            vecs[layer, at : at + 1, :] = terms[:, 256 * at : 256 * (at + 1)]
        vecs[layer, 12:16, :] = jnp.zeros((4, 256), f32)

        @pl.when(layer == section_at)
        def _():
            for copy in staying(layer):
                copy.start()

        @pl.when(layer != section_at)
        def _():
            for copy in leaving(layer, section_at):
                copy.start()

    backward(1)
    backward(0)
    for copy in staying(section_at):
        copy.wait()
    for copy in leaving(other, section_at):
        copy.wait_send()
    for copy in leaving(other, other):
        copy.wait_recv()
    links.finish()


def run_layers(tokens, cotangent, lengths, vec, *weights):
    vmem = pl.BlockSpec(memory_space=pltpu.VMEM)
    anywhere = pl.BlockSpec(memory_space=pl.ANY)

    def per_micro(shape, kind):
        return jax.ShapeDtypeStruct((2,) + shape, kind)

    sems = 6 + 4 + 1 + 3 * 14 + 2 * 6 + 8 * 6

    def scratch(shape, kind=bf16, lead=2):
        return pltpu.VMEM((lead,) + shape, kind)

    return pl.pallas_call(
        layers_kernel,
        out_shape=(
            per_micro((SPAN, D), bf16),
            per_micro((SPAN, D), f32),
            per_micro((ZDEV, SPAN, D), bf16),
            per_micro((ROW, 2 * WIN), bf16),
            per_micro((ROW, WIN), bf16),
            per_micro((ZDEV, SPAN, D), bf16),
            per_micro((SPAN, 2 * D), bf16),
            per_micro((SPAN, QKV + D), bf16),
            per_micro((16, 256), f32),
        ),
        in_specs=[vmem, vmem, pl.BlockSpec(memory_space=pltpu.SMEM), vmem] + [anywhere] * 5,
        out_specs=[vmem] * 9,
        scratch_shapes=[
            scratch((ZDEV, OWN, QKV + D)),
            scratch((ZDEV, RING, RING, 16, 2 * WIN)),
            scratch((WIN, D)),
            scratch((ZDEV, 8, 384), f32),
            pltpu.VMEM((64, D), bf16),
            pltpu.VMEM((SPAN, ROW), f32),
            pltpu.VMEM((SPAN, 128), f32),
            pltpu.VMEM((SPAN, 128), f32),
            pltpu.VMEM((SPAN, 128), f32),
            scratch((SPAN, D), lead=3),
            scratch((SPAN, D)),
            scratch((SPAN, D)),
            scratch((ZDEV, SPAN, 2 * KV_WIDTH)),
            scratch((HEADS * SPAN, ROW), f32),
            scratch((SPAN, D)),
            scratch((SPAN, D), f32),
            scratch((ZDEV, SPAN, D)),
            scratch((2, ROW, WIN), f32),
            scratch((ROW, WIN)),
            scratch((ZDEV, SPAN, D)),
            scratch((SPAN // 2, D), lead=4),
            scratch((SPAN // 2, D), lead=4),
            scratch((SPAN, D), lead=4),
            scratch((SPAN, D), lead=4),
            pltpu.VMEM((SPAN, D), f32),
            pltpu.VMEM((SPAN, D), f32),
            scratch((ZDEV, SPAN, D)),
            scratch((ROW, 2 * WIN)),
            pltpu.VMEM((ROW, D), f32),
            scratch((ZDEV, SPAN, D)),
            scratch((ZDEV, SPAN, 2 * KV_WIDTH)),
            scratch((ZDEV, SPAN, 2 * KV_WIDTH)),
            scratch((SPAN, 2 * D)),
            scratch((SPAN, QKV + D)),
            scratch((16, 256), f32),
            scratch((SPAN, D), f32),
            pltpu.SemaphoreType.DMA((2, 6, 3)),
            pltpu.SemaphoreType.DMA((2, 6, 3)),
            pltpu.SemaphoreType.DMA((9,)),
            pltpu.SemaphoreType.DMA((9,)),
            pltpu.SemaphoreType.DMA((9,)),
            pltpu.SemaphoreType.DMA((sems,)),
            pltpu.SemaphoreType.DMA((sems,)),
            pltpu.SemaphoreType.DMA((8,)),
        ],
        compiler_params=pltpu.CompilerParams(
            collective_id=3, has_side_effects=True, vmem_limit_bytes=60 * 1024 * 1024
        ),
        name="layers",
    )(tokens, cotangent, lengths, vec, *weights)


def on_device(
    tokens, cotangent, doc_lengths, w_qkv, b_qkv, w_out, w_gate, w_up, w_down, norm_attn, norm_ffn
):
    group_at = lax.axis_index("group")
    vec = jnp.zeros((8 * 384,), f32)
    for member, start in ((b_qkv, 0), (norm_attn, QKV), (norm_ffn, QKV + D)):
        width = member.shape[1]
        vec = lax.dynamic_update_slice(
            vec, member[0].astype(f32), (start + width * group_at,)
        )
    acts, input_grads, *pieces = run_layers(
        tokens[:, 0],
        cotangent[:, 0],
        doc_lengths,
        vec.reshape(8, 384),
        w_qkv[0],
        w_out[0],
        w_gate[0],
        w_up[0],
        w_down[0],
    )
    grads = weight_grads(*pieces)
    return (acts[None, :, None], input_grads[None, :, None]) + tuple(g[None] for g in grads)


def solution(mesh):
    rows = P("section", "group", None)
    vector = P("section", "group")
    spans = P("section", None, "replica", "group", None)
    return jax.shard_map(
        on_device,
        mesh=mesh,
        in_specs=(
            P(None, "replica", "group", None),
            P(None, "replica", "group", None),
            P(None, "replica", None),
            rows,
            vector,
            rows,
            rows,
            rows,
            rows,
            vector,
            vector,
        ),
        out_specs=(spans, spans, rows, vector, rows, rows, rows, rows, vector, vector),
        check_vma=False,
    )
```
